32 devices in a mesh: seq: 8 (over z, y), grp: 4 (over x, core).
Axes of the slice: x: 2, y: 2, z: 4, core: 2. Of those that a mesh axis runs over, the one named last changes fastest.
Arguments:
- frames_in: float32 [4, 1024, 512], P('grp', 'seq'), may hold values from -6 to 6
- cotangent: float32 [4, 1024, 512], P('grp', 'seq'), may hold values from -6 to 6
- lengths: int32 [4, 4], P('grp'), may hold values from 1 to 1024, as said below
- rate_flags: int32 [4, 4], P('grp'), may hold values 0 or 1
- owner_list: int32 [48, 1], replicated, may hold values from 0 to 3; in each aligned block of 48 rows (0 to 47, 48 to 95, ...) at most 16 rows name the same one
- master: float32 [64, 262144], P('grp', 'seq'), may hold values from -0.25 to 0.25
- moment_one: float32 [64, 262144], P('grp', 'seq'), may hold values from -6 to 6
- moment_two: float32 [64, 262144], P('grp', 'seq'), may hold values from 0.16384 to 0.65536
- average: float32 [64, 262144], P('grp', 'seq'), may hold values from -0.25 to 0.25
- small_params: float32 [2, 23, 512], replicated
- small_moment_one: float32 [2, 23, 512], replicated, may hold values from -20 to 20
- small_moment_two: float32 [2, 23, 512], replicated, may hold values from 0.8192 to 3.2768
- small_average: float32 [2, 23, 512], replicated
Outputs:
- output: float32 [4, 1024, 512], P('grp', 'seq')
- grad_in: float32 [4, 1024, 512], P('grp', 'seq')
- new_master: float32 [64, 262144], P('grp', 'seq')
- master_copy: bfloat16 [64, 262144], P('grp', 'seq')
- new_moment_one: float32 [64, 262144], P('grp', 'seq')
- new_moment_two: float32 [64, 262144], P('grp', 'seq')
- new_average: float32 [64, 262144], P('grp', 'seq')
- new_small: float32 [2, 23, 512], replicated
- new_small_one: float32 [2, 23, 512], replicated
- new_small_two: float32 [2, 23, 512], replicated
- new_small_average: float32 [2, 23, 512], replicated
The draws below stay inside these ranges and needn't reach their ends.
Inputs may be any that keep to these rules, and one draw needn't show every extreme that they name: `lengths`: each row sums to 1024. In each row one item, at a place drawn from the seed, starts within the first 128 frames and ends within the last 128; every other item has at most 32 frames. `owner_list`: each owner holds at most 16 blocks, and some owner holds exactly 16.
All inputs are finite; a program needn't handle non-finite values. No bound on the sum of `rate_flags` on one device may be relied on, other than what follows from the above.
Results may differ from the reference program's by a relative error of at most 0.001.
Values sent between devices are 32-bit elements; how exact they have to be, the bound alone decides.
A program may use at most 384 MiB of HBM per device.

```python
import math
import jax
import jax.numpy as jnp
import numpy as np
from jax import lax

D = 512
HEADS = 8
KERNEL = 9
NB = 128
L = 2
ITEMS = 4
CAP = 16
STEP = 10
TOK_DEV = 128
STREAM = 1024
FRAMES = 4096
NUNIT = 48
UNIT = 262144
SROWS = 23
N_GRP = 4


def shape_rows(base):
    row_number = jnp.arange(SROWS, dtype=jnp.int32)[None, :, None]
    gains = 1.0 + 0.1 * base
    shifts = 0.1 * base
    kernel_taps = base / 3.0
    pos_biases = 0.5 * base
    normal_rows = jnp.where(row_number % 2 == 0, gains, shifts)
    other_rows = jnp.where(row_number < 12 + KERNEL, kernel_taps, pos_biases)
    return jnp.where(row_number < 12, normal_rows, other_rows).astype(jnp.float32)


def draw_lengths(key, part):
    key = jax.random.fold_in(key, 5)
    key_big, key_small = jax.random.split(key)
    longest = jax.random.randint(key_big, (N_GRP, 1), 0, ITEMS)
    shorter = jax.random.randint(key_small, (N_GRP, ITEMS), 1, TOK_DEV // ITEMS + 1)
    numbers = jnp.arange(ITEMS, dtype=jnp.int32)[None, :]
    shorter = jnp.where(numbers == longest, 0, shorter)
    remain = STREAM - jnp.sum(shorter, axis=1, keepdims=True)
    return jnp.where(numbers == longest, remain, shorter).astype(jnp.int32)


def draw_small_params(key, part):
    key = jax.random.fold_in(key, 11)
    base = jax.random.normal(key, (L, SROWS, D), jnp.float32)
    return shape_rows(base)


def draw_small_average(key, part):
    key = jax.random.fold_in(key, 13)
    base = jax.random.normal(key, (L, SROWS, D), jnp.float32)
    return shape_rows(base)


def with_ends(entries, own_key, smallest, largest):
    extent = entries.shape
    index_at = [jax.random.randint(jax.random.fold_in(own_key, axis), (), 0, extent[axis]) for axis in range(len(extent))]
    entries = entries.at[tuple(index_at)].set(smallest)
    longest = extent.index(max(extent))
    index_at[longest] = (index_at[longest] + 1) % extent[longest]
    return entries.at[tuple(index_at)].set(largest)


def level_of(own_key, shape, shards, low, top_value):
    def one(axis_at, blocks):
        draws = jax.random.uniform(jax.random.fold_in(jax.random.fold_in(own_key, 6), axis_at), (blocks,), jnp.float32, low / len(shards), top_value / len(shards))
        return jnp.repeat(jnp.exp(draws), shape[axis_at] // blocks).reshape((-1,) + (1,) * (len(shape) - axis_at - 1))

    gain = one(*shards[0])
    for cut in shards[1:]:
        gain = gain * one(*cut)
    return gain


def shared_out(own_key, own, number, rows, number_of, top, limit, slope):
    ranking = jax.random.permutation(own_key, number_of)
    packed, common = shares(number_of, rows * top, limit, slope, True), shares(number_of, rows * top, limit, slope, False)
    places = jnp.arange(number_of)

    def named(sizes, rotation):
        used = int((sizes > 0).sum())
        fixed = max(1, used // 4)
        passed = fixed + (places - fixed + rotation * (used - fixed)) % max(1, number_of - fixed)
        return jnp.zeros((number_of,), jnp.int32).at[ranking[jnp.where(places < fixed, places, passed)]].set(jnp.asarray(sizes, jnp.int32))

    sizes = jnp.where(number % 4 == 0, named(packed, number // 4), named(common, number - number // 4 - 1))
    mixed = jax.random.permutation(jax.random.fold_in(own, 3), number_of)
    donor, taker = mixed[0:number_of // 2 * 2:2], mixed[1:number_of // 2 * 2:2]
    slack = jnp.minimum(sizes[donor] - 1, limit - sizes[taker]) // 2
    slack = jnp.where((donor == ranking[0]) | (taker == ranking[0]) | (sizes[taker] == 0), 0, jnp.maximum(slack, 0))
    passed = jax.random.randint(jax.random.fold_in(own, 4), (number_of // 2,), 0, 1 << 20) % (slack + 1)
    sizes = sizes.at[donor].add(-passed).at[taker].add(passed)
    members = jnp.searchsorted(jnp.cumsum(sizes), jnp.arange(rows * top), side="right").astype(jnp.int32)
    grid = members.reshape(top, rows).T
    grid = grid[jax.random.permutation(jax.random.fold_in(own, 1), rows)]
    rotation = jax.random.randint(jax.random.fold_in(own, 2), (rows, 1), 0, top)
    return jnp.take_along_axis(grid, (jnp.arange(top)[None, :] + rotation) % top, axis=1)


def shares(count, total, reach, lean, full):
    portions = [(1 << 20) // math.isqrt(standing ** lean) + 1 for standing in range(1, count + 1)]
    largest = reach if full else min(reach, max(-(-total // count), total * portions[0] // sum(portions)))
    least = 1 if total - largest >= count - 1 else 0
    holding, spare = [largest] + [least] * (count - 1), total - largest - least * (count - 1)
    while spare > 0:
        free = [i for i in range(1, count) if holding[i] < largest] or [i for i in range(1, count) if holding[i] < reach]
        whole, budget = sum([portions[i] for i in free]), spare
        for i in free:
            addition = min(reach - holding[i], max(1, budget * portions[i] // whole), spare)
            holding[i] = holding[i] + addition
            spare = spare - addition
    return np.array(holding)


def bell_draw(stream_key, dims, scale, bound, shards=(), kind=jnp.bfloat16):
    loudness = level_of(stream_key, dims, shards, -0.22, 0.18) if shards else 1.0
    array = jax.random.normal(stream_key, dims, jnp.float32) * scale * loudness
    return jnp.minimum(jnp.maximum(array, -bound), bound).astype(kind)


def setup_inputs(seed: int = 0) -> dict:
    keys = jax.random.split(jax.random.key(seed), 14)
    frames_in = bell_draw(keys[0], (N_GRP, STREAM, D), 1.0, 6.0, ((0, 4), (1, 8)), jnp.float32)
    cotangent = bell_draw(keys[1], (N_GRP, STREAM, D), 1.0, 6.0, ((0, 4), (1, 8)), jnp.float32)
    lengths = draw_lengths(jax.random.fold_in(keys[13], 71), 0)
    rate_flags = with_ends((jax.random.randint(keys[3], (N_GRP, ITEMS), 0, 2) < 1).astype(jnp.int32), jax.random.fold_in(keys[3], 1), 0, 1)
    owner_list_keys = jax.random.split(jax.random.fold_in(keys[4], 1), NUNIT // NUNIT)
    owner_list_turns = jax.random.permutation(jax.random.fold_in(keys[4], 3), NUNIT // NUNIT)
    owner_list = jax.vmap(lambda own, number: shared_out(jax.random.fold_in(keys[4], 2), own, number, NUNIT, N_GRP, 1, CAP, 2))(owner_list_keys, owner_list_turns).reshape((NUNIT, 1))
    master = bell_draw(keys[5], (N_GRP * CAP, UNIT), D ** -0.5, 0.25, ((0, 4), (1, 8)), jnp.float32)
    moment_one = bell_draw(keys[6], (N_GRP * CAP, UNIT), (0.022 * FRAMES ** 0.5), 6.0, ((0, 4), (1, 8)), jnp.float32)
    moment_two = jnp.clip(jnp.exp(math.log(0.65536) - 1.3862944 * jax.random.uniform(keys[7], (N_GRP * CAP, UNIT), jnp.float32) ** level_of(keys[7], (N_GRP * CAP, UNIT), ((0, 4), (1, 8)), -0.2, 0.2)), 0.16384, 0.65536)
    average = bell_draw(keys[8], (N_GRP * CAP, UNIT), D ** -0.5, 0.25, ((0, 4), (1, 8)), jnp.float32)
    small_params = draw_small_params(jax.random.fold_in(keys[13], 71), 0)
    small_moment_one = bell_draw(keys[10], (L, SROWS, D), (0.05 * FRAMES ** 0.5), 20.0, (), jnp.float32)
    small_moment_two = jnp.clip(jnp.exp(jax.random.uniform(keys[11], (L, SROWS, D), jnp.float32, math.log(0.8192), math.log(3.2768))), 0.8192, 3.2768)
    small_average = draw_small_average(jax.random.fold_in(keys[13], 71), 0)
    return dict(frames_in=frames_in, cotangent=cotangent, lengths=lengths, rate_flags=rate_flags, owner_list=owner_list, master=master, moment_one=moment_one, moment_two=moment_two, average=average, small_params=small_params, small_moment_one=small_moment_one, small_moment_two=small_moment_two, small_average=small_average)


PRECISION_HIGH = lax.Precision.HIGHEST
EPS_NORM = 1e-05
BETA_ONE = 0.9
BETA_TWO = 0.999
ADAM_EPS = 1e-08
RATE_MATRIX = 0.03
RATE_SMALL = 0.1
DECAY_WEIGHT = 0.01
AVERAGE_KEEP = 0.99

@jax.custom_vjp
def low(v):
    return lax.optimization_barrier(v.astype(jnp.bfloat16)).astype(jnp.float32)

@jax.custom_vjp
def low_back(v):
    return v

def low_keep(v):
    return (low(v), None)

def low_pass(kept, grad):
    return (grad,)

def back_keep(v):
    return (v, None)

def back_low(kept, grad):
    return (low(grad),)
low.defvjp(low_keep, low_pass)
low_back.defvjp(back_keep, back_low)

def product(left, right):
    return jnp.dot(left, right, precision=PRECISION_HIGH)

def layer_norm(values, norm_gain, norm_shift):
    center = values - lax.optimization_barrier(jnp.mean(values, axis=-1, keepdims=True))
    spread = lax.optimization_barrier(jnp.mean(center * center, axis=-1, keepdims=True))
    return center * lax.rsqrt(spread + EPS_NORM) * norm_gain + norm_shift

def widen_blocks(blocks):
    return jnp.transpose(blocks, (1, 0, 2)).reshape(blocks.shape[1], -1)

def feed_forward(values, blocks, norm_gain, norm_shift):
    normed = layer_norm(values, norm_gain, norm_shift)
    hidden = jax.nn.silu(product(normed, widen_blocks(blocks[0:4])))
    return 0.5 * product(hidden, blocks[4:8].reshape(-1, values.shape[-1]))

def rel_table(bucket_count, hidden_width):
    offset = (jnp.arange(bucket_count, dtype=jnp.int32) - bucket_count // 2).astype(jnp.float32)[:, None]
    column = jnp.arange(hidden_width, dtype=jnp.int32)
    frequency = jnp.exp(-math.log(10000.0) * (2 * (column // 2)).astype(jnp.float32) / hidden_width)[None, :]
    angles = offset * frequency
    return jnp.where(column[None, :] % 2 == 0, jnp.sin(angles), jnp.cos(angles))

def attention_inputs(values, w_query, w_key, w_value, w_pos, norm_gain, norm_shift, bias_u, bias_v):
    normed = layer_norm(values, norm_gain, norm_shift)
    queries = product(normed, w_query)
    pos_table = product(rel_table(NB, values.shape[-1]), w_pos)
    return (queries + bias_u, queries + bias_v, pos_table, product(normed, w_key), product(normed, w_value))

def conv_inputs(values, w_value, w_gate, norm_gain, norm_shift):
    normed = layer_norm(values, norm_gain, norm_shift)
    return product(normed, w_value) * jax.nn.sigmoid(product(normed, w_gate))

def conv_outputs(extended, kernel_rows, w_out, norm_gain, norm_shift, item_mask):
    row_count = extended.shape[0] - KERNEL + 1
    mixed_rows = jnp.zeros((row_count, extended.shape[1]), jnp.float32)
    for tap_index in range(KERNEL):
        mixed_rows = mixed_rows + extended[tap_index:tap_index + row_count] * item_mask[tap_index][:, None] * kernel_rows[tap_index]
    normed = layer_norm(mixed_rows, norm_gain, norm_shift)
    return product(jax.nn.silu(normed), w_out)

def frame_info(frame_index, lengths_row, flags_row):
    item_ends = jnp.cumsum(lengths_row).astype(jnp.int32)
    item_starts = item_ends - lengths_row
    inside = (frame_index[:, None] >= item_starts[None, :]) & (frame_index[:, None] < item_ends[None, :])
    numbers = jnp.arange(lengths_row.shape[0], dtype=jnp.int32)
    frame_items = lax.optimization_barrier(jnp.sum(jnp.where(inside, numbers[None, :] + 1, 0), axis=1)).astype(jnp.int32) - 1
    first_frame = lax.optimization_barrier(jnp.sum(jnp.where(inside, item_starts[None, :], 0), axis=1)).astype(jnp.int32)
    stride = lax.optimization_barrier(jnp.sum(jnp.where(inside, 1 + flags_row[None, :], 0), axis=1)).astype(jnp.int32)
    return (frame_items, ((frame_index - first_frame) * stride).astype(jnp.int32))

def slot_index(owner_list):
    owners = owner_list[:, 0]
    numbers = jnp.arange(owners.shape[0], dtype=jnp.int32)
    earlier = (owners[None, :] == owners[:, None]) & (numbers[None, :] < numbers[:, None])
    owner_rank = lax.optimization_barrier(jnp.sum(earlier.astype(jnp.int32), axis=1)).astype(jnp.int32)
    return (owners * CAP + owner_rank).astype(jnp.int32)

def adam_step(attention_weights, first_moment, second_moment, gradient, step_rate, decay_rate):
    first_moment = BETA_ONE * first_moment + (1.0 - BETA_ONE) * gradient
    second_moment = BETA_TWO * second_moment + (1.0 - BETA_TWO) * gradient * gradient
    fixed_one = 1.0 - BETA_ONE ** STEP
    fixed_two = 1.0 - BETA_TWO ** STEP
    direction = first_moment / fixed_one / (jnp.sqrt(second_moment / fixed_two) + ADAM_EPS)
    return (attention_weights - step_rate * (direction + decay_rate * attention_weights), first_moment, second_moment)

def full_attention(q_u, q_v, pos_table, key_rows, value_rows, frame_items, frame_pos):
    row_count, hidden_width = q_u.shape
    head_size = hidden_width // HEADS
    bucket_count = pos_table.shape[0]
    rows_per_block = 4 * TOK_DEV
    score_scale = 1.0 / math.sqrt(head_size)
    query_with_bias = q_u.reshape(row_count, HEADS, head_size)
    query_pos = jnp.einsum('nhd,bhd->hnb', q_v.reshape(row_count, HEADS, head_size), pos_table.reshape(bucket_count, HEADS, head_size), precision=PRECISION_HIGH)
    heads_of_keys = key_rows.reshape(row_count, HEADS, head_size)
    heads_of_values = value_rows.reshape(row_count, HEADS, head_size)

    def one_block(block_start):
        block_query_bias = lax.dynamic_slice_in_dim(query_with_bias, block_start, rows_per_block, 0)
        block_pos = lax.dynamic_slice_in_dim(query_pos, block_start, rows_per_block, 1)
        block_items = lax.dynamic_slice_in_dim(frame_items, block_start, rows_per_block, 0)
        block_places = lax.dynamic_slice_in_dim(frame_pos, block_start, rows_per_block, 0)
        attention_scores = jnp.einsum('qbp,cbp->bqc', block_query_bias, heads_of_keys, precision=PRECISION_HIGH)
        bucket = jnp.clip(block_places[:, None] - frame_pos[None, :], -(bucket_count // 2), bucket_count // 2 - 1) + bucket_count // 2
        attention_scores = attention_scores + jnp.take_along_axis(block_pos, jnp.broadcast_to(bucket[None], (HEADS, rows_per_block, row_count)), axis=2)
        attention_scores = attention_scores * score_scale
        same_item = (block_items[:, None] == frame_items[None, :])[None]
        attention_scores = jnp.where(same_item, attention_scores, -1e+30)
        row_top = lax.optimization_barrier(jnp.max(attention_scores, axis=-1, keepdims=True))
        attention_weights = jnp.where(same_item, jnp.exp(attention_scores - row_top), 0.0)
        attention_weights = attention_weights / lax.optimization_barrier(jnp.sum(attention_weights, axis=-1, keepdims=True))
        return jnp.einsum('jxi,ijf->xjf', attention_weights, heads_of_values, precision=PRECISION_HIGH).reshape(rows_per_block, hidden_width)
    block_starts = (jnp.arange(row_count // rows_per_block, dtype=jnp.int32) * rows_per_block).astype(jnp.int32)
    context = lax.map(jax.checkpoint(one_block), block_starts)
    return context.reshape(row_count, hidden_width)

def layer_forward(values, blocks, rows_small, frame_items, frame_pos, item_mask):
    values = values + feed_forward(values, blocks[0:8], rows_small[0], rows_small[1])
    q_u, q_v, pos_table, key_rows, value_rows = attention_inputs(values, blocks[8], blocks[9], blocks[10], blocks[12], rows_small[2], rows_small[3], rows_small[12 + KERNEL], rows_small[13 + KERNEL])
    context = full_attention(q_u, q_v, pos_table, key_rows, value_rows, frame_items, frame_pos)
    values = values + product(context, blocks[11])
    glu_rows = conv_inputs(values, blocks[13], blocks[14], rows_small[4], rows_small[5])
    half_width = (KERNEL - 1) // 2
    extended = jnp.pad(glu_rows, ((half_width, half_width), (0, 0)))
    values = values + conv_outputs(extended, rows_small[12:12 + KERNEL], blocks[15], rows_small[6], rows_small[7], item_mask)
    values = values + feed_forward(values, blocks[16:24], rows_small[8], rows_small[9])
    return layer_norm(values, rows_small[10], rows_small[11])

def reference(frames_in, cotangent, lengths, rate_flags, owner_list, master, moment_one, moment_two, average, small_params, small_moment_one, small_moment_two, small_average):
    slot_of = slot_index(owner_list)
    half_width = (KERNEL - 1) // 2
    frame_index = jnp.arange(STREAM, dtype=jnp.int32)
    stream_items = []
    stream_places = []
    stream_masks = []
    for group_index in range(N_GRP):
        frame_items, frame_pos = frame_info(frame_index, lengths[group_index], rate_flags[group_index])
        padded = jnp.pad(frame_items, (half_width, half_width), constant_values=-1)
        item_mask = jnp.stack([(padded[tap_index:tap_index + STREAM] == frame_items).astype(jnp.float32) for tap_index in range(KERNEL)])
        stream_items.append(frame_items)
        stream_places.append(frame_pos)
        stream_masks.append(item_mask)

    def forward(frames, slot_rows, small_rows):
        blocks_all = slot_rows[slot_of].reshape(NUNIT, D, D)
        results = []
        for group_index in range(N_GRP):
            values = frames[group_index]
            for layer_index in range(L):
                values = layer_forward(values, blocks_all[24 * layer_index:24 * layer_index + 24], small_rows[layer_index], stream_items[group_index], stream_places[group_index], stream_masks[group_index])
            results.append(values)
        return jnp.stack(results)
    output, pull_back = jax.vjp(forward, frames_in, master, small_params)
    grad_in, grad_slots, grad_small = pull_back(cotangent)
    new_master, new_one, new_two = adam_step(master, moment_one, moment_two, grad_slots, RATE_MATRIX, DECAY_WEIGHT)
    new_average = AVERAGE_KEEP * average + (1.0 - AVERAGE_KEEP) * new_master
    new_small, new_small_one, new_small_two = adam_step(small_params, small_moment_one, small_moment_two, grad_small, RATE_SMALL, 0.0)
    new_small_average = AVERAGE_KEEP * small_average + (1.0 - AVERAGE_KEEP) * new_small
    return (output, grad_in, new_master, new_master.astype(jnp.bfloat16), new_one, new_two, new_average, new_small, new_small_one, new_small_two, new_small_average)
```

```python
import functools
import math

import jax
import jax.numpy as jnp
import numpy as np
from jax import lax
from jax.experimental import pallas as pl
from jax.experimental.pallas import tpu as pltpu
from jax.sharding import PartitionSpec as P

HEADS = 8
KERNEL = 9
NB = 128
L = 2
CAP = 16
STEP = 10
EPS_NORM = 1e-05
BETA_ONE = 0.9
BETA_TWO = 0.999
ADAM_EPS = 1e-08
RATE_MATRIX = 0.03
RATE_SMALL = 0.1
DECAY_WEIGHT = 0.01
AVERAGE_KEEP = 0.99


def position_tables(width):
    falling = NB // 2 - 1 - np.arange(NB)
    doubled = np.clip(2 * falling, -(NB // 2), NB // 2 - 1)
    offset = np.concatenate([falling, doubled]).astype(np.float64)[:, None]
    column = np.arange(width)
    frequency = np.exp(-math.log(10000.0) * (2 * (column // 2)) / width)[None, :]
    angles = offset * frequency
    return jnp.asarray(np.where(column[None, :] % 2 == 0, np.sin(angles), np.cos(angles)), jnp.float32)


def frame_info(frame_index, lengths_row, flags_row):
    item_ends = jnp.cumsum(lengths_row)
    item_starts = item_ends - lengths_row
    inside = (frame_index[:, None] >= item_starts[None, :]) & (
        frame_index[:, None] < item_ends[None, :]
    )
    numbers = jnp.arange(lengths_row.shape[0], dtype=jnp.int32)
    frame_items = jnp.sum(jnp.where(inside, numbers[None, :] + 1, 0), axis=1) - 1
    first_frame = jnp.sum(jnp.where(inside, item_starts[None, :], 0), axis=1)
    stride = jnp.sum(jnp.where(inside, 1 + flags_row[None, :], 0), axis=1)
    return (frame_items, (frame_index - first_frame) * stride)


def slot_index(owner_list):
    owners = owner_list[:, 0]
    numbers = jnp.arange(owners.shape[0], dtype=jnp.int32)
    earlier = (owners[None, :] == owners[:, None]) & (numbers[None, :] < numbers[:, None])
    owner_rank = jnp.sum(earlier.astype(jnp.int32), axis=1)
    return owners * CAP + owner_rank


def adam_step(attention_weights, first_moment, second_moment, gradient, step_rate, decay_rate):
    first_moment = BETA_ONE * first_moment + (1.0 - BETA_ONE) * gradient
    second_moment = BETA_TWO * second_moment + (1.0 - BETA_TWO) * gradient * gradient
    fixed_one = 1.0 - BETA_ONE**STEP
    fixed_two = 1.0 - BETA_TWO**STEP
    direction = first_moment / fixed_one / (jnp.sqrt(second_moment / fixed_two) + ADAM_EPS)
    return (
        attention_weights - step_rate * (direction + decay_rate * attention_weights),
        first_moment,
        second_moment,
    )


MESH = pl.DeviceIdType.MESH
CHUNKS = 12
GROUP = 4


def places():
    seq = lax.axis_index("seq")
    grp = lax.axis_index("grp")
    return seq, grp, seq // 2, seq % 2, grp // 2, grp % 2


def over(lo, hi, fn):
    def body(i, carry):
        fn(i)
        return carry

    lax.fori_loop(lo, hi, body, 0)


def remote(src, dst, s, r, dev):
    return pltpu.make_async_remote_copy(
        src_ref=src, dst_ref=dst, send_sem=s, recv_sem=r, device_id=dev, device_id_type=MESH
    )


def update_kernel(
    block_ref, used_ref, shares_ref, master_ref, one_ref, two_ref, average_ref,
    new_master, copy, new_one, new_two, new_average, rows_ref, sems,
):
    i = pl.program_id(0)
    slots = master_ref.shape[0]

    def fetch(s):
        return pltpu.make_async_copy(shares_ref.at[block_ref[s]], rows_ref.at[s], sems.at[s])

    @pl.when(i == 0)
    def _():
        over(0, slots, lambda s: fetch(s).start())
        over(0, slots, lambda s: fetch(s).wait())

    half = rows_ref.shape[-1]
    pieces = []
    for r in range(8):
        for h in range(2):
            pieces.append(rows_ref[:, h, i * 8 + r, :])
    gradient = jnp.concatenate(pieces, axis=1) * used_ref[...]
    master = master_ref[...]
    master, one, two = adam_step(
        master, one_ref[...], two_ref[...], gradient, RATE_MATRIX, DECAY_WEIGHT
    )
    new_master[...] = master
    copy[...] = master.astype(jnp.bfloat16)
    new_one[...] = one
    new_two[...] = two
    new_average[...] = AVERAGE_KEEP * average_ref[...] + (1.0 - AVERAGE_KEEP) * master


def update_slots(shares, block, used, master, moment_one, moment_two, average):
    slab, half = shares.shape[2:]
    slots, entries = master.shape
    columns = 8 * 2 * half
    spec = pl.BlockSpec((slots, columns), lambda i, block: (0, i))
    full = jax.ShapeDtypeStruct((slots, entries), jnp.float32)
    return pl.pallas_call(
        update_kernel,
        grid_spec=pltpu.PrefetchScalarGridSpec(
            num_scalar_prefetch=1,
            grid=(slab // 8,),
            in_specs=[
                pl.BlockSpec((slots, 1), lambda i, block: (0, 0)), pl.BlockSpec(memory_space=pl.ANY),
                spec, spec, spec, spec,
            ],
            out_specs=[spec] * 5,
            scratch_shapes=[
                pltpu.VMEM((slots, 2, slab, half), jnp.float32), pltpu.SemaphoreType.DMA((slots,)),
            ],
        ),
        out_shape=[full, jax.ShapeDtypeStruct((slots, entries), jnp.bfloat16), full, full, full],
        compiler_params=pltpu.CompilerParams(vmem_limit_bytes=LIMIT),
        name="update_slots",
    )(block, used, shares, master, moment_one, moment_two, average)


BF16 = jnp.bfloat16
F32 = jnp.float32
ROWS = 32
KEYS = 1024


def split(value):
    high = value.astype(BF16)
    return high, (value - high.astype(F32)).astype(BF16)


def dot(left, right, dims):
    return lax.dot_general(left, right, (dims, ((), ())), preferred_element_type=F32)


def dot3(left, right, dims):
    (lh, ll), (rh, rl) = left, right
    rows = lh.shape[0]
    if dims[0] == (1,) and rows <= 128:
        both = dot(jnp.concatenate([lh, ll], axis=0), rh, dims)
        return both[:rows] + (both[rows:] + dot(lh, rl, dims))
    return dot(lh, rh, dims) + (dot(ll, rh, dims) + dot(lh, rl, dims))


def nn(left, right):
    return dot3(left, right, ((1,), (0,)))


def nt(left, right):
    return dot3(left, right, ((1,), (1,)))


def tn(left, right):
    (lh, ll), (rh, rl) = left, right
    return dot(
        jnp.concatenate([lh, lh, ll], axis=0),
        jnp.concatenate([rh, rl, rh], axis=0),
        ((0,), (0,)),
    )


def tn_long(left, right):
    return dot3(left, right, ((0,), (0,)))


def norm(value):
    center = value - jnp.mean(value, axis=-1, keepdims=True)
    scale = lax.rsqrt(jnp.mean(center * center, axis=-1, keepdims=True) + EPS_NORM)
    return center * scale, scale


def norm_back(grad, unit, scale, gain):
    inner = grad * gain
    value_grad = scale * (
        inner
        - jnp.mean(inner, axis=-1, keepdims=True)
        - unit * jnp.mean(inner * unit, axis=-1, keepdims=True)
    )
    return (
        value_grad,
        jnp.sum(grad * unit, axis=0, keepdims=True),
        jnp.sum(grad, axis=0, keepdims=True),
    )


def sigmoid(value):
    return 1.0 / (1.0 + jnp.exp(-value))


def ffn_forward(v, small, row, weights, first, z_ref, middle=None):
    unit, _ = norm(v)
    h = split(unit * small[row : row + 1] + small[row + 1 : row + 2])
    total = None
    for j in range(4):
        z = nn(h, split(weights.get(first + j)))
        z_ref[:, 512 * j : 512 * j + 512] = z
        part = nn(split(z * sigmoid(z)), split(weights.get(first + 4 + j)))
        total = part if total is None else total + part
        if j == 1 and middle is not None:
            middle()
    return v + 0.5 * total


def ffn_backward(grad, v, z_ref, small, row, weights, first, grads, at, ds_ref, middle):
    unit, scale = norm(v)
    gain = small[row : row + 1]
    hth, htl = split((unit * gain + small[row + 1 : row + 2]).T)
    wide = jnp.concatenate([hth, hth, htl], axis=1)
    half = split(0.5 * grad)
    for j in range(4):
        z = z_ref[:, 512 * j : 512 * j + 512]
        grads.put(at + 4 + j, tn(split(z * sigmoid(z)), half))
    middle()
    total = None
    for j in range(4):
        z = z_ref[:, 512 * j : 512 * j + 512]
        s = sigmoid(z)
        da = nt(half, split(weights.get(first + 4 + j)))
        dz = split(da * (s * (1.0 + z * (1.0 - s))))
        tall = jnp.concatenate([dz[0], dz[1], dz[0]], axis=0)
        grads.put(at + j, dot(wide, tall, ((1,), (0,))))
        part = nt(dz, split(weights.get(first + j)))
        total = part if total is None else total + part
    back, dg, dc = norm_back(total, unit, scale, gain)
    ds_ref[row : row + 1] = dg
    ds_ref[row + 1 : row + 2] = dc
    return grad + back


def conv_mix(ext_ref, masks, small):
    mixed = None
    for t in range(KERNEL):
        part = ext_ref[t : t + masks.shape[0], :] * masks[:, t : t + 1] * small[12 + t : 13 + t]
        mixed = part if mixed is None else mixed + part
    return mixed


def conv_forward(v, ext_ref, masks, small, wc):
    unit, _ = norm(conv_mix(ext_ref, masks, small))
    n = unit * small[6:7] + small[7:8]
    return v + nn(split(n * sigmoid(n)), split(wc))


def conv_backward(grad, ext_ref, masks, small, wc, grads, at, dext_ref, ds_ref):
    unit, scale = norm(conv_mix(ext_ref, masks, small))
    gain = small[6:7]
    n = unit * gain + small[7:8]
    s = sigmoid(n)
    g = split(grad)
    grads.put(at, tn(split(n * s), g))
    dn = nt(g, split(wc)) * (s * (1.0 + n * (1.0 - s)))
    dm, dg, dc = norm_back(dn, unit, scale, gain)
    ds_ref[6:7] = dg
    ds_ref[7:8] = dc
    rows = masks.shape[0]
    dext_ref[...] = jnp.zeros_like(dext_ref)
    for t in range(KERNEL):
        dmt = dm * masks[:, t : t + 1]
        ds_ref[12 + t : 13 + t] = jnp.sum(dmt * ext_ref[t : t + rows, :], axis=0, keepdims=True)
        dext_ref[t : t + rows, :] += dmt * small[12 + t : 13 + t]


def fill_ext(ext_ref, low, middle, high):
    half = (KERNEL - 1) // 2
    rows = middle.shape[0]
    ext_ref[0:half, :] = low
    ext_ref[half : half + rows, :] = middle
    ext_ref[half + rows : 2 * half + rows, :] = high


def gate_forward(v, small, wa, wg):
    unit, _ = norm(v)
    h = split(unit * small[4:5] + small[5:6])
    za, zg = nn(h, split(wa)), nn(h, split(wg))
    return za, zg, za * sigmoid(zg)


def gate_backward(grad_glu, grad, v, za, zg, small, wa, wg, grads, at, ds_ref):
    unit, scale = norm(v)
    gain = small[4:5]
    h = split(unit * gain + small[5:6])
    s = sigmoid(zg)
    da = split(grad_glu * s)
    dg_ = split(grad_glu * za * s * (1.0 - s))
    grads.put(at, tn(h, da))
    grads.put(at + 1, tn(h, dg_))
    back, dg, dc = norm_back(nt(da, split(wa)) + nt(dg_, split(wg)), unit, scale, gain)
    ds_ref[4:5] = dg
    ds_ref[5:6] = dc
    return grad + back


def stacked(quad):
    rows = quad.shape[0]
    tall = jnp.concatenate([quad] * 4, axis=0)
    shape = (4 * rows, 256)
    head = lax.broadcasted_iota(jnp.int32, shape, 0) // rows
    lane = lax.broadcasted_iota(jnp.int32, shape, 1) // 64
    return jnp.where(head == lane, tall, 0.0)


def unstacked(tall, rows):
    shape = (rows, 256)
    lane = lax.broadcasted_iota(jnp.int32, shape, 1) // 64
    quad = tall[0:rows]
    for n in range(1, 4):
        quad = jnp.where(lane == n, tall[n * rows : (n + 1) * rows], quad)
    return quad


def turned(value):
    rows = value.shape[0]
    shape = (rows, rows)
    place = lax.broadcasted_iota(jnp.int32, shape, 0) + lax.broadcasted_iota(jnp.int32, shape, 1)
    swap = jnp.where(place == rows - 1, 1.0, 0.0).astype(BF16)
    high, low = split(value)
    return dot(swap, high, ((1,), (0,))) + dot(swap, low, ((1,), (0,)))


def place_bias(quad_q, table, rate, bias_ref, head0):
    rows = quad_q.shape[0]
    near = nt(split(stacked(quad_q)), split(table))
    row = lax.broadcasted_iota(jnp.int32, (rows, 3 * rows), 0)
    column = lax.broadcasted_iota(jnp.int32, (rows, 3 * rows), 1)
    place = column - row - 65
    for n in range(4):
        both = near[n * rows : (n + 1) * rows]
        one = jnp.where(rate == 2, both[:, 128:], both[:, :128])
        last, first = one[:, 0:1], one[:, 127:128]
        wide = jnp.concatenate([one, jnp.zeros((rows, 2 * rows), F32)], axis=1)
        rolled = pltpu.roll(wide, 65, 1, stride=1, stride_axis=0)
        window = jnp.where(place < 0, last, jnp.where(place > 127, first, rolled))
        bias_ref[head0 + n, 0] = jnp.broadcast_to(last, (rows, rows))
        for i in range(3):
            bias_ref[head0 + n, 1 + i] = window[:, i * rows : (i + 1) * rows]
        bias_ref[head0 + n, 4] = jnp.broadcast_to(first, (rows, rows))


def tile_scores(s_ref, bias_ref, items_q, items_k, tile, head0, own, chunk, rows):
    per = rows // ROWS
    head, part = tile // per, tile % per
    r0 = pl.multiple_of(part * ROWS, ROWS)
    s0 = pl.multiple_of(tile * ROWS, ROWS)
    iq = items_q[pl.ds(r0, ROWS), :]
    tiles = []
    keys = s_ref.shape[1]
    for jt in range(keys // rows):
        kind = jnp.clip(chunk * (keys // rows) + jt - own + 2, 0, 4)
        bias = bias_ref[head0 + head, kind, pl.ds(r0, ROWS), :]
        tiles.append(s_ref[pl.ds(s0, ROWS), jt * rows : (jt + 1) * rows] + bias)
    scores = jnp.concatenate(tiles, axis=1) * 0.125
    return scores, iq == items_k, s0, r0


def vmem(*shape, dtype=jnp.float32):
    return pltpu.VMEM(shape, dtype)


def shape_of(*shape):
    return jax.ShapeDtypeStruct(shape, jnp.float32)


WHOLE = pl.BlockSpec(memory_space=pltpu.VMEM)
FAR = pl.BlockSpec(memory_space=pl.ANY)
LIMIT = 62 * 1024 * 1024


ORDER = (0, 1, 2, 3, 4, 5, 6, 7, 8, 12, 9, 10, 11, 13, 14, 15, 16, 17, 18, 19, 20, 21, 22, 23)
PQ, PP, PK, PV, PO, PA, PG, PC = range(8, 16)
PER = 6
RIM = 8
X, V1, V2, CTX, Q, ZA, ZG, GLU, V3, V4 = range(10)


def signal_rims(barrier, seq, count):
    for to in ((seq + 1) % count, (seq + count - 1) % count):
        pl.semaphore_signal(barrier, inc=1, device_id={"seq": to}, device_id_type=MESH)


def enter_all(seq, grp, zs):
    y, z = seq % 2, seq // 2
    barrier = pltpu.get_barrier_semaphore()
    for peer in (grp + 1 - 2 * (grp % 2), (grp + 2) % 4):
        pl.semaphore_signal(barrier, inc=1, device_id={"grp": peer}, device_id_type=MESH)
    pl.semaphore_signal(barrier, inc=1, device_id={"seq": z * 2 + 1 - y}, device_id_type=MESH)

    def greet(d):
        pl.semaphore_signal(
            barrier, inc=1, device_id={"seq": ((z + d) % zs) * 2 + y}, device_id_type=MESH
        )

    over(1, zs, greet)
    signal_rims(barrier, seq, 2 * zs)
    pl.semaphore_wait(barrier, zs + 4)


def joined(halves):
    size = halves.shape[1] * halves.shape[2] * halves.shape[3]
    return jnp.concatenate([halves[i].reshape(size, halves.shape[-1]) for i in range(2)], axis=1)


class Gather:
    def __init__(self, zs, rows_ref, slot_ref, owned_ref, whole, table, sib, face, own, sems):
        self.zs = zs
        self.seq, self.grp, self.z, self.y, self.x, self.c = places()
        self.rows_ref, self.slot_ref, self.owned_ref = rows_ref, slot_ref, owned_ref
        self.whole, self.table, self.sib, self.face, self.own = whole, table, sib, face, own
        (
            self.local, self.sib_s, self.sib_r, self.face_s, self.face_r, self.z_s, self.z_r,
            self.a_s, self.a_r, self.b_s, self.b_r, self.c_s, self.c_r,
        ) = sems
        self.to_core = {"grp": self.grp + 1 - 2 * self.c}
        self.to_x = {"grp": (self.grp + 2) % 4}
        self.to_y = {"seq": self.z * 2 + 1 - self.y}
        self.place = 2 * self.c + self.x
        self.other = 2 * self.c + 1 - self.x

    def mine(self, place):
        return self.rows_ref[self.slot_ref[place]] * self.owned_ref[place]

    def sib_copy(self, k):
        return remote(self.table.at[k], self.sib.at[k], self.sib_s.at[k], self.sib_r.at[k], self.to_core)

    def face_copy(self, k):
        return remote(
            self.sib.at[k, 1 - self.x], self.face.at[k], self.face_s.at[k], self.face_r.at[k], self.to_x
        )

    def z_any(self, k, d, z):
        return remote(
            self.own.at[k], self.whole.at[GROUP * k + self.place, :, z, self.y], self.z_s.at[k, d], self.z_r.at[k, d],
            {"seq": ((self.z + d) % self.zs) * 2 + self.y},
        )

    def z_copy(self, k, d):
        return self.z_any(k, d, self.z)

    def z_arrival(self, k, d):
        return self.z_any(k, d, (self.z + self.zs - d) % self.zs)

    def keep(self, k):
        return pltpu.make_async_copy(
            self.own.at[k], self.whole.at[GROUP * k + self.place, :, self.z, self.y], self.local.at[k]
        )

    def two(self, k, parts, s, r):
        return [
            remote(part, part, s.at[k, i], r.at[k, i], to) for i, (part, to) in enumerate(parts)
        ]

    def a_any(self, k, first, second):
        parts = [(first, self.to_y), (second, self.to_x)]
        return self.two(k, parts, self.a_s, self.a_r)

    def a_copies(self, k):
        block = self.whole.at[GROUP * k + self.place]
        return self.a_any(k, block.at[0, :, self.y], block.at[1, :, self.y])

    def a_arrivals(self, k):
        return self.a_any(
            k,
            self.whole.at[GROUP * k + self.place, 0, :, 1 - self.y],
            self.whole.at[GROUP * k + self.other, 1, :, self.y],
        )

    def both(self, k, core):
        return pl.ds(GROUP * k + 2 * core, 2)

    def b_any(self, k, place, y):
        parts = [
            (self.whole.at[GROUP * k + place, 0], self.to_x),
            (self.whole.at[self.both(k, self.c), 1, :, y], self.to_y),
        ]
        return self.two(k, parts, self.b_s, self.b_r)

    def b_copies(self, k):
        return self.b_any(k, self.place, self.y)

    def b_arrivals(self, k):
        return self.b_any(k, self.other, 1 - self.y)

    def c_any(self, k, core):
        part = self.whole.at[self.both(k, core)]
        return remote(part, part, self.c_s.at[k], self.c_r.at[k], self.to_core)

    def begin(self, k):
        for i in range(2):
            self.table[k, i] = self.mine(GROUP * k + 2 * (1 - self.c) + i)
        self.sib_copy(k).start()

    def to_face(self, k):
        self.sib_copy(k).wait_recv()
        for i in range(2):
            self.sib[k, i] += self.mine(GROUP * k + 2 * self.c + i)
        self.face_copy(k).start()

    def to_z(self, k):
        self.face_copy(k).wait_recv()
        self.own[k] = self.sib[k, self.x] + self.face[k]
        over(1, self.zs, lambda d: self.z_copy(k, d).start())
        self.keep(k).start()

    def to_a(self, k):
        over(1, self.zs, lambda d: self.z_arrival(k, d).wait_recv())
        self.keep(k).wait()
        for copy in self.a_copies(k):
            copy.start()

    def to_b(self, k):
        for copy in self.a_arrivals(k):
            copy.wait_recv()
        for copy in self.b_copies(k):
            copy.start()

    def to_c(self, k):
        for copy in self.b_arrivals(k):
            copy.wait_recv()
        self.c_any(k, self.c).start()

    def open(self):
        over(0, CHUNKS, self.begin)
        over(0, 5, self.to_face)
        over(0, 3, self.to_z)

    def step(self, t):
        def stage(k, fn):
            @pl.when((k >= 0) & (k < CHUNKS))
            def _():
                fn(k)

        stage(t - 2, self.to_b)
        stage(t, self.to_a)
        stage(t - 3, self.to_c)
        stage(t + 5, self.to_face)
        stage(t + 3, self.to_z)

    def arrived(self, k):
        self.c_any(k, 1 - self.c).wait_recv()

    def finish(self, k):
        self.c_any(k, self.c).wait_send()
        for copy in self.a_copies(k) + self.b_copies(k):
            copy.wait_send()
        over(1, self.zs, lambda d: self.z_copy(k, d).wait_send())
        self.face_copy(k).wait_send()
        self.sib_copy(k).wait_send()


class Share:
    def __init__(self, zs, layer, source, out, keep_sem, z_s, z_r, y_s, y_r):
        self.zs, self.layer, self.source, self.out = zs, layer, source, out
        self.seq = lax.axis_index("seq")
        self.z, self.y = self.seq // 2, self.seq % 2
        self.sems = (keep_sem, z_s, z_r, y_s, y_r)

    def z_any(self, d, z, i):
        _, z_s, z_r, _, _ = self.sems
        block = self.out.at[self.layer, z * 2 + (self.y if i == 0 else 1 - self.y)]
        return remote(
            self.source if i == 0 else block, block, z_s.at[self.layer, d, i], z_r.at[self.layer, d, i],
            {"seq": ((self.z + d) % self.zs) * 2 + self.y},
        )

    def z_copy(self, d, i):
        return self.z_any(d, self.z, i)

    def z_arrival(self, d, i):
        return self.z_any(d, (self.z + self.zs - d) % self.zs, i)

    def y_any(self, y):
        _, _, _, y_s, y_r = self.sems
        return remote(
            self.source, self.out.at[self.layer, self.z * 2 + y], y_s.at[self.layer], y_r.at[self.layer],
            {"seq": self.z * 2 + 1 - self.y},
        )

    def keep(self):
        return pltpu.make_async_copy(
            self.source, self.out.at[self.layer, self.seq], self.sems[0].at[self.layer]
        )

    def start(self):
        self.y_any(self.y).start()
        over(1, self.zs, lambda d: self.z_copy(d, 0).start())
        self.keep().start()

    def forward(self):
        self.y_any(1 - self.y).wait_recv()
        over(1, self.zs, lambda d: self.z_copy(d, 1).start())

    def wait(self):
        for i in range(2):
            over(1, self.zs, lambda d: self.z_arrival(d, i).wait_recv())
        self.keep().wait()

    def finish(self):
        self.y_any(self.y).wait_send()
        for i in range(2):
            over(1, self.zs, lambda d: self.z_copy(d, i).wait_send())


class Rims:
    def __init__(self, count, layer, low, high, before, after, sems, recv):
        seq = lax.axis_index("seq")
        self.up = remote(
            high, before.at[layer], sems.at[layer, 0], recv.at[layer, 0], {"seq": (seq + 1) % count}
        )
        self.down = remote(
            low, after.at[layer], sems.at[layer, 1], recv.at[layer, 1], {"seq": (seq + count - 1) % count}
        )

    def start(self):
        self.up.start()
        self.down.start()

    def wait(self):
        self.up.wait_recv()
        self.down.wait_recv()

    def finish(self):
        self.up.wait_send()
        self.down.wait_send()


def forward_kernel(
    zs, chunks,
    rows_ref, slot_ref, owned_ref, x_ref, small_all, table_ref, iq_ref, ik_ref, rate_ref, masks_ref,
    whole, out_ref, rows_s, z_s, hs_s, k_s, val_s, lse_s, p_s, before_s, after_s, scores_s,
    table_w, sib, face, own_w, weights, x_v, kept, z_v, h_v, hs_v, k_v, val_v, p_v, lse_v, before, after, ext, bias_ref, s_ref, e_ref, top_ref, sum_ref, acc_ref,
    local, sib_sm, sib_rm, face_sm, face_rm, z_sm, z_rm, a_sm, a_rm, b_sm, b_rm, c_sm, c_rm,
    load_sems, save_sems, keep_sem, sz_s, sz_r, sy_s, sy_r, rim_s, rim_r, key_sems,
):
    seq = lax.axis_index("seq")
    grp = lax.axis_index("grp")
    count = 2 * zs
    enter_all(seq, grp, zs)
    gather = Gather(
        zs, rows_ref, slot_ref, owned_ref, whole, table_w, sib, face, own_w,
        (local, sib_sm, sib_rm, face_sm, face_rm, z_sm, z_rm, a_sm, a_rm, b_sm, b_rm, c_sm, c_rm),
    )
    gather.open()
    for t in range(5):
        gather.step(t)
    rows, width = x_ref.shape
    x_v[...] = x_ref[...]
    half = (KERNEL - 1) // 2
    slots = (0, 1, 2, 3, 0, 1)

    def layer_body(layer, carry):
        small = small_all.at[layer]

        def block(n):
            return joined(weights[slots[n // 4], n % 4])

        def load(i):
            return pltpu.make_async_copy(
                whole.at[pl.ds(GROUP * (PER * layer + i), GROUP)], weights.at[slots[i]], load_sems.at[slots[i]]
            )

        def saves(layer):
            pairs = [(kept, rows_s), (z_v, z_s), (lse_v, lse_s), (p_v, p_s)]
            return [
                pltpu.make_async_copy(v, s.at[layer], save_sems.at[i]) for i, (v, s) in enumerate(pairs)
            ]

        share = Share(zs, layer, h_v.at[layer], hs_s, keep_sem, sz_s, sz_r, sy_s, sy_r)
        rims = Rims(
            count, layer, kept.at[GLU, 0:RIM], kept.at[GLU, rows - RIM : rows], before, after, rim_s, rim_r
        )

        def steps(*numbers):
            for i in numbers:
                gather.step(PER * layer + i)

        def arrived(*numbers):
            for i in numbers:
                gather.arrived(PER * layer + i)
                load(i).start()

        class Held:
            def __init__(self):
                self.waited = set()

            def get(self, n):
                if n // 4 not in self.waited:
                    load(n // 4).wait()
                    self.waited.add(n // 4)
                return block(n)

        held = Held()
        arrived(0, 1)

        @pl.when(layer > 0)
        def _():
            for copy in saves(layer - 1):
                copy.wait()

        v1 = ffn_forward(x_v[...], small, 0, held, 0, z_v.at[0])
        kept[X] = x_v[...]
        kept[V1] = v1
        unit, _ = norm(v1)
        h_v[layer] = unit * small[2:3] + small[3:4]
        share.start()
        steps(5)
        arrived(2)
        q = nn(split(h_v[layer]), split(held.get(PQ)))
        kept[Q] = q
        table = nn(split(table_ref[...]), split(held.get(PP)))
        p_v[...] = table
        qv = q + small[22:23]
        for d in range(2):
            cols = slice(256 * d, 256 * d + 256)
            place_bias(qv[:, cols], table[:, cols], rate_ref[...], bias_ref, 4 * d)
        share.forward()
        steps(6, 7, 8)
        arrived(3)
        share.wait()
        attention_forward(
            chunks, count, layer, held, small, hs_s, k_s, val_s, scores_s, e_ref, hs_v, k_v, val_v, kept.at[Q], ik_ref, iq_ref,
            bias_ref, s_ref, top_ref, sum_ref, acc_ref, key_sems, rows, seq, lambda d: steps(9) if d == 0 else None,
        )
        lse_v[...] = top_ref[...] + jnp.log(sum_ref[...])
        for d in range(2):
            span = slice(4 * rows * d, 4 * rows * (d + 1))
            kept[CTX, :, 256 * d : 256 * d + 256] = unstacked(acc_ref[span, :] / sum_ref[span, :], rows)
        v2 = kept[V1] + nn(split(kept[CTX]), split(held.get(PO)))
        kept[V2] = v2
        za, zg, glu = gate_forward(v2, small, held.get(PA), held.get(PG))
        kept[ZA] = za
        kept[ZG] = zg
        kept[GLU] = glu
        rims.start()
        steps(10)
        arrived(4, 5)
        rims.wait()
        fill_ext(ext, before[layer, RIM - half : RIM, :], kept[GLU], after[layer, 0:half, :])
        v3 = conv_forward(kept[V2], ext, masks_ref[...], small, held.get(PC))
        kept[V3] = v3
        v4 = ffn_forward(v3, small, 8, held, 16, z_v.at[1])
        kept[V4] = v4
        unit, _ = norm(v4)
        x_v[...] = unit * small[10:11] + small[11:12]
        for copy in saves(layer):
            copy.start()
        rims.finish()
        share.finish()
        return carry

    lax.fori_loop(0, L, layer_body, 0)
    out_ref[...] = x_v[...]
    last = [
        pltpu.make_async_copy(v, s.at[L - 1], save_sems.at[i])
        for i, (v, s) in enumerate([(kept, rows_s), (z_v, z_s), (lse_v, lse_s), (p_v, p_s)])
    ]
    edges = [
        pltpu.make_async_copy(before, before_s, save_sems.at[4]),
        pltpu.make_async_copy(after, after_s, save_sems.at[5]),
    ]
    for copy in edges:
        copy.start()
    for copy in last + edges:
        copy.wait()

    over(0, CHUNKS, gather.finish)


def attention_forward(
    chunks, count, layer, held, small, hs_s, k_s, val_s, scores_s, e_ref, hs_v, k_v, val_v, q_v, ik_ref, iq_ref,
    bias_ref, s_ref, top_ref, sum_ref, acc_ref, key_sems, rows, own, between,
):
    per = KEYS // rows
    wk, wv = split(held.get(PK)), split(held.get(PV))
    if chunks > 1:
        top_ref[...] = jnp.full_like(top_ref, -1e30)
        sum_ref[...] = jnp.zeros_like(sum_ref)
        acc_ref[...] = jnp.zeros_like(acc_ref)

    def one(chunk):
        def fetch(b):
            return pltpu.make_async_copy(
                hs_s.at[layer, chunk * per + b],
                hs_v.at[pl.ds(pl.multiple_of(b * rows, rows), rows)],
                key_sems.at[b],
            )

        over(0, per, lambda b: fetch(b).start())
        over(0, per, lambda b: fetch(b).wait())
        hs = split(hs_v[...])
        k_v[...] = nn(hs, wk)
        val_v[...] = nn(hs, wv)
        span = pl.ds(pl.multiple_of(chunk * KEYS, KEYS), KEYS)
        out = [
            pltpu.make_async_copy(k_v, k_s.at[layer, span], key_sems.at[per]),
            pltpu.make_async_copy(val_v, val_s.at[layer, span], key_sems.at[per + 1]),
        ]
        for copy in out:
            copy.start()
        items_k = ik_ref[:, span] if chunks > 1 else ik_ref[...]
        for d in range(2):
            cols = slice(256 * d, 256 * d + 256)
            qs = split(stacked(q_v[:, cols] + small[21:22, cols]))
            s_ref[...] = nt(qs, split(k_v[:, cols]))

            def tile(i):
                scores, same, s0, _ = tile_scores(
                    s_ref, bias_ref, iq_ref, items_k, i, 4 * d, own, chunk, rows
                )
                scores = jnp.where(same, scores, -1e30)
                at_rows = pl.ds(pl.multiple_of(4 * rows * d + s0, ROWS), ROWS)
                top = jnp.max(scores, axis=-1, keepdims=True)
                if chunks > 1:
                    old = top_ref[at_rows, :]
                    top = jnp.maximum(top, old)
                    factor = jnp.exp(old - top)
                s_ref[pl.ds(s0, ROWS), :] = scores
                e = jnp.where(same, jnp.exp(scores - top), 0.0)
                total = jnp.sum(e, axis=-1, keepdims=True)
                if chunks > 1:
                    total = total + sum_ref[at_rows, :] * factor
                    acc_ref[at_rows, :] = acc_ref[at_rows, :] * factor
                top_ref[at_rows, :] = top
                sum_ref[at_rows, :] = total
                high, low = split(e)
                e_ref[0, pl.ds(s0, ROWS), :] = high
                e_ref[1, pl.ds(s0, ROWS), :] = low

            over(0, 4 * rows // ROWS, tile)
            kept_scores = pltpu.make_async_copy(
                s_ref, scores_s.at[layer, d, :, span if chunks > 1 else slice(None)], key_sems.at[per + 2]
            )
            kept_scores.start()
            part = nn((e_ref[0], e_ref[1]), split(val_v[:, cols]))
            kept_scores.wait()
            span_q = slice(4 * rows * d, 4 * rows * (d + 1))
            if chunks > 1:
                acc_ref[span_q, :] += part
                pl.when(chunk == 0)(lambda d=d: between(d))
            else:
                acc_ref[span_q, :] = part
                between(d)
        for copy in out:
            copy.wait()

    if chunks > 1:
        over(0, chunks, one)
    else:
        one(0)


def run_forward(rows3, slot, owned, x, small, table, items_q, items_k, rate, masks, seq_size):
    slab = rows3.shape[2]
    width = x.shape[1]
    thin = width // 2
    rows = x.shape[0]
    zs = seq_size // 2
    frames = seq_size * rows
    dma = pltpu.SemaphoreType.DMA
    smem = pl.BlockSpec(memory_space=pltpu.SMEM)
    block = (rows, width)
    tab = table.shape
    saved = [
        (10,) + block, (2, rows, 4 * width), (seq_size, rows, width), (frames, width), (frames, width),
        (8 * rows, 1), tab, (RIM, width), (RIM, width), (2, 4 * rows, frames),
    ]
    n = CHUNKS
    return pl.pallas_call(
        functools.partial(forward_kernel, zs, frames // KEYS),
        in_specs=[WHOLE, smem, smem] + [WHOLE] * 7,
        out_specs=[FAR, WHOLE] + [FAR] * len(saved),
        out_shape=[shape_of(GROUP * n, 2, zs, 2, slab, thin), shape_of(*block)]
        + [shape_of(L, *s) for s in saved],
        scratch_shapes=[
            vmem(n, 2, 2, slab, thin), vmem(n, 2, 2, slab, thin), vmem(n, 2, slab, thin), vmem(n, 2, slab, thin),
            vmem(4, 4, 2, zs, 2, slab, thin), vmem(*block), vmem(10, *block), vmem(2, rows, 4 * width), vmem(L, *block),
            vmem(KEYS, width), vmem(KEYS, width), vmem(KEYS, width), vmem(*tab), vmem(8 * rows, 1),
            vmem(L, RIM, width), vmem(L, RIM, width),
            vmem(rows + 8, width), vmem(8, 5, rows, rows), vmem(4 * rows, KEYS),
            vmem(2, 4 * rows, KEYS, dtype=jnp.bfloat16), vmem(8 * rows, 1), vmem(8 * rows, 1), vmem(8 * rows, 256),
            dma((n,)), dma((n,)), dma((n,)), dma((n,)), dma((n,)), dma((n, zs)), dma((n, zs)),
            dma((n, 2)), dma((n, 2)), dma((n, 2)), dma((n, 2)), dma((n,)), dma((n,)),
            dma((4,)), dma((6,)), dma((L,)), dma((L, zs, 2)), dma((L, zs, 2)), dma((L,)), dma((L,)),
            dma((L, 2)), dma((L, 2)), dma((KEYS // rows + 3,)),
        ],
        compiler_params=pltpu.CompilerParams(
            collective_id=0, has_side_effects=True, vmem_limit_bytes=LIMIT
        ),
        name="forward",
    )(rows3, slot, owned, x, small, table, items_q, items_k, rate, masks)


HOLD = 4
STAGE = 3
RING = 4
BACK_KEYS = 512


class Scatter:
    def __init__(self, zs, g, out, near, own, ga, gy, gb, gz, mine, sems, free):
        self.zs = zs
        self.seq, self.grp, self.z, self.y, self.x, self.c = places()
        self.g, self.out, self.near, self.own = g, out, near, own
        self.ga, self.gy, self.gb, self.gz, self.mine = ga, gy, gb, gz, mine
        (
            self.own_sem, self.keep_sem, self.n_s, self.n_r, self.a_s, self.a_r, self.b_s, self.b_r,
            self.z_s, self.z_r, self.x_s, self.x_r, self.c_s, self.c_r,
        ) = sems
        self.near_free, self.a_free, self.b_free = free
        self.to_core = {"grp": self.grp + 1 - 2 * self.c}
        self.to_x = {"grp": (self.grp + 2) % 4}
        self.to_y = {"seq": self.z * 2 + 1 - self.y}
        self.place = 2 * self.c + self.x
        self.other = 2 * self.c + 1 - self.x

    def n_copy(self, e):
        return remote(
            self.g.at[CHUNKS - 1 - e, 1 - self.c], self.near.at[e % HOLD], self.n_s.at[e], self.n_r.at[e],
            self.to_core,
        )

    def load(self, e):
        return pltpu.make_async_copy(self.g.at[CHUNKS - 1 - e, self.c], self.own, self.own_sem)

    def a_copies(self, e):
        slot = self.near.at[e % HOLD]
        return [
            remote(
                slot.at[1 - self.x, 0], self.ga.at[e % 2], self.a_s.at[e, 0], self.a_r.at[e, 0], self.to_x
            ),
            remote(
                slot.at[:, 1, :, 1 - self.y], self.gy.at[e % 2], self.a_s.at[e, 1], self.a_r.at[e, 1], self.to_y
            ),
        ]

    def b_copies(self, e):
        slot = self.near.at[e % HOLD]
        return [
            remote(
                slot.at[self.x, 0, :, 1 - self.y], self.gb.at[e % 2, 0], self.b_s.at[e, 0], self.b_r.at[e, 0],
                self.to_y,
            ),
            remote(
                slot.at[1 - self.x, 1, :, self.y], self.gb.at[e % 2, 1], self.b_s.at[e, 1], self.b_r.at[e, 1],
                self.to_x,
            ),
        ]

    def z_copy(self, e, d):
        to = (self.z + d) % self.zs
        return remote(
            self.near.at[e % HOLD, self.x, :, to, self.y], self.gz.at[e, d - 1], self.z_s.at[e, d],
            self.z_r.at[e, d], {"seq": to * 2 + self.y},
        )

    def pair(self, e):
        return pl.ds(CHUNKS - 1 - e, 2)

    def x_any(self, e, place):
        return remote(
            self.mine.at[self.pair(e)], self.out.at[self.pair(e), place], self.x_s.at[e], self.x_r.at[e], self.to_x
        )

    def c_any(self, e, parts):
        return [
            remote(p, q, self.c_s.at[e, i], self.c_r.at[e, i], self.to_core) for i, (p, q) in enumerate(parts)
        ]

    def c_copies(self, e):
        far = self.out.at[self.pair(e), self.other]
        return self.c_any(e, [(self.mine.at[self.pair(e)], self.out.at[self.pair(e), self.place]), (far, far)])

    def c_arrivals(self, e):
        sibling = 2 * (1 - self.c) + self.x
        parts = [self.out.at[self.pair(e), p] for p in (sibling, 2 * (1 - self.c) + 1 - self.x)]
        return self.c_any(e, [(p, p) for p in parts])

    def keep(self, e):
        return pltpu.make_async_copy(
            self.mine.at[self.pair(e)], self.out.at[self.pair(e), self.place], self.keep_sem.at[e]
        )

    def start(self, e):
        @pl.when(e >= HOLD)
        def _():
            pl.semaphore_wait(self.near_free, 1)

        self.n_copy(e).start()

    def signal(self, sem, to):
        pl.semaphore_signal(sem, inc=1, device_id=to, device_id_type=MESH)

    def to_a(self, e):
        self.n_copy(e).wait_recv()
        self.load(e).wait()
        slot = e % HOLD

        def add(i):
            self.near[slot, :, :, i] += self.own[:, :, i]

        over(0, self.zs, add)

        @pl.when(e >= 2)
        def _():
            pl.semaphore_wait(self.a_free.at[0], 1)
            pl.semaphore_wait(self.a_free.at[1], 1)

        for copy in self.a_copies(e):
            copy.start()

    def to_b(self, e):
        for copy in self.a_copies(e):
            copy.wait_recv()
        slot = e % HOLD

        def add(i):
            self.near[slot, self.x, 0, i] += self.ga[e % 2, i]
            for j in range(2):
                self.near[slot, j, 1, i, self.y] += self.gy[e % 2, j, i]

        over(0, self.zs, add)

        @pl.when(e + 2 < CHUNKS)
        def _():
            self.signal(self.a_free.at[0], self.to_x)
            self.signal(self.a_free.at[1], self.to_y)

        @pl.when(e >= 2)
        def _():
            pl.semaphore_wait(self.b_free.at[0], 1)
            pl.semaphore_wait(self.b_free.at[1], 1)

        for copy in self.b_copies(e):
            copy.start()

    def to_z(self, e):
        for copy in self.b_copies(e):
            copy.wait_recv()
        slot = e % HOLD

        def add(i):
            for h in range(2):
                self.near[slot, self.x, h, i, self.y] += self.gb[e % 2, h, i]

        over(0, self.zs, add)

        @pl.when(e + 2 < CHUNKS)
        def _():
            self.signal(self.b_free.at[0], self.to_y)
            self.signal(self.b_free.at[1], self.to_x)

        over(1, self.zs, lambda d: self.z_copy(e, d).start())
        self.mine[CHUNKS - 1 - e] = self.near[slot, self.x, :, self.z, self.y]

    def to_out(self, e, last):
        k = CHUNKS - 1 - e

        def add(d):
            self.z_copy(e, d).wait_recv()
            self.mine[k] += self.gz[e, d - 1]

        over(1, self.zs, add)
        if last:
            self.x_any(e, self.place).start()
            self.keep(e).start()
        for copy in [self.n_copy(e)] + self.a_copies(e) + self.b_copies(e):
            copy.wait_send()
        over(1, self.zs, lambda d: self.z_copy(e, d).wait_send())

        @pl.when(e + HOLD < CHUNKS)
        def _():
            self.signal(self.near_free, self.to_core)

    def to_core_out(self, e):
        self.x_any(e, self.other).wait_recv()
        for copy in self.c_copies(e):
            copy.start()

    def pump(self, t, even):
        def stage(lag, fn, *rest):
            @pl.when((t >= lag) & (t - lag < CHUNKS))
            def _():
                fn(t - lag, *rest)

        stage(0, lambda e: self.load(e).start())
        if not even:
            stage(4, self.to_core_out)
        stage(3, self.to_out, even)
        stage(2, self.to_z)
        stage(1, self.to_b)
        stage(0, self.to_a)

    def finish(self, p):
        e = 2 * p + 1
        for copy in self.c_arrivals(e):
            copy.wait_recv()
        self.keep(e).wait()
        self.x_any(e, self.place).wait_send()
        for copy in self.c_copies(e):
            copy.wait_send()


class Staged:
    def __init__(self, buffer, g, sems, layer):
        self.buffer, self.g, self.sems, self.layer = buffer, g, sems, layer
        self.count, self.open = 0, {}

    def copy(self, number, slot):
        j = number % 4
        return pltpu.make_async_copy(
            self.buffer.at[slot], self.g.at[PER * self.layer + number // 4, j // 2, j % 2], self.sems.at[slot]
        )

    def put(self, number, value):
        slot = self.count % STAGE
        self.count += 1
        for other, place in list(self.open.items()):
            if place == slot:
                self.close(other)
        shape, thin = self.buffer.shape[2:], self.buffer.shape[-1]
        for i in range(2):
            self.buffer[slot, i] = value[:, i * thin : (i + 1) * thin].reshape(shape)
        self.copy(number, slot).start()
        self.open[number] = slot

    def close(self, number):
        self.copy(number, self.open.pop(number)).wait()

    def flush(self, chunk):
        for number in list(self.open):
            if number // 4 == chunk:
                self.close(number)


class Sum:
    def __init__(self, zs, layer, d, from_y, from_z, held, extra, load_sem, y_s, y_r, z_s, z_r):
        self.zs, self.layer, self.d = zs, layer, d
        self.from_y, self.from_z, self.held, self.extra = from_y, from_z, held, extra
        self.sems = (load_sem, y_s, y_r, z_s, z_r)
        seq = lax.axis_index("seq")
        self.z, self.y = seq // 2, seq % 2

    def y_copy(self, to):
        _, y_s, y_r, _, _ = self.sems
        return remote(
            self.d.at[self.layer, to * 2 + 1 - self.y], self.from_y.at[self.layer, to],
            y_s.at[self.layer, to], y_r.at[self.layer, to], {"seq": self.z * 2 + 1 - self.y},
        )

    def z_copy(self, to):
        _, _, _, z_s, z_r = self.sems
        return remote(
            self.held.at[to % RING], self.from_z.at[self.layer, self.z], z_s.at[self.layer, to],
            z_r.at[self.layer, self.z], {"seq": to * 2 + self.y},
        )

    def z_arrival(self, source):
        _, _, _, z_s, z_r = self.sems
        return remote(
            self.held.at[source % RING], self.from_z.at[self.layer, source], z_s.at[self.layer, source],
            z_r.at[self.layer, source], {"seq": source * 2 + self.y},
        )

    def fetch(self, source, to, i):
        return pltpu.make_async_copy(source, to, self.sems[0].at[i])

    def both(self, z, to):
        own = self.fetch(self.d.at[self.layer, z * 2 + self.y], to, 0)
        own.start()
        self.y_copy(z).wait_recv()
        got = self.fetch(self.from_y.at[self.layer, z], self.extra, 1)
        got.start()
        own.wait()
        got.wait()
        to[...] += self.extra[...]

    def start(self, low, high):
        over(low, high, lambda z: self.y_copy(z).start())

    def forward(self, low, high):
        def one(to):
            @pl.when((to >= RING) & (to - RING != self.z))
            def _():
                self.z_copy(to - RING).wait_send()

            @pl.when(to != self.z)
            def _():
                self.both(to, self.held.at[to % RING])
                self.z_copy(to).start()

        over(low, high, one)

    def result(self, out):
        self.both(self.z, out)

        def add(source):
            @pl.when(source != self.z)
            def _():
                self.z_arrival(source).wait_recv()
                got = self.fetch(self.from_z.at[self.layer, source], self.extra, 1)
                got.start()
                got.wait()
                out[...] += self.extra[...]

        over(0, self.zs, add)

    def finish(self):
        over(0, self.zs, lambda z: self.y_copy(z).wait_send())

        def sent(to):
            @pl.when(to != self.z)
            def _():
                self.z_copy(to).wait_send()

        over(max(0, self.zs - RING), self.zs, sent)


def backward_kernel(
    zs, chunks,
    cot_ref, small_all, table_ref, rate_ref, masks_ref, whole,
    rows_s, zz_s, hs_s, k_s, val_s, lse_s, p_s, before_s, after_s, scores_s,
    grad_ref, out, small_out, g, dh_s, from_y, from_z,
    weights, staging, near, own, ga, gy, gb, gz, mine, grad_v, kept, z_v, hs_v, k_v, val_v,
    lse_v, p_v, before_v, after_v, ext, dext, rim_before, rim_after,
    s_ref, dp_ref, dctx_v, delta_v, dq_v, dwin, left_v, right_v, dh_own_v, dh_v, held_v, extra_v,
    ds_all, srecv, szr,
    own_sem, keep_sem, n_s, n_r, a_s, a_r, b_s, b_r, z_s, z_r, x_sm, x_rm, c_s, c_r, near_free, a_free, b_free,
    load_sems, save_sems, stage_sems, rim_s, rim_r, key_sems, sum_load, sy_s, sy_r, sz_s, sz_r,
    t_s, t_r, tz_s, tz_r,
):
    seq = lax.axis_index("seq")
    grp = lax.axis_index("grp")
    count = 2 * zs
    enter_all(seq, grp, zs)
    scatter = Scatter(
        zs, g, out, near, own, ga, gy, gb, gz, mine,
        (own_sem, keep_sem, n_s, n_r, a_s, a_r, b_s, b_r, z_s, z_r, x_sm, x_rm, c_s, c_r),
        (near_free, a_free, b_free),
    )
    rows, width = cot_ref.shape
    half = (KERNEL - 1) // 2
    grad_v[...] = cot_ref[...]
    edges = [
        pltpu.make_async_copy(before_s, before_v, save_sems.at[4]),
        pltpu.make_async_copy(after_s, after_v, save_sems.at[5]),
    ]
    for copy in edges:
        copy.start()
    for copy in edges:
        copy.wait()

    def layer_body(lay, carry):
        layer = L - 1 - lay
        e0 = PER * lay
        small = small_all.at[layer]
        ds_ref = ds_all.at[layer]
        ds_ref[...] = jnp.zeros_like(ds_ref)
        staged = Staged(staging, g, stage_sems, layer)

        class Held:
            def __init__(self):
                self.where, self.waited = {}, set()

            def copy(self, chunk):
                return pltpu.make_async_copy(
                    whole.at[pl.ds(GROUP * (PER * layer + chunk), GROUP)],
                    weights.at[pl.ds(GROUP * self.where[chunk], GROUP)],
                    load_sems.at[self.where[chunk]],
                )

            def begin(self, chunk, place):
                self.where[chunk] = place
                self.copy(chunk).start()

            def get(self, n):
                chunk = n // 4
                if chunk not in self.waited:
                    self.copy(chunk).wait()
                    self.waited.add(chunk)
                return joined(weights[GROUP * self.where[chunk] + n % 4])

        def starts(*numbers):
            for i in numbers:
                scatter.start(e0 + i)

        def early(*numbers):
            pl.when(lay == 0)(lambda: starts(*numbers))

        def late(*numbers):
            pl.when(lay > 0)(lambda: starts(*numbers))

        def pumps(*numbers):
            for i in numbers:
                scatter.pump(e0 + i, i % 2 == 0)

        held = Held()
        pairs = {
            "rows": (rows_s.at[layer], kept), "z": (zz_s.at[layer, 1], z_v), "lse": (lse_s.at[layer], lse_v),
            "p": (p_s.at[layer], p_v), "z1": (zz_s.at[layer, 0], z_v),
        }

        def saved(name):
            source, to = pairs[name]
            return pltpu.make_async_copy(source, to, save_sems.at[list(pairs).index(name) % 4])

        for name in ("rows", "z"):
            saved(name).start()
        held.begin(5, 1)
        held.begin(4, 0)
        held.begin(3, 2)
        for name in ("lse", "p"):
            saved(name).start()
        keys = Keys(chunks, layer, hs_s, k_s, val_s, scores_s, hs_v, k_v, val_v, s_ref, key_sems, rows)
        keys.start(0)
        for d in range(2):
            keys.scores(0, d).start()

        saved("rows").wait()
        saved("z").wait()
        unit, scale = norm(kept[V4])
        grad, dg, dc = norm_back(grad_v[...], unit, scale, small[10:11])
        ds_ref[10:11] = dg
        ds_ref[11:12] = dc

        def second_half():
            staged.flush(5)
            early(0)
            pumps(-1)
            late(0)

        grad = ffn_backward(
            grad, kept[V3], z_v, small, 8, held, 16, staged, 16, ds_ref,
            second_half,
        )
        staged.flush(4)
        early(1)
        grad_v[...] = grad
        saved("z1").start()
        fill_ext(ext, before_v[layer, RIM - half : RIM, :], kept[GLU], after_v[layer, 0:half, :])
        conv_backward(grad, ext, masks_ref[...], small, held.get(PC), staged, PC, dext, ds_ref)
        rims = Rims(
            count, layer, dext.at[0:RIM], dext.at[rows + 2 * half - RIM : rows + 2 * half],
            rim_before, rim_after, rim_s, rim_r,
        )
        rims.start()
        held.begin(2, 0)
        pumps(0)
        late(1)

        saved("lse").wait()
        saved("p").wait()
        rims.wait()
        dq_v[...] = dext[half : half + rows, :]
        dq_v[0:half, :] += rim_before[layer, RIM - half : RIM, :]
        dq_v[rows - half : rows, :] += rim_after[layer, 0:half, :]
        grad = gate_backward(
            dq_v[...], grad_v[...], kept[V2], kept[ZA], kept[ZG], small, held.get(PA), held.get(PG),
            staged, PA, ds_ref,
        )
        grad_v[...] = grad
        halves = split(grad)
        staged.put(PO, tn(split(kept[CTX]), halves))
        dctx = nt(halves, split(held.get(PO)))
        dctx_v[...] = dctx
        staged.flush(3)
        held.begin(0, 2)
        early(2)

        prod = dctx_v[...] * kept[CTX]
        for d in range(2):
            cols = slice(256 * d, 256 * d + 256)
            delta_v[4 * rows * d : 4 * rows * (d + 1), :] = jnp.sum(
                stacked(prod[:, cols]), axis=-1, keepdims=True
            )
        pumps(1)
        late(2)
        total = Sum(
            zs, layer, dh_s, from_y, from_z, held_v, extra_v, sum_load, sy_s, sy_r, sz_s, sz_r
        )

        def between():
            pumps(2)

        attention_backward(
            chunks, layer, keys, held, small, staged, kept.at[Q], lse_v,
            dctx_v, delta_v, s_ref, dp_ref, dq_v, dwin, left_v, right_v, weights.at[4:6], dh_s, key_sems,
            rows, seq, between, total,
        )
        total.forward(0, zs // 2)
        attention_ends(
            held, small, staged, rate_ref, table_ref, kept.at[Q], p_v, dq_v, dwin, left_v, right_v, kept.at[V1], dh_own_v,
            ds_ref, rows,
        )
        held.begin(1, 1)
        staged.flush(2)
        starts(3)
        total.forward(zs // 2, zs)
        pumps(3)
        total.result(dh_v)
        unit, scale = norm(kept[V1])
        back, dg, dc = norm_back(dh_own_v[...] + dh_v[...], unit, scale, small[2:3])
        ds_ref[2:3] = dg
        ds_ref[3:4] = dc
        grad = grad_v[...] + back
        saved("z1").wait()

        def first_half():
            staged.flush(1)
            starts(4)
            pumps(4)

        grad_v[...] = ffn_backward(
            grad, kept[X], z_v, small, 0, held, 0, staged, 0, ds_ref, first_half
        )
        staged.flush(0)
        starts(5)
        rims.finish()
        total.finish()
        return carry

    lax.fori_loop(0, L, layer_body, 0)
    grad_ref[...] = grad_v[...]

    z, y = seq // 2, seq % 2
    devices = (
        {"grp": grp + 1 - 2 * (grp % 2)}, {"grp": (grp + 2) % 4}, {"seq": z * 2 + 1 - y},
    )

    def t_copy(i):
        return remote(ds_all, srecv.at[i], t_s.at[i], t_r.at[i], devices[i])

    for i in range(3):
        t_copy(i).start()
        scatter.pump(CHUNKS - 1 + i, i % 2 == 1)
        t_copy(i).wait()
        ds_all[...] += srecv[i]

    def tz_any(d, block):
        return remote(
            ds_all, szr.at[block], tz_s.at[d], tz_r.at[d], {"seq": ((z + d) % zs) * 2 + y}
        )

    over(1, zs, lambda d: tz_any(d, z).start())
    for t in range(CHUNKS + 2, CHUNKS + 4):
        scatter.pump(t, t % 2 == 0)

    def arrived(d):
        tz_any(d, (z + zs - d) % zs).wait_recv()
        tz_any(d, z).wait_send()

    over(1, zs, arrived)
    szr[z] = ds_all[...]
    small_out[...] = szr[0]

    def add(i):
        small_out[...] += szr[i]

    over(1, zs, add)
    over(0, CHUNKS // 2, scatter.finish)


class Keys:
    def __init__(self, chunks, layer, hs_s, k_s, val_s, scores_s, hs_v, k_v, val_v, s_ref, sems, rows):
        self.chunks, self.layer, self.rows = chunks, layer, rows
        self.hs_s, self.k_s, self.val_s = hs_s, k_s, val_s
        self.hs, self.k, self.val, self.sems = hs_v, k_v, val_v, sems
        self.scores_s, self.s_ref = scores_s, s_ref

    def scores(self, chunk, d):
        span = pl.ds(chunk * BACK_KEYS if isinstance(chunk, int) else pl.multiple_of(chunk * BACK_KEYS, BACK_KEYS), BACK_KEYS)
        return pltpu.make_async_copy(
            self.scores_s.at[self.layer, d, :, span], self.s_ref.at[d],
            self.sems.at[BACK_KEYS // self.rows + 2 + d],
        )

    def any(self, chunk, fn):
        per = BACK_KEYS // self.rows
        span = pl.ds(chunk * BACK_KEYS if isinstance(chunk, int) else pl.multiple_of(chunk * BACK_KEYS, BACK_KEYS), BACK_KEYS)
        fn(pltpu.make_async_copy(self.k_s.at[self.layer, span], self.k, self.sems.at[per]))
        fn(pltpu.make_async_copy(self.val_s.at[self.layer, span], self.val, self.sems.at[per + 1]))

        def one(b):
            fn(
                pltpu.make_async_copy(
                    self.hs_s.at[self.layer, chunk * per + b],
                    self.hs.at[pl.ds(pl.multiple_of(b * self.rows, self.rows), self.rows)],
                    self.sems.at[b],
                )
            )

        over(0, per, one)

    def start(self, chunk):
        self.any(chunk, lambda copy: copy.start())

    def wait(self, chunk):
        self.any(chunk, lambda copy: copy.wait())


def attention_backward(
    chunks, layer, keys, held, small, staged, q_v, lse_v,
    dctx_v, delta_v, s_ref, dp_ref, dq_v, dwin, left_v, right_v, dwkv, dh_s, key_sems,
    rows, own, between, total,
):
    per = BACK_KEYS // rows
    wk, wv = split(held.get(PK)), split(held.get(PV))
    dq_v[...] = jnp.zeros_like(dq_v)
    dwin[...] = jnp.zeros_like(dwin)
    left_v[...] = jnp.zeros_like(left_v)
    right_v[...] = jnp.zeros_like(right_v)
    if chunks > 1:
        for i in range(2):
            dwkv[i] = jnp.zeros(dwkv.shape[1:], F32)

    def quad(d, chunk):
        cols = slice(256 * d, 256 * d + 256)
        tall_q = stacked(q_v[:, cols] + small[21:22, cols])
        tall_c = stacked(dctx_v[:, cols])
        ks = split(keys.k[:, cols])
        dp_ref[...] = nt(split(tall_c), split(keys.val[:, cols]))
        keys.scores(chunk, d).wait()
        blocks = [chunk * per + jt for jt in range(per)]
        before = [jnp.where(block <= own - 2, 1.0, 0.0) for block in blocks]
        after = [jnp.where(block >= own + 2, 1.0, 0.0) for block in blocks]

        def tile(i):
            s0 = pl.multiple_of(i * ROWS, ROWS)
            at_rows = pl.ds(pl.multiple_of(4 * rows * d + s0, ROWS), ROWS)
            p = jnp.exp(s_ref[d, pl.ds(s0, ROWS), :] - lse_v[at_rows, :])
            s_ref[d, pl.ds(s0, ROWS), :] = p
            grad = p * (dp_ref[pl.ds(s0, ROWS), :] - delta_v[at_rows, :]) * 0.125
            dp_ref[pl.ds(s0, ROWS), :] = grad
            left = right = None
            for jt in range(per):
                part = grad[:, jt * rows : (jt + 1) * rows]
                left = part * before[jt] if left is None else left + part * before[jt]
                right = part * after[jt] if right is None else right + part * after[jt]
            left_v[at_rows, :] += jnp.sum(left, axis=-1, keepdims=True)
            right_v[at_rows, :] += jnp.sum(right, axis=-1, keepdims=True)

        over(0, 4 * rows // ROWS, tile)
        for i in range(3):
            block = own - 1 + i - chunk * per

            @pl.when((block >= 0) & (block < per))
            def _():
                lanes = pl.ds(pl.multiple_of(block * rows, rows), rows)
                dwin[d, :, i * rows : (i + 1) * rows] = dp_ref[:, lanes]

        dss = split(dp_ref[...])
        dq_v[:, cols] += unstacked(nn(dss, ks), rows)
        keys.val[:, cols] = nn(split(tall_c.T), split(s_ref[d])).T
        keys.k[:, cols] = nn(split(tall_q.T), dss).T
        if chunks > 1:

            @pl.when(chunk + 1 < chunks)
            def _():
                keys.scores(chunk + 1, d).start()

    def one(chunk):
        keys.wait(chunk)
        quad(0, chunk)
        quad(1, chunk)
        hst = split(keys.hs[...].T)
        dk, dval = split(keys.k[...]), split(keys.val[...])
        keys.hs[...] = nt(dk, wk) + nt(dval, wv)

        def store(b):
            return pltpu.make_async_copy(
                keys.hs.at[pl.ds(pl.multiple_of(b * rows, rows), rows)],
                dh_s.at[layer, chunk * per + b],
                key_sems.at[b],
            )

        over(0, per, lambda b: store(b).start())
        dwk, dwv = nn(hst, dk), nn(hst, dval)
        over(0, per, lambda b: store(b).wait())
        total.start(chunk * (per // 2), (chunk + 1) * (per // 2))
        if chunks > 1:
            thin = dwk.shape[1] // 2
            for i, value in enumerate((dwk, dwv)):
                for j in range(2):
                    dwkv[i, j] += value[:, j * thin : (j + 1) * thin].reshape(dwkv.shape[2:])
        else:
            staged.put(PK, dwk)
            staged.put(PV, dwv)
        if chunks > 1:
            pl.when(chunk + 1 < chunks)(lambda: keys.start(chunk + 1))
        pl.when(chunk == 0)(between)

    if chunks > 1:
        over(0, chunks, one)
        staged.put(PK, joined(dwkv[0]))
        staged.put(PV, joined(dwkv[1]))
    else:
        one(0)


def attention_ends(
    held, small, staged, rate_ref, table_ref, q_v, p_v, dq_v, dwin, left_v, right_v, v1_v, dh_own_v, ds_ref, rows,
):
    lane = lax.broadcasted_iota(jnp.int32, (rows, 128), 1)
    shape = (rows, 3 * rows)
    place = lax.broadcasted_iota(jnp.int32, shape, 1) - lax.broadcasted_iota(jnp.int32, shape, 0) - 65
    rate = rate_ref[...]
    qv = q_v[...] + small[22:23]
    dqu = dq_v[...]
    ds_ref[21:22] = jnp.sum(dqu, axis=0, keepdims=True)
    dtable, dqv = [], []
    for d in range(2):
        cols = slice(256 * d, 256 * d + 256)
        near = []
        for n in range(4):
            whole_window = dwin[d, n * rows : (n + 1) * rows, :]
            window = turned(whole_window)
            back = pltpu.roll(window, 3 * rows - 192, 1, stride=1, stride_axis=0)
            back = turned(back[:, :128])
            span = slice(4 * rows * d + n * rows, 4 * rows * d + (n + 1) * rows)
            left = left_v[span, :] + jnp.sum(
                jnp.where(place < 0, whole_window, 0.0), axis=-1, keepdims=True
            )
            right = right_v[span, :] + jnp.sum(
                jnp.where(place > 127, whole_window, 0.0), axis=-1, keepdims=True
            )
            back = back + jnp.where(lane == 0, left, 0.0)
            back = back + jnp.where(lane == 127, right, 0.0)
            near.append(
                jnp.concatenate(
                    [jnp.where(rate == 2, 0.0, back), jnp.where(rate == 2, back, 0.0)], axis=1
                )
            )
        near = split(jnp.concatenate(near, axis=0))
        dtable.append(tn_long(near, split(stacked(qv[:, cols]))))
        dqv.append(unstacked(nn(near, split(p_v[:, cols])), rows))
    dqv = jnp.concatenate(dqv, axis=1)
    ds_ref[22:23] = jnp.sum(dqv, axis=0, keepdims=True)
    staged.put(PP, tn_long(split(table_ref[...]), split(jnp.concatenate(dtable, axis=1))))
    dq = split(dqu + dqv)
    unit, _ = norm(v1_v[...])
    staged.put(PQ, tn(split(unit * small[2:3] + small[3:4]), dq))
    dh_own_v[...] = nt(dq, split(held.get(PQ)))


def run_backward(cot, small, table, rate, masks, whole, saved, seq_size):
    slab = whole.shape[-2]
    width = cot.shape[1]
    half_width = width // 2
    rows = cot.shape[0]
    zs = seq_size // 2
    frames = seq_size * rows
    chunks = frames // BACK_KEYS
    dma = pltpu.SemaphoreType.DMA
    regular = pltpu.SemaphoreType.REGULAR
    block = (rows, width)
    thin = (zs, 2, slab, half_width)
    square = (2,) + thin
    n = CHUNKS
    stream = (L, seq_size, rows, width)
    half = (L, zs, rows, width)
    return pl.pallas_call(
        functools.partial(backward_kernel, zs, chunks),
        in_specs=[WHOLE] * 5 + [FAR] + [FAR] * len(saved),
        out_specs=[WHOLE, FAR, WHOLE, FAR, FAR, FAR, FAR],
        out_shape=[
            shape_of(*block), shape_of(n, GROUP, 2, slab, half_width), shape_of(L, 24, width),
            shape_of(n, 2, 2, *square), shape_of(*stream), shape_of(*half), shape_of(*half),
        ],
        scratch_shapes=[
            vmem(12, *square), vmem(STAGE, *square), vmem(HOLD, 2, *square), vmem(2, *square),
            vmem(2, *thin), vmem(2, 2, zs, slab, half_width), vmem(2, 2, zs, slab, half_width),
            vmem(n, zs - 1, 2, slab, half_width), vmem(n, 2, slab, half_width),
            vmem(*block), vmem(10, *block), vmem(rows, 4 * width), vmem(BACK_KEYS, width), vmem(BACK_KEYS, width),
            vmem(BACK_KEYS, width), vmem(8 * rows, 1), vmem(*table.shape), vmem(L, RIM, width), vmem(L, RIM, width),
            vmem(rows + 8, width), vmem(rows + 8, width), vmem(L, RIM, width), vmem(L, RIM, width),
            vmem(2, 4 * rows, BACK_KEYS), vmem(4 * rows, BACK_KEYS), vmem(*block), vmem(8 * rows, 1),
            vmem(*block), vmem(2, 4 * rows, 3 * rows), vmem(8 * rows, 1), vmem(8 * rows, 1), vmem(*block),
            vmem(*block), vmem(RING, *block), vmem(*block),
            vmem(L, 24, width), vmem(3, L, 24, width),
            vmem(zs, L, 24, width),
            dma, dma((n,)), dma((n,)), dma((n,)), dma((n, 2)), dma((n, 2)), dma((n, 2)), dma((n, 2)),
            dma((n, zs)), dma((n, zs)), dma((n,)), dma((n,)), dma((n, 2)), dma((n, 2)),
            regular, regular((2,)), regular((2,)),
            dma((3,)), dma((6,)), dma((STAGE,)), dma((L, 2)), dma((L, 2)), dma((BACK_KEYS // rows + 4,)), dma((2,)),
            dma((L, zs)), dma((L, zs)), dma((L, zs)), dma((L, zs)), dma((3,)), dma((3,)), dma((zs,)), dma((zs,)),
        ],
        compiler_params=pltpu.CompilerParams(
            collective_id=1, has_side_effects=True, vmem_limit_bytes=LIMIT
        ),
        name="backward",
    )(cot, small, table, rate, masks, whole, *saved)


def on_device(
    frames_in,
    cotangent,
    lengths,
    rate_flags,
    owner_list,
    master,
    moment_one,
    moment_two,
    average,
    small_params,
    small_moment_one,
    small_moment_two,
    small_average,
):
    local_rows, hidden_width = frames_in.shape[1:]
    seq_size = lax.axis_size("seq")
    me = lax.axis_index("grp")
    slab = hidden_width // seq_size
    stream_rows = local_rows * seq_size
    first_row = lax.axis_index("seq") * local_rows
    half_width = (KERNEL - 1) // 2
    lengths_row = lengths[0]
    flags_row = rate_flags[0]
    own_index = first_row + jnp.arange(local_rows, dtype=jnp.int32)
    own_items, _ = frame_info(own_index, lengths_row, flags_row)
    item_numbers = jnp.arange(lengths_row.shape[0], dtype=jnp.int32)
    rate = 1 + jnp.sum(
        jnp.where(own_items[:, None] == item_numbers[None, :], flags_row[None, :], 0),
        axis=1,
        keepdims=True,
    )
    key_items, _ = frame_info(jnp.arange(stream_rows, dtype=jnp.int32), lengths_row, flags_row)
    rim_index = first_row - half_width + jnp.arange(local_rows + 2 * half_width, dtype=jnp.int32)
    rim_items, _ = frame_info(rim_index, lengths_row, flags_row)
    masks = jnp.stack(
        [
            (rim_items[tap : tap + local_rows] == own_items).astype(jnp.float32)
            for tap in range(KERNEL)
        ],
        axis=1,
    )
    items_q, items_k = own_items[:, None], key_items[None, :]
    table = position_tables(hidden_width)

    places_of = jnp.concatenate([24 * layer + jnp.array(ORDER, jnp.int32) for layer in range(L)])
    slot_of = slot_index(owner_list)[places_of]
    local_slot = slot_of - me * CAP
    owned = ((local_slot >= 0) & (local_slot < CAP)).astype(jnp.int32)
    local_slot = jnp.clip(local_slot, 0, CAP - 1)
    w, values, *saved = run_forward(
        master.reshape(CAP, slab, 2, hidden_width // 2).transpose(0, 2, 1, 3), local_slot, owned.astype(jnp.float32), frames_in[0],
        small_params, table, items_q, items_k, rate, masks, seq_size,
    )
    grad, shares, small_sum = run_backward(
        cotangent[0], small_params, table, rate, masks, w, saved, seq_size
    )[:3]
    small_total = small_sum[:, : small_params.shape[1]]
    here = (
        slot_of[None, :] == (me * CAP + jnp.arange(CAP, dtype=jnp.int32))[:, None]
    ).astype(jnp.int32)
    used = jnp.sum(here, axis=1)
    block_of = jnp.sum(here * jnp.arange(here.shape[1], dtype=jnp.int32)[None, :], axis=1)
    new_master, master_copy, new_one, new_two, new_average = update_slots(
        shares.reshape((-1,) + shares.shape[2:]), block_of, used.astype(jnp.float32)[:, None],
        master, moment_one, moment_two, average,
    )
    new_small, new_small_one, new_small_two = adam_step(
        small_params, small_moment_one, small_moment_two, small_total, RATE_SMALL, 0.0
    )
    new_small_average = AVERAGE_KEEP * small_average + (1.0 - AVERAGE_KEEP) * new_small
    return (
        values[None],
        grad[None],
        new_master,
        master_copy,
        new_one,
        new_two,
        new_average,
        new_small,
        new_small_one,
        new_small_two,
        new_small_average,
    )


def solution(mesh):
    in_specs = (
        P("grp", "seq", None),
        P("grp", "seq", None),
        P("grp", None),
        P("grp", None),
        P(),
        P("grp", "seq"),
        P("grp", "seq"),
        P("grp", "seq"),
        P("grp", "seq"),
        P(),
        P(),
        P(),
        P(),
    )
    out_specs = (
        P("grp", "seq", None),
        P("grp", "seq", None),
        P("grp", "seq"),
        P("grp", "seq"),
        P("grp", "seq"),
        P("grp", "seq"),
        P("grp", "seq"),
        P(),
        P(),
        P(),
        P(),
    )
    return jax.shard_map(
        on_device, mesh=mesh, in_specs=in_specs, out_specs=out_specs, check_vma=False
    )
```

```python
import functools
import math

import jax
import jax.numpy as jnp
import numpy as np
from jax import lax
from jax.experimental import pallas as pl
from jax.experimental.pallas import tpu as pltpu
from jax.sharding import PartitionSpec as P

HEADS = 8
KERNEL = 9
NB = 128
L = 2
CAP = 16
STEP = 10
EPS_NORM = 1e-05
BETA_ONE = 0.9
BETA_TWO = 0.999
ADAM_EPS = 1e-08
RATE_MATRIX = 0.03
RATE_SMALL = 0.1
DECAY_WEIGHT = 0.01
AVERAGE_KEEP = 0.99


def position_tables(width):
    falling = NB // 2 - 1 - np.arange(NB)
    doubled = np.clip(2 * falling, -(NB // 2), NB // 2 - 1)
    offset = np.concatenate([falling, doubled]).astype(np.float64)[:, None]
    column = np.arange(width)
    frequency = np.exp(-math.log(10000.0) * (2 * (column // 2)) / width)[None, :]
    angles = offset * frequency
    return jnp.asarray(np.where(column[None, :] % 2 == 0, np.sin(angles), np.cos(angles)), jnp.float32)


def frame_info(frame_index, lengths_row, flags_row):
    item_ends = jnp.cumsum(lengths_row)
    item_starts = item_ends - lengths_row
    inside = (frame_index[:, None] >= item_starts[None, :]) & (
        frame_index[:, None] < item_ends[None, :]
    )
    numbers = jnp.arange(lengths_row.shape[0], dtype=jnp.int32)
    frame_items = jnp.sum(jnp.where(inside, numbers[None, :] + 1, 0), axis=1) - 1
    first_frame = jnp.sum(jnp.where(inside, item_starts[None, :], 0), axis=1)
    stride = jnp.sum(jnp.where(inside, 1 + flags_row[None, :], 0), axis=1)
    return (frame_items, (frame_index - first_frame) * stride)


def slot_index(owner_list):
    owners = owner_list[:, 0]
    numbers = jnp.arange(owners.shape[0], dtype=jnp.int32)
    earlier = (owners[None, :] == owners[:, None]) & (numbers[None, :] < numbers[:, None])
    owner_rank = jnp.sum(earlier.astype(jnp.int32), axis=1)
    return owners * CAP + owner_rank


def adam_step(attention_weights, first_moment, second_moment, gradient, step_rate, decay_rate):
    first_moment = BETA_ONE * first_moment + (1.0 - BETA_ONE) * gradient
    second_moment = BETA_TWO * second_moment + (1.0 - BETA_TWO) * gradient * gradient
    fixed_one = 1.0 - BETA_ONE**STEP
    fixed_two = 1.0 - BETA_TWO**STEP
    direction = first_moment / fixed_one / (jnp.sqrt(second_moment / fixed_two) + ADAM_EPS)
    return (
        attention_weights - step_rate * (direction + decay_rate * attention_weights),
        first_moment,
        second_moment,
    )


MESH = pl.DeviceIdType.MESH
CHUNKS = 12
GROUP = 4


def places():
    seq = lax.axis_index("seq")
    grp = lax.axis_index("grp")
    return seq, grp, seq // 2, seq % 2, grp // 2, grp % 2


def over(lo, hi, fn):
    def body(i, carry):
        fn(i)
        return carry

    lax.fori_loop(lo, hi, body, 0)


def remote(src, dst, s, r, dev):
    return pltpu.make_async_remote_copy(
        src_ref=src, dst_ref=dst, send_sem=s, recv_sem=r, device_id=dev, device_id_type=MESH
    )


def update_kernel(
    block_ref, used_ref, shares_ref, master_ref, one_ref, two_ref, average_ref,
    new_master, copy, new_one, new_two, new_average, rows_ref, sems,
):
    i = pl.program_id(0)
    slots = master_ref.shape[0]

    def fetch(s):
        return pltpu.make_async_copy(shares_ref.at[block_ref[s]], rows_ref.at[s], sems.at[s])

    @pl.when(i == 0)
    def _():
        over(0, slots, lambda s: fetch(s).start())
        over(0, slots, lambda s: fetch(s).wait())

    half = rows_ref.shape[-1]
    pieces = []
    for r in range(8):
        for h in range(2):
            pieces.append(rows_ref[:, h, i * 8 + r, :])
    gradient = jnp.concatenate(pieces, axis=1) * used_ref[...]
    master = master_ref[...]
    master, one, two = adam_step(
        master, one_ref[...], two_ref[...], gradient, RATE_MATRIX, DECAY_WEIGHT
    )
    new_master[...] = master
    copy[...] = master.astype(jnp.bfloat16)
    new_one[...] = one
    new_two[...] = two
    new_average[...] = AVERAGE_KEEP * average_ref[...] + (1.0 - AVERAGE_KEEP) * master


def update_slots(shares, block, used, master, moment_one, moment_two, average):
    slab, half = shares.shape[2:]
    slots, entries = master.shape
    columns = 8 * 2 * half
    spec = pl.BlockSpec((slots, columns), lambda i, block: (0, i))
    full = jax.ShapeDtypeStruct((slots, entries), jnp.float32)
    return pl.pallas_call(
        update_kernel,
        grid_spec=pltpu.PrefetchScalarGridSpec(
            num_scalar_prefetch=1,
            grid=(slab // 8,),
            in_specs=[
                pl.BlockSpec((slots, 1), lambda i, block: (0, 0)), pl.BlockSpec(memory_space=pl.ANY),
                spec, spec, spec, spec,
            ],
            out_specs=[spec] * 5,
            scratch_shapes=[
                pltpu.VMEM((slots, 2, slab, half), jnp.float32), pltpu.SemaphoreType.DMA((slots,)),
            ],
        ),
        out_shape=[full, jax.ShapeDtypeStruct((slots, entries), jnp.bfloat16), full, full, full],
        compiler_params=pltpu.CompilerParams(vmem_limit_bytes=LIMIT),
        name="update_slots",
    )(block, used, shares, master, moment_one, moment_two, average)


BF16 = jnp.bfloat16
F32 = jnp.float32
ROWS = 32
KEYS = 1024


def split(value):
    high = value.astype(BF16)
    return high, (value - high.astype(F32)).astype(BF16)


def dot(left, right, dims):
    return lax.dot_general(left, right, (dims, ((), ())), preferred_element_type=F32)


def dot3(left, right, dims):
    (lh, ll), (rh, rl) = left, right
    rows = lh.shape[0]
    if dims[0] == (1,) and rows <= 128:
        both = dot(jnp.concatenate([lh, ll], axis=0), rh, dims)
        return both[:rows] + (both[rows:] + dot(lh, rl, dims))
    return dot(lh, rh, dims) + (dot(ll, rh, dims) + dot(lh, rl, dims))


def nn(left, right):
    return dot3(left, right, ((1,), (0,)))


def nt(left, right):
    return dot3(left, right, ((1,), (1,)))


def tn(left, right):
    (lh, ll), (rh, rl) = left, right
    return dot(
        jnp.concatenate([lh, lh, ll], axis=0),
        jnp.concatenate([rh, rl, rh], axis=0),
        ((0,), (0,)),
    )


def tn_long(left, right):
    return dot3(left, right, ((0,), (0,)))


def norm(value):
    center = value - jnp.mean(value, axis=-1, keepdims=True)
    scale = lax.rsqrt(jnp.mean(center * center, axis=-1, keepdims=True) + EPS_NORM)
    return center * scale, scale


def norm_back(grad, unit, scale, gain):
    inner = grad * gain
    value_grad = scale * (
        inner
        - jnp.mean(inner, axis=-1, keepdims=True)
        - unit * jnp.mean(inner * unit, axis=-1, keepdims=True)
    )
    return (
        value_grad,
        jnp.sum(grad * unit, axis=0, keepdims=True),
        jnp.sum(grad, axis=0, keepdims=True),
    )


def sigmoid(value):
    return 1.0 / (1.0 + jnp.exp(-value))


def ffn_forward(v, small, row, weights, first, z_ref, middle=None):
    unit, _ = norm(v)
    h = split(unit * small[row : row + 1] + small[row + 1 : row + 2])
    total = None
    for j in range(4):
        z = nn(h, split(weights.get(first + j)))
        z_ref[:, 512 * j : 512 * j + 512] = z
        part = nn(split(z * sigmoid(z)), split(weights.get(first + 4 + j)))
        total = part if total is None else total + part
        if j == 1 and middle is not None:
            middle()
    return v + 0.5 * total


def ffn_backward(grad, v, z_ref, small, row, weights, first, grads, at, ds_ref, middle):
    unit, scale = norm(v)
    gain = small[row : row + 1]
    hth, htl = split((unit * gain + small[row + 1 : row + 2]).T)
    wide = jnp.concatenate([hth, hth, htl], axis=1)
    half = split(0.5 * grad)
    for j in range(4):
        z = z_ref[:, 512 * j : 512 * j + 512]
        grads.put(at + 4 + j, tn(split(z * sigmoid(z)), half))
    middle()
    total = None
    for j in range(4):
        z = z_ref[:, 512 * j : 512 * j + 512]
        s = sigmoid(z)
        da = nt(half, split(weights.get(first + 4 + j)))
        dz = split(da * (s * (1.0 + z * (1.0 - s))))
        tall = jnp.concatenate([dz[0], dz[1], dz[0]], axis=0)
        grads.put(at + j, dot(wide, tall, ((1,), (0,))))
        part = nt(dz, split(weights.get(first + j)))
        total = part if total is None else total + part
    back, dg, dc = norm_back(total, unit, scale, gain)
    ds_ref[row : row + 1] = dg
    ds_ref[row + 1 : row + 2] = dc
    return grad + back


def conv_mix(ext_ref, masks, small):
    mixed = None
    for t in range(KERNEL):
        part = ext_ref[t : t + masks.shape[0], :] * masks[:, t : t + 1] * small[12 + t : 13 + t]
        mixed = part if mixed is None else mixed + part
    return mixed


def conv_forward(v, ext_ref, masks, small, wc):
    unit, _ = norm(conv_mix(ext_ref, masks, small))
    n = unit * small[6:7] + small[7:8]
    return v + nn(split(n * sigmoid(n)), split(wc))


def conv_backward(grad, ext_ref, masks, small, wc, grads, at, dext_ref, ds_ref):
    unit, scale = norm(conv_mix(ext_ref, masks, small))
    gain = small[6:7]
    n = unit * gain + small[7:8]
    s = sigmoid(n)
    g = split(grad)
    grads.put(at, tn(split(n * s), g))
    dn = nt(g, split(wc)) * (s * (1.0 + n * (1.0 - s)))
    dm, dg, dc = norm_back(dn, unit, scale, gain)
    ds_ref[6:7] = dg
    ds_ref[7:8] = dc
    rows = masks.shape[0]
    dext_ref[...] = jnp.zeros_like(dext_ref)
    for t in range(KERNEL):
        dmt = dm * masks[:, t : t + 1]
        ds_ref[12 + t : 13 + t] = jnp.sum(dmt * ext_ref[t : t + rows, :], axis=0, keepdims=True)
        dext_ref[t : t + rows, :] += dmt * small[12 + t : 13 + t]


def fill_ext(ext_ref, low, middle, high):
    half = (KERNEL - 1) // 2
    rows = middle.shape[0]
    ext_ref[0:half, :] = low
    ext_ref[half : half + rows, :] = middle
    ext_ref[half + rows : 2 * half + rows, :] = high


def gate_forward(v, small, wa, wg):
    unit, _ = norm(v)
    h = split(unit * small[4:5] + small[5:6])
    za, zg = nn(h, split(wa)), nn(h, split(wg))
    return za, zg, za * sigmoid(zg)


def gate_backward(grad_glu, grad, v, za, zg, small, wa, wg, grads, at, ds_ref):
    unit, scale = norm(v)
    gain = small[4:5]
    h = split(unit * gain + small[5:6])
    s = sigmoid(zg)
    da = split(grad_glu * s)
    dg_ = split(grad_glu * za * s * (1.0 - s))
    grads.put(at, tn(h, da))
    grads.put(at + 1, tn(h, dg_))
    back, dg, dc = norm_back(nt(da, split(wa)) + nt(dg_, split(wg)), unit, scale, gain)
    ds_ref[4:5] = dg
    ds_ref[5:6] = dc
    return grad + back


def stacked(quad):
    rows = quad.shape[0]
    tall = jnp.concatenate([quad] * 4, axis=0)
    shape = (4 * rows, 256)
    head = lax.broadcasted_iota(jnp.int32, shape, 0) // rows
    lane = lax.broadcasted_iota(jnp.int32, shape, 1) // 64
    return jnp.where(head == lane, tall, 0.0)


def unstacked(tall, rows):
    shape = (rows, 256)
    lane = lax.broadcasted_iota(jnp.int32, shape, 1) // 64
    quad = tall[0:rows]
    for n in range(1, 4):
        quad = jnp.where(lane == n, tall[n * rows : (n + 1) * rows], quad)
    return quad


def turned(value):
    rows = value.shape[0]
    shape = (rows, rows)
    place = lax.broadcasted_iota(jnp.int32, shape, 0) + lax.broadcasted_iota(jnp.int32, shape, 1)
    swap = jnp.where(place == rows - 1, 1.0, 0.0).astype(BF16)
    high, low = split(value)
    return dot(swap, high, ((1,), (0,))) + dot(swap, low, ((1,), (0,)))


def place_bias(quad_q, table, rate, bias_ref, head0):
    rows = quad_q.shape[0]
    near = nt(split(stacked(quad_q)), split(table))
    row = lax.broadcasted_iota(jnp.int32, (rows, 3 * rows), 0)
    column = lax.broadcasted_iota(jnp.int32, (rows, 3 * rows), 1)
    place = column - row - 65
    for n in range(4):
        both = near[n * rows : (n + 1) * rows]
        one = jnp.where(rate == 2, both[:, 128:], both[:, :128])
        last, first = one[:, 0:1], one[:, 127:128]
        wide = jnp.concatenate([one, jnp.zeros((rows, 2 * rows), F32)], axis=1)
        rolled = pltpu.roll(wide, 65, 1, stride=1, stride_axis=0)
        window = jnp.where(place < 0, last, jnp.where(place > 127, first, rolled))
        bias_ref[head0 + n, 0] = jnp.broadcast_to(last, (rows, rows))
        for i in range(3):
            bias_ref[head0 + n, 1 + i] = window[:, i * rows : (i + 1) * rows]
        bias_ref[head0 + n, 4] = jnp.broadcast_to(first, (rows, rows))


def tile_scores(s_ref, bias_ref, items_q, items_k, tile, head0, own, chunk, rows):
    per = rows // ROWS
    head, part = tile // per, tile % per
    r0 = pl.multiple_of(part * ROWS, ROWS)
    s0 = pl.multiple_of(tile * ROWS, ROWS)
    iq = items_q[pl.ds(r0, ROWS), :]
    tiles = []
    keys = s_ref.shape[1]
    for jt in range(keys // rows):
        kind = jnp.clip(chunk * (keys // rows) + jt - own + 2, 0, 4)
        bias = bias_ref[head0 + head, kind, pl.ds(r0, ROWS), :]
        tiles.append(s_ref[pl.ds(s0, ROWS), jt * rows : (jt + 1) * rows] + bias)
    scores = jnp.concatenate(tiles, axis=1) * 0.125
    return scores, iq == items_k, s0, r0


def vmem(*shape, dtype=jnp.float32):
    return pltpu.VMEM(shape, dtype)


def shape_of(*shape):
    return jax.ShapeDtypeStruct(shape, jnp.float32)


WHOLE = pl.BlockSpec(memory_space=pltpu.VMEM)
FAR = pl.BlockSpec(memory_space=pl.ANY)
LIMIT = 62 * 1024 * 1024


ORDER = (0, 1, 2, 3, 4, 5, 6, 7, 8, 12, 9, 10, 11, 13, 14, 15, 16, 17, 18, 19, 20, 21, 22, 23)
PQ, PP, PK, PV, PO, PA, PG, PC = range(8, 16)
PER = 6
RIM = 8
X, V1, V2, CTX, Q, ZA, ZG, GLU, V3, V4 = range(10)


def signal_rims(barrier, seq, count):
    for to in ((seq + 1) % count, (seq + count - 1) % count):
        pl.semaphore_signal(barrier, inc=1, device_id={"seq": to}, device_id_type=MESH)


def enter_all(seq, grp, zs):
    y, z = seq % 2, seq // 2
    barrier = pltpu.get_barrier_semaphore()
    for peer in (grp + 1 - 2 * (grp % 2), (grp + 2) % 4):
        pl.semaphore_signal(barrier, inc=1, device_id={"grp": peer}, device_id_type=MESH)
    pl.semaphore_signal(barrier, inc=1, device_id={"seq": z * 2 + 1 - y}, device_id_type=MESH)

    def greet(d):
        pl.semaphore_signal(
            barrier, inc=1, device_id={"seq": ((z + d) % zs) * 2 + y}, device_id_type=MESH
        )

    over(1, zs, greet)
    signal_rims(barrier, seq, 2 * zs)
    pl.semaphore_wait(barrier, zs + 4)


def side(even):
    return 0 if even else 1


def joined(halves):
    size = halves.shape[1] * halves.shape[2] * halves.shape[3]
    return jnp.concatenate([halves[i].reshape(size, halves.shape[-1]) for i in range(2)], axis=1)


class Gather:
    def __init__(self, zs, rows_ref, slot_ref, owned_ref, whole, table, sib, face, own, sems):
        self.zs = zs
        self.seq, self.grp, self.z, self.y, self.x, self.c = places()
        self.rows_ref, self.slot_ref, self.owned_ref = rows_ref, slot_ref, owned_ref
        self.whole, self.table, self.sib, self.face, self.own = whole, table, sib, face, own
        (
            self.local, self.sib_s, self.sib_r, self.face_s, self.face_r, self.z_s, self.z_r,
            self.a_s, self.a_r, self.b_s, self.b_r, self.c_s, self.c_r,
        ) = sems
        self.to_core = {"grp": self.grp + 1 - 2 * self.c}
        self.to_x = {"grp": (self.grp + 2) % 4}
        self.to_y = {"seq": self.z * 2 + 1 - self.y}
        self.place = 2 * self.c + self.x
        self.other = 2 * self.c + 1 - self.x

    def mine(self, place):
        return self.rows_ref[self.slot_ref[place]] * self.owned_ref[place]

    def sib_copy(self, k):
        return remote(self.table.at[k], self.sib.at[k], self.sib_s.at[k], self.sib_r.at[k], self.to_core)

    def face_copy(self, k):
        return remote(
            self.sib.at[k, 1 - self.x], self.face.at[k], self.face_s.at[k], self.face_r.at[k], self.to_x
        )

    def z_any(self, t, d, even, z):
        return remote(
            self.own.at[t // 2, side(even)],
            self.whole.at[GROUP * (t // 2) + self.place, side(even), z, self.y],
            self.z_s.at[t, d], self.z_r.at[t, d],
            {"seq": ((self.z + d) % self.zs) * 2 + self.y},
        )

    def z_copy(self, t, d, even):
        return self.z_any(t, d, even, self.z)

    def z_arrival(self, t, d, even):
        return self.z_any(t, d, even, (self.z + self.zs - d) % self.zs)

    def keep(self, k):
        return pltpu.make_async_copy(
            self.own.at[k], self.whole.at[GROUP * k + self.place, :, self.z, self.y], self.local.at[k]
        )

    def a_copy(self, t, even):
        part = self.whole.at[GROUP * (t // 2) + self.place, side(even), :, self.y]
        return remote(part, part, self.a_s.at[t], self.a_r.at[t], self.to_y if even else self.to_x)

    def a_arrival(self, t, even):
        first = GROUP * (t // 2)
        if even:
            part = self.whole.at[first + self.place, side(even), :, 1 - self.y]
        else:
            part = self.whole.at[first + self.other, side(even), :, self.y]
        return remote(part, part, self.a_s.at[t], self.a_r.at[t], self.to_y if even else self.to_x)

    def both(self, t, core):
        return pl.ds(GROUP * (t // 2) + 2 * core, 2)

    def b_any(self, t, even, place):
        if even:
            part = self.whole.at[GROUP * (t // 2) + place, 0]
        else:
            part = self.whole.at[self.both(t, self.c), 1, :, place]
        to = self.to_x if even else self.to_y
        return remote(part, part, self.b_s.at[t], self.b_r.at[t], to)

    def b_copy(self, t, even):
        return self.b_any(t, even, self.place if even else self.y)

    def b_arrival(self, t, even):
        return self.b_any(t, even, self.other if even else 1 - self.y)

    def c_any(self, t, even, core):
        part = self.whole.at[self.both(t, core), side(even)]
        return remote(part, part, self.c_s.at[t], self.c_r.at[t], self.to_core)

    def c_copy(self, t, even):
        return self.c_any(t, even, self.c)

    def c_arrival(self, t, even):
        return self.c_any(t, even, 1 - self.c)

    def begin(self, k):
        for i in range(2):
            self.table[k, i] = self.mine(GROUP * k + 2 * (1 - self.c) + i)
        self.sib_copy(k).start()

    def to_face(self, k):
        self.sib_copy(k).wait_recv()
        for i in range(2):
            self.sib[k, i] += self.mine(GROUP * k + 2 * self.c + i)
        self.face_copy(k).start()

    def to_z(self, t, even):
        if even:
            k = t // 2
            self.face_copy(k).wait_recv()
            self.own[k] = self.sib[k, self.x] + self.face[k]
            self.keep(k).start()
        over(1, self.zs, lambda d: self.z_copy(t, d, even).start())

    def to_a(self, t, even):
        over(1, self.zs, lambda d: self.z_arrival(t, d, even).wait_recv())
        if even:
            self.keep(t // 2).wait()
        self.a_copy(t, even).start()

    def to_b(self, t, even):
        self.a_arrival(t, even).wait_recv()
        self.b_copy(t, even).start()

    def to_c(self, t, even):
        self.b_arrival(t, even).wait_recv()
        self.c_copy(t, even).start()

    def open(self):
        over(0, CHUNKS, self.begin)
        over(0, 6, self.to_face)
        for t in range(4):
            self.to_z(t, t % 2 == 0)

    def step(self, t, even):
        steps = 2 * CHUNKS

        @pl.when((t >= 4) & (t - 4 < steps))
        def _():
            self.to_c(t - 4, even)

        @pl.when((t >= 2) & (t - 2 < steps))
        def _():
            self.to_b(t - 2, even)

        @pl.when(t < steps)
        def _():
            self.to_a(t, even)

        if even:

            @pl.when(t // 2 + 6 < CHUNKS)
            def _():
                self.to_face(t // 2 + 6)

        @pl.when(t + 4 < steps)
        def _():
            self.to_z(t + 4, even)

    def arrived(self, k):
        for even in (True, False):
            self.c_arrival(2 * k + (0 if even else 1), even).wait_recv()

    def finish(self, k):
        for even in (True, False):
            t = 2 * k + (0 if even else 1)
            self.c_copy(t, even).wait_send()
            self.b_copy(t, even).wait_send()
            self.a_copy(t, even).wait_send()
            over(1, self.zs, lambda d: self.z_copy(t, d, even).wait_send())
        self.face_copy(k).wait_send()
        self.sib_copy(k).wait_send()


class Share:
    def __init__(self, zs, layer, source, out, keep_sem, z_s, z_r, y_s, y_r):
        self.zs, self.layer, self.source, self.out = zs, layer, source, out
        self.seq = lax.axis_index("seq")
        self.z, self.y = self.seq // 2, self.seq % 2
        self.sems = (keep_sem, z_s, z_r, y_s, y_r)

    def z_any(self, d, z, i):
        _, z_s, z_r, _, _ = self.sems
        block = self.out.at[self.layer, z * 2 + (self.y if i == 0 else 1 - self.y)]
        return remote(
            self.source if i == 0 else block, block, z_s.at[self.layer, d, i], z_r.at[self.layer, d, i],
            {"seq": ((self.z + d) % self.zs) * 2 + self.y},
        )

    def z_copy(self, d, i):
        return self.z_any(d, self.z, i)

    def z_arrival(self, d, i):
        return self.z_any(d, (self.z + self.zs - d) % self.zs, i)

    def y_any(self, y):
        _, _, _, y_s, y_r = self.sems
        return remote(
            self.source, self.out.at[self.layer, self.z * 2 + y], y_s.at[self.layer], y_r.at[self.layer],
            {"seq": self.z * 2 + 1 - self.y},
        )

    def keep(self):
        return pltpu.make_async_copy(
            self.source, self.out.at[self.layer, self.seq], self.sems[0].at[self.layer]
        )

    def start(self):
        self.y_any(self.y).start()
        over(1, self.zs, lambda d: self.z_copy(d, 0).start())
        self.keep().start()

    def forward(self):
        self.y_any(1 - self.y).wait_recv()
        over(1, self.zs, lambda d: self.z_copy(d, 1).start())

    def wait(self):
        for i in range(2):
            over(1, self.zs, lambda d: self.z_arrival(d, i).wait_recv())
        self.keep().wait()

    def finish(self):
        self.y_any(self.y).wait_send()
        for i in range(2):
            over(1, self.zs, lambda d: self.z_copy(d, i).wait_send())


class Rims:
    def __init__(self, count, layer, low, high, before, after, sems, recv):
        seq = lax.axis_index("seq")
        self.up = remote(
            high, before.at[layer], sems.at[layer, 0], recv.at[layer, 0], {"seq": (seq + 1) % count}
        )
        self.down = remote(
            low, after.at[layer], sems.at[layer, 1], recv.at[layer, 1], {"seq": (seq + count - 1) % count}
        )

    def start(self):
        self.up.start()
        self.down.start()

    def wait(self):
        self.up.wait_recv()
        self.down.wait_recv()

    def finish(self):
        self.up.wait_send()
        self.down.wait_send()


def forward_kernel(
    zs, chunks,
    rows_ref, slot_ref, owned_ref, x_ref, small_all, table_ref, iq_ref, ik_ref, rate_ref, masks_ref,
    whole, out_ref, rows_s, z_s, hs_s, k_s, val_s, lse_s, p_s, before_s, after_s, scores_s,
    table_w, sib, face, own_w, weights, x_v, kept, z_v, h_v, hs_v, k_v, val_v, p_v, lse_v, before, after, ext, bias_ref, s_ref, e_ref, top_ref, sum_ref, acc_ref,
    local, sib_sm, sib_rm, face_sm, face_rm, z_sm, z_rm, a_sm, a_rm, b_sm, b_rm, c_sm, c_rm,
    load_sems, save_sems, keep_sem, sz_s, sz_r, sy_s, sy_r, rim_s, rim_r, key_sems,
):
    seq = lax.axis_index("seq")
    grp = lax.axis_index("grp")
    count = 2 * zs
    enter_all(seq, grp, zs)
    gather = Gather(
        zs, rows_ref, slot_ref, owned_ref, whole, table_w, sib, face, own_w,
        (local, sib_sm, sib_rm, face_sm, face_rm, z_sm, z_rm, a_sm, a_rm, b_sm, b_rm, c_sm, c_rm),
    )
    gather.open()
    for t in range(8):
        gather.step(t, t % 2 == 0)
    rows, width = x_ref.shape
    x_v[...] = x_ref[...]
    half = (KERNEL - 1) // 2
    slots = (0, 1, 2, 3, 0, 1)

    def layer_body(layer, carry):
        small = small_all.at[layer]

        def block(n):
            return joined(weights[slots[n // 4], n % 4])

        def load(i):
            return pltpu.make_async_copy(
                whole.at[pl.ds(GROUP * (PER * layer + i), GROUP)], weights.at[slots[i]], load_sems.at[slots[i]]
            )

        def saves(layer):
            pairs = [(kept, rows_s), (z_v, z_s), (lse_v, lse_s), (p_v, p_s)]
            return [
                pltpu.make_async_copy(v, s.at[layer], save_sems.at[i]) for i, (v, s) in enumerate(pairs)
            ]

        share = Share(zs, layer, h_v.at[layer], hs_s, keep_sem, sz_s, sz_r, sy_s, sy_r)
        rims = Rims(
            count, layer, kept.at[GLU, 0:RIM], kept.at[GLU, rows - RIM : rows], before, after, rim_s, rim_r
        )

        def steps(*numbers):
            for i in numbers:
                gather.step(2 * PER * layer + i, i % 2 == 0)

        def arrived(*numbers):
            for i in numbers:
                gather.arrived(PER * layer + i)
                load(i).start()

        class Held:
            def __init__(self):
                self.waited = set()

            def get(self, n):
                if n // 4 not in self.waited:
                    load(n // 4).wait()
                    self.waited.add(n // 4)
                return block(n)

        held = Held()
        arrived(0, 1)

        @pl.when(layer > 0)
        def _():
            for copy in saves(layer - 1):
                copy.wait()

        v1 = ffn_forward(x_v[...], small, 0, held, 0, z_v.at[0])
        kept[X] = x_v[...]
        kept[V1] = v1
        unit, _ = norm(v1)
        h_v[layer] = unit * small[2:3] + small[3:4]
        share.start()
        steps(8, 9)
        arrived(2)
        q = nn(split(h_v[layer]), split(held.get(PQ)))
        kept[Q] = q
        table = nn(split(table_ref[...]), split(held.get(PP)))
        p_v[...] = table
        qv = q + small[22:23]
        for d in range(2):
            cols = slice(256 * d, 256 * d + 256)
            place_bias(qv[:, cols], table[:, cols], rate_ref[...], bias_ref, 4 * d)
        share.forward()
        steps(10, 11, 12, 13)
        arrived(3)
        share.wait()
        attention_forward(
            chunks, count, layer, held, small, hs_s, k_s, val_s, scores_s, e_ref, hs_v, k_v, val_v, kept.at[Q], ik_ref, iq_ref,
            bias_ref, s_ref, top_ref, sum_ref, acc_ref, key_sems, rows, seq, lambda d: steps(14, 15) if d == 0 else None,
        )
        lse_v[...] = top_ref[...] + jnp.log(sum_ref[...])
        for d in range(2):
            span = slice(4 * rows * d, 4 * rows * (d + 1))
            kept[CTX, :, 256 * d : 256 * d + 256] = unstacked(acc_ref[span, :] / sum_ref[span, :], rows)
        v2 = kept[V1] + nn(split(kept[CTX]), split(held.get(PO)))
        kept[V2] = v2
        za, zg, glu = gate_forward(v2, small, held.get(PA), held.get(PG))
        kept[ZA] = za
        kept[ZG] = zg
        kept[GLU] = glu
        rims.start()
        steps(16)
        arrived(4)
        steps(17)
        rims.wait()
        fill_ext(ext, before[layer, RIM - half : RIM, :], kept[GLU], after[layer, 0:half, :])
        v3 = conv_forward(kept[V2], ext, masks_ref[...], small, held.get(PC))
        kept[V3] = v3
        arrived(5)
        v4 = ffn_forward(v3, small, 8, held, 16, z_v.at[1], lambda: steps(18))
        kept[V4] = v4
        unit, _ = norm(v4)
        x_v[...] = unit * small[10:11] + small[11:12]
        for copy in saves(layer):
            copy.start()
        steps(19)
        rims.finish()
        share.finish()
        return carry

    lax.fori_loop(0, L, layer_body, 0)
    out_ref[...] = x_v[...]
    last = [
        pltpu.make_async_copy(v, s.at[L - 1], save_sems.at[i])
        for i, (v, s) in enumerate([(kept, rows_s), (z_v, z_s), (lse_v, lse_s), (p_v, p_s)])
    ]
    edges = [
        pltpu.make_async_copy(before, before_s, save_sems.at[4]),
        pltpu.make_async_copy(after, after_s, save_sems.at[5]),
    ]
    for copy in edges:
        copy.start()
    for copy in last + edges:
        copy.wait()

    over(0, CHUNKS, gather.finish)


def attention_forward(
    chunks, count, layer, held, small, hs_s, k_s, val_s, scores_s, e_ref, hs_v, k_v, val_v, q_v, ik_ref, iq_ref,
    bias_ref, s_ref, top_ref, sum_ref, acc_ref, key_sems, rows, own, between,
):
    per = KEYS // rows
    wk, wv = split(held.get(PK)), split(held.get(PV))
    if chunks > 1:
        top_ref[...] = jnp.full_like(top_ref, -1e30)
        sum_ref[...] = jnp.zeros_like(sum_ref)
        acc_ref[...] = jnp.zeros_like(acc_ref)

    def one(chunk):
        def fetch(b):
            return pltpu.make_async_copy(
                hs_s.at[layer, chunk * per + b],
                hs_v.at[pl.ds(pl.multiple_of(b * rows, rows), rows)],
                key_sems.at[b],
            )

        over(0, per, lambda b: fetch(b).start())
        over(0, per, lambda b: fetch(b).wait())
        hs = split(hs_v[...])
        k_v[...] = nn(hs, wk)
        val_v[...] = nn(hs, wv)
        span = pl.ds(pl.multiple_of(chunk * KEYS, KEYS), KEYS)
        out = [
            pltpu.make_async_copy(k_v, k_s.at[layer, span], key_sems.at[per]),
            pltpu.make_async_copy(val_v, val_s.at[layer, span], key_sems.at[per + 1]),
        ]
        for copy in out:
            copy.start()
        items_k = ik_ref[:, span] if chunks > 1 else ik_ref[...]
        for d in range(2):
            cols = slice(256 * d, 256 * d + 256)
            qs = split(stacked(q_v[:, cols] + small[21:22, cols]))
            s_ref[...] = nt(qs, split(k_v[:, cols]))

            def tile(i):
                scores, same, s0, _ = tile_scores(
                    s_ref, bias_ref, iq_ref, items_k, i, 4 * d, own, chunk, rows
                )
                scores = jnp.where(same, scores, -1e30)
                at_rows = pl.ds(pl.multiple_of(4 * rows * d + s0, ROWS), ROWS)
                top = jnp.max(scores, axis=-1, keepdims=True)
                if chunks > 1:
                    old = top_ref[at_rows, :]
                    top = jnp.maximum(top, old)
                    factor = jnp.exp(old - top)
                s_ref[pl.ds(s0, ROWS), :] = scores
                e = jnp.where(same, jnp.exp(scores - top), 0.0)
                total = jnp.sum(e, axis=-1, keepdims=True)
                if chunks > 1:
                    total = total + sum_ref[at_rows, :] * factor
                    acc_ref[at_rows, :] = acc_ref[at_rows, :] * factor
                top_ref[at_rows, :] = top
                sum_ref[at_rows, :] = total
                high, low = split(e)
                e_ref[0, pl.ds(s0, ROWS), :] = high
                e_ref[1, pl.ds(s0, ROWS), :] = low

            over(0, 4 * rows // ROWS, tile)
            kept_scores = pltpu.make_async_copy(
                s_ref, scores_s.at[layer, d, :, span if chunks > 1 else slice(None)], key_sems.at[per + 2]
            )
            kept_scores.start()
            part = nn((e_ref[0], e_ref[1]), split(val_v[:, cols]))
            kept_scores.wait()
            span_q = slice(4 * rows * d, 4 * rows * (d + 1))
            if chunks > 1:
                acc_ref[span_q, :] += part
                pl.when(chunk == 0)(lambda d=d: between(d))
            else:
                acc_ref[span_q, :] = part
                between(d)
        for copy in out:
            copy.wait()

    if chunks > 1:
        over(0, chunks, one)
    else:
        one(0)


def run_forward(rows3, slot, owned, x, small, table, items_q, items_k, rate, masks, seq_size):
    slab = rows3.shape[2]
    width = x.shape[1]
    thin = width // 2
    rows = x.shape[0]
    zs = seq_size // 2
    frames = seq_size * rows
    dma = pltpu.SemaphoreType.DMA
    smem = pl.BlockSpec(memory_space=pltpu.SMEM)
    block = (rows, width)
    tab = table.shape
    saved = [
        (10,) + block, (2, rows, 4 * width), (seq_size, rows, width), (frames, width), (frames, width),
        (8 * rows, 1), tab, (RIM, width), (RIM, width), (2, 4 * rows, frames),
    ]
    n = CHUNKS
    return pl.pallas_call(
        functools.partial(forward_kernel, zs, frames // KEYS),
        in_specs=[WHOLE, smem, smem] + [WHOLE] * 7,
        out_specs=[FAR, WHOLE] + [FAR] * len(saved),
        out_shape=[shape_of(GROUP * n, 2, zs, 2, slab, thin), shape_of(*block)]
        + [shape_of(L, *s) for s in saved],
        scratch_shapes=[
            vmem(n, 2, 2, slab, thin), vmem(n, 2, 2, slab, thin), vmem(n, 2, slab, thin), vmem(n, 2, slab, thin),
            vmem(4, 4, 2, zs, 2, slab, thin), vmem(*block), vmem(10, *block), vmem(2, rows, 4 * width), vmem(L, *block),
            vmem(KEYS, width), vmem(KEYS, width), vmem(KEYS, width), vmem(*tab), vmem(8 * rows, 1),
            vmem(L, RIM, width), vmem(L, RIM, width),
            vmem(rows + 8, width), vmem(8, 5, rows, rows), vmem(4 * rows, KEYS),
            vmem(2, 4 * rows, KEYS, dtype=jnp.bfloat16), vmem(8 * rows, 1), vmem(8 * rows, 1), vmem(8 * rows, 256),
            dma((n,)), dma((n,)), dma((n,)), dma((n,)), dma((n,)), dma((2 * n, zs)), dma((2 * n, zs)),
            dma((2 * n,)), dma((2 * n,)), dma((2 * n,)), dma((2 * n,)), dma((2 * n,)), dma((2 * n,)),
            dma((4,)), dma((6,)), dma((L,)), dma((L, zs, 2)), dma((L, zs, 2)), dma((L,)), dma((L,)),
            dma((L, 2)), dma((L, 2)), dma((KEYS // rows + 3,)),
        ],
        compiler_params=pltpu.CompilerParams(
            collective_id=0, has_side_effects=True, vmem_limit_bytes=LIMIT
        ),
        name="forward",
    )(rows3, slot, owned, x, small, table, items_q, items_k, rate, masks)


HOLD = 5
LANDED = 3
STAGE = 3
RING = 4
BACK_KEYS = 512


class Scatter:
    def __init__(self, zs, g, out, near, own, ga, gy, gb, gz, gz_v, mine, sems, free):
        self.zs = zs
        self.seq, self.grp, self.z, self.y, self.x, self.c = places()
        self.g, self.out, self.near, self.own = g, out, near, own
        self.ga, self.gy, self.gb, self.gz, self.gz_v, self.mine = ga, gy, gb, gz, gz_v, mine
        (
            self.own_sem, self.keep_sem, self.n_s, self.n_r, self.a_s, self.a_r, self.b_s, self.b_r,
            self.z_s, self.z_r, self.x_s, self.x_r, self.c_s, self.c_r,
        ) = sems
        self.near_free, self.a_free, self.b_free = free
        self.to_core = {"grp": self.grp + 1 - 2 * self.c}
        self.to_x = {"grp": (self.grp + 2) % 4}
        self.to_y = {"seq": self.z * 2 + 1 - self.y}
        self.place = 2 * self.c + self.x
        self.other = 2 * self.c + 1 - self.x

    def n_copy(self, e):
        return remote(
            self.g.at[CHUNKS - 1 - e, 1 - self.c], self.near.at[e % HOLD], self.n_s.at[e], self.n_r.at[e],
            self.to_core,
        )

    def load(self, e):
        return pltpu.make_async_copy(self.g.at[CHUNKS - 1 - e, self.c], self.own, self.own_sem.at[0])

    def a_copies(self, e):
        slot = self.near.at[e % HOLD]
        return [
            remote(
                slot.at[1 - self.x, 0], self.ga.at[e % LANDED], self.a_s.at[e, 0], self.a_r.at[e, 0], self.to_x
            ),
            remote(
                slot.at[:, 1, :, 1 - self.y], self.gy.at[e % LANDED], self.a_s.at[e, 1], self.a_r.at[e, 1], self.to_y
            ),
        ]

    def b_copies(self, e):
        slot = self.near.at[e % HOLD]
        return [
            remote(
                slot.at[self.x, 0, :, 1 - self.y], self.gb.at[e % 2, 0], self.b_s.at[e, 0], self.b_r.at[e, 0],
                self.to_y,
            ),
            remote(
                slot.at[1 - self.x, 1, :, self.y], self.gb.at[e % 2, 1], self.b_s.at[e, 1], self.b_r.at[e, 1],
                self.to_x,
            ),
        ]

    def z_copy(self, e, d):
        to = (self.z + d) % self.zs
        return remote(
            self.near.at[e % HOLD, self.x, :, to, self.y], self.gz.at[e, d - 1], self.z_s.at[e, d],
            self.z_r.at[e, d], {"seq": to * 2 + self.y},
        )

    def pair(self, e):
        return pl.ds(CHUNKS - 1 - e, 2)

    def x_any(self, e, place):
        return remote(
            self.mine.at[self.pair(e)], self.out.at[self.pair(e), place], self.x_s.at[e], self.x_r.at[e], self.to_x
        )

    def c_any(self, e, parts):
        return [
            remote(p, q, self.c_s.at[e, i], self.c_r.at[e, i], self.to_core) for i, (p, q) in enumerate(parts)
        ]

    def c_copies(self, e):
        far = self.out.at[self.pair(e), self.other]
        return self.c_any(e, [(self.mine.at[self.pair(e)], self.out.at[self.pair(e), self.place]), (far, far)])

    def c_arrivals(self, e):
        sibling = 2 * (1 - self.c) + self.x
        parts = [self.out.at[self.pair(e), p] for p in (sibling, 2 * (1 - self.c) + 1 - self.x)]
        return self.c_any(e, [(p, p) for p in parts])

    def keep(self, e):
        return pltpu.make_async_copy(
            self.mine.at[self.pair(e)], self.out.at[self.pair(e), self.place], self.keep_sem.at[e]
        )

    def start(self, e):
        @pl.when(e >= HOLD)
        def _():
            pl.semaphore_wait(self.near_free, 1)

        self.n_copy(e).start()

    def signal(self, sem, to):
        pl.semaphore_signal(sem, inc=1, device_id=to, device_id_type=MESH)

    def to_a(self, e):
        self.n_copy(e).wait_recv()
        self.load(e).wait()
        slot = e % HOLD

        def add(i):
            self.near[slot, :, :, i] += self.own[:, :, i]

        over(0, self.zs, add)

        @pl.when(e >= LANDED)
        def _():
            pl.semaphore_wait(self.a_free.at[0], 1)
            pl.semaphore_wait(self.a_free.at[1], 1)

        for copy in self.a_copies(e):
            copy.start()

    def to_b(self, e):
        for copy in self.a_copies(e):
            copy.wait_recv()
        slot = e % HOLD

        def add(i):
            self.near[slot, self.x, 0, i] += self.ga[e % LANDED, i]
            for j in range(2):
                self.near[slot, j, 1, i, self.y] += self.gy[e % LANDED, j, i]

        over(0, self.zs, add)

        @pl.when(e + LANDED < CHUNKS)
        def _():
            self.signal(self.a_free.at[0], self.to_x)
            self.signal(self.a_free.at[1], self.to_y)

        @pl.when(e >= 2)
        def _():
            pl.semaphore_wait(self.b_free.at[0], 1)
            pl.semaphore_wait(self.b_free.at[1], 1)

        for copy in self.b_copies(e):
            copy.start()

    def to_z(self, e):
        for copy in self.b_copies(e):
            copy.wait_recv()
        slot = e % HOLD

        def add(i):
            for h in range(2):
                self.near[slot, self.x, h, i, self.y] += self.gb[e % 2, h, i]

        over(0, self.zs, add)

        @pl.when(e + 2 < CHUNKS)
        def _():
            self.signal(self.b_free.at[0], self.to_y)
            self.signal(self.b_free.at[1], self.to_x)

        over(1, self.zs, lambda d: self.z_copy(e, d).start())
        self.mine[CHUNKS - 1 - e] = self.near[slot, self.x, :, self.z, self.y]

    def to_out(self, e, last):
        k = CHUNKS - 1 - e

        over(1, self.zs, lambda d: self.z_copy(e, d).wait_recv())
        got = pltpu.make_async_copy(self.gz.at[e], self.gz_v, self.own_sem.at[1])
        got.start()
        got.wait()

        def add(d):
            self.mine[k] += self.gz_v[d]

        over(0, self.zs - 1, add)
        if last:
            self.x_any(e, self.place).start()
            self.keep(e).start()
        for copy in [self.n_copy(e)] + self.a_copies(e) + self.b_copies(e):
            copy.wait_send()
        over(1, self.zs, lambda d: self.z_copy(e, d).wait_send())

        @pl.when(e + HOLD < CHUNKS)
        def _():
            self.signal(self.near_free, self.to_core)

    def to_core_out(self, e):
        self.x_any(e, self.other).wait_recv()
        for copy in self.c_copies(e):
            copy.start()

    def pump(self, t, even):
        def stage(lag, fn, *rest):
            @pl.when((t >= lag) & (t - lag < CHUNKS))
            def _():
                fn(t - lag, *rest)

        stage(0, lambda e: self.load(e).start())
        stage(2, self.to_b)
        stage(3, self.to_z)
        stage(4, self.to_out, not even)
        if not even:
            stage(6, self.to_core_out)
        stage(0, self.to_a)

    def finish(self, p):
        e = 2 * p + 1
        for copy in self.c_arrivals(e):
            copy.wait_recv()
        self.keep(e).wait()
        self.x_any(e, self.place).wait_send()
        for copy in self.c_copies(e):
            copy.wait_send()


class Staged:
    def __init__(self, buffer, g, sems, layer):
        self.buffer, self.g, self.sems, self.layer = buffer, g, sems, layer
        self.count, self.open = 0, {}

    def copy(self, number, slot):
        j = number % 4
        return pltpu.make_async_copy(
            self.buffer.at[slot], self.g.at[PER * self.layer + number // 4, j // 2, j % 2], self.sems.at[slot]
        )

    def put(self, number, value):
        slot = self.count % STAGE
        self.count += 1
        for other, place in list(self.open.items()):
            if place == slot:
                self.close(other)
        shape, thin = self.buffer.shape[2:], self.buffer.shape[-1]
        for i in range(2):
            self.buffer[slot, i] = value[:, i * thin : (i + 1) * thin].reshape(shape)
        self.copy(number, slot).start()
        self.open[number] = slot

    def close(self, number):
        self.copy(number, self.open.pop(number)).wait()

    def flush(self, chunk):
        for number in list(self.open):
            if number // 4 == chunk:
                self.close(number)


class Sum:
    def __init__(self, zs, layer, d, from_y, from_z, held, extra, load_sem, y_s, y_r, z_s, z_r):
        self.zs, self.layer, self.d = zs, layer, d
        self.from_y, self.from_z, self.held, self.extra = from_y, from_z, held, extra
        self.sems = (load_sem, y_s, y_r, z_s, z_r)
        seq = lax.axis_index("seq")
        self.z, self.y = seq // 2, seq % 2

    def y_copy(self, to):
        _, y_s, y_r, _, _ = self.sems
        return remote(
            self.d.at[self.layer, to * 2 + 1 - self.y], self.from_y.at[self.layer, to],
            y_s.at[self.layer, to], y_r.at[self.layer, to], {"seq": self.z * 2 + 1 - self.y},
        )

    def z_copy(self, to):
        _, _, _, z_s, z_r = self.sems
        return remote(
            self.held.at[to % RING], self.from_z.at[self.layer, self.z], z_s.at[self.layer, to],
            z_r.at[self.layer, self.z], {"seq": to * 2 + self.y},
        )

    def z_arrival(self, source):
        _, _, _, z_s, z_r = self.sems
        return remote(
            self.held.at[source % RING], self.from_z.at[self.layer, source], z_s.at[self.layer, source],
            z_r.at[self.layer, source], {"seq": source * 2 + self.y},
        )

    def fetch(self, source, to, i):
        return pltpu.make_async_copy(source, to, self.sems[0].at[i])

    def both(self, z, to):
        own = self.fetch(self.d.at[self.layer, z * 2 + self.y], to, 0)
        own.start()
        self.y_copy(z).wait_recv()
        got = self.fetch(self.from_y.at[self.layer, z], self.extra, 1)
        got.start()
        own.wait()
        got.wait()
        to[...] += self.extra[...]

    def start(self, low, high):
        over(low, high, lambda z: self.y_copy(z).start())

    def forward(self, low, high):
        def one(to):
            @pl.when((to >= RING) & (to - RING != self.z))
            def _():
                self.z_copy(to - RING).wait_send()

            @pl.when(to != self.z)
            def _():
                self.both(to, self.held.at[to % RING])
                self.z_copy(to).start()

        over(low, high, one)

    def result(self, out):
        self.both(self.z, out)

        def add(source):
            @pl.when(source != self.z)
            def _():
                self.z_arrival(source).wait_recv()
                got = self.fetch(self.from_z.at[self.layer, source], self.extra, 1)
                got.start()
                got.wait()
                out[...] += self.extra[...]

        over(0, self.zs, add)

    def finish(self):
        over(0, self.zs, lambda z: self.y_copy(z).wait_send())

        def sent(to):
            @pl.when(to != self.z)
            def _():
                self.z_copy(to).wait_send()

        over(max(0, self.zs - RING), self.zs, sent)


def backward_kernel(
    zs, chunks,
    cot_ref, small_all, table_ref, rate_ref, masks_ref, whole,
    rows_s, zz_s, hs_s, k_s, val_s, lse_s, p_s, before_s, after_s, scores_s,
    grad_ref, out, small_out, g, dh_s, from_y, from_z, gz,
    weights, staging, near, own, ga, gy, gb, gz_v, mine, grad_v, kept, z_v, hs_v, k_v, val_v,
    lse_v, p_v, before_v, after_v, ext, dext, rim_before, rim_after,
    s_ref, dp_ref, dctx_v, delta_v, dq_v, dwin, left_v, right_v, dh_own_v, dh_v, held_v, extra_v,
    ds_all, srecv, szr,
    own_sem, keep_sem, n_s, n_r, a_s, a_r, b_s, b_r, z_s, z_r, x_sm, x_rm, c_s, c_r, near_free, a_free, b_free,
    load_sems, save_sems, stage_sems, rim_s, rim_r, key_sems, sum_load, sy_s, sy_r, sz_s, sz_r,
    t_s, t_r, tz_s, tz_r,
):
    seq = lax.axis_index("seq")
    grp = lax.axis_index("grp")
    count = 2 * zs
    enter_all(seq, grp, zs)
    scatter = Scatter(
        zs, g, out, near, own, ga, gy, gb, gz, gz_v, mine,
        (own_sem, keep_sem, n_s, n_r, a_s, a_r, b_s, b_r, z_s, z_r, x_sm, x_rm, c_s, c_r),
        (near_free, a_free, b_free),
    )
    rows, width = cot_ref.shape
    half = (KERNEL - 1) // 2
    grad_v[...] = cot_ref[...]
    edges = [
        pltpu.make_async_copy(before_s, before_v, save_sems.at[4]),
        pltpu.make_async_copy(after_s, after_v, save_sems.at[5]),
    ]
    for copy in edges:
        copy.start()
    for copy in edges:
        copy.wait()

    def layer_body(lay, carry):
        layer = L - 1 - lay
        e0 = PER * lay
        small = small_all.at[layer]
        ds_ref = ds_all.at[layer]
        ds_ref[...] = jnp.zeros_like(ds_ref)
        staged = Staged(staging, g, stage_sems, layer)

        class Held:
            def __init__(self):
                self.where, self.waited = {}, set()

            def copy(self, chunk):
                return pltpu.make_async_copy(
                    whole.at[pl.ds(GROUP * (PER * layer + chunk), GROUP)],
                    weights.at[pl.ds(GROUP * self.where[chunk], GROUP)],
                    load_sems.at[self.where[chunk]],
                )

            def begin(self, chunk, place):
                self.where[chunk] = place
                self.copy(chunk).start()

            def get(self, n):
                chunk = n // 4
                if chunk not in self.waited:
                    self.copy(chunk).wait()
                    self.waited.add(chunk)
                return joined(weights[GROUP * self.where[chunk] + n % 4])

        def starts(*numbers):
            for i in numbers:
                scatter.start(e0 + i)

        def early(*numbers):
            pl.when(lay == 0)(lambda: starts(*numbers))

        def late(*numbers):
            pl.when(lay > 0)(lambda: starts(*numbers))

        def pumps(*numbers):
            for i in numbers:
                scatter.pump(e0 + i, i % 2 == 0)

        held = Held()
        pairs = {
            "rows": (rows_s.at[layer], kept), "z": (zz_s.at[layer, 1], z_v), "lse": (lse_s.at[layer], lse_v),
            "p": (p_s.at[layer], p_v), "z1": (zz_s.at[layer, 0], z_v),
        }

        def saved(name):
            source, to = pairs[name]
            return pltpu.make_async_copy(source, to, save_sems.at[list(pairs).index(name) % 4])

        for name in ("rows", "z"):
            saved(name).start()
        held.begin(5, 1)
        held.begin(4, 0)
        held.begin(3, 2)
        for name in ("lse", "p"):
            saved(name).start()
        keys = Keys(chunks, layer, hs_s, k_s, val_s, scores_s, hs_v, k_v, val_v, s_ref, key_sems, rows)
        keys.start(0)
        for d in range(2):
            keys.scores(0, d).start()

        saved("rows").wait()
        saved("z").wait()
        unit, scale = norm(kept[V4])
        grad, dg, dc = norm_back(grad_v[...], unit, scale, small[10:11])
        ds_ref[10:11] = dg
        ds_ref[11:12] = dc

        def second_half():
            staged.flush(5)
            early(0)
            pumps(-1)
            late(0)

        grad = ffn_backward(
            grad, kept[V3], z_v, small, 8, held, 16, staged, 16, ds_ref,
            second_half,
        )
        staged.flush(4)
        early(1)
        grad_v[...] = grad
        saved("z1").start()
        fill_ext(ext, before_v[layer, RIM - half : RIM, :], kept[GLU], after_v[layer, 0:half, :])
        conv_backward(grad, ext, masks_ref[...], small, held.get(PC), staged, PC, dext, ds_ref)
        rims = Rims(
            count, layer, dext.at[0:RIM], dext.at[rows + 2 * half - RIM : rows + 2 * half],
            rim_before, rim_after, rim_s, rim_r,
        )
        rims.start()
        held.begin(2, 0)
        pumps(0)
        late(1)

        saved("lse").wait()
        saved("p").wait()
        rims.wait()
        dq_v[...] = dext[half : half + rows, :]
        dq_v[0:half, :] += rim_before[layer, RIM - half : RIM, :]
        dq_v[rows - half : rows, :] += rim_after[layer, 0:half, :]
        grad = gate_backward(
            dq_v[...], grad_v[...], kept[V2], kept[ZA], kept[ZG], small, held.get(PA), held.get(PG),
            staged, PA, ds_ref,
        )
        grad_v[...] = grad
        halves = split(grad)
        staged.put(PO, tn(split(kept[CTX]), halves))
        dctx = nt(halves, split(held.get(PO)))
        dctx_v[...] = dctx
        staged.flush(3)
        held.begin(0, 2)
        early(2)

        prod = dctx_v[...] * kept[CTX]
        for d in range(2):
            cols = slice(256 * d, 256 * d + 256)
            delta_v[4 * rows * d : 4 * rows * (d + 1), :] = jnp.sum(
                stacked(prod[:, cols]), axis=-1, keepdims=True
            )
        pumps(1)
        late(2)
        total = Sum(
            zs, layer, dh_s, from_y, from_z, held_v, extra_v, sum_load, sy_s, sy_r, sz_s, sz_r
        )

        def between():
            pass

        attention_backward(
            chunks, layer, keys, held, small, staged, kept.at[Q], lse_v,
            dctx_v, delta_v, s_ref, dp_ref, dq_v, dwin, left_v, right_v, weights.at[4:6], dh_s, key_sems,
            rows, seq, between, total,
        )
        total.forward(0, zs // 2)
        attention_ends(
            held, small, staged, rate_ref, table_ref, kept.at[Q], p_v, dq_v, dwin, left_v, right_v, kept.at[V1], dh_own_v,
            ds_ref, rows,
        )
        held.begin(1, 1)
        staged.flush(2)
        early(3)
        pumps(2)
        late(3)
        total.forward(zs // 2, zs)
        pumps(3)
        total.result(dh_v)
        unit, scale = norm(kept[V1])
        back, dg, dc = norm_back(dh_own_v[...] + dh_v[...], unit, scale, small[2:3])
        ds_ref[2:3] = dg
        ds_ref[3:4] = dc
        grad = grad_v[...] + back
        saved("z1").wait()

        def first_half():
            staged.flush(1)
            starts(4)
            pumps(4)

        grad_v[...] = ffn_backward(
            grad, kept[X], z_v, small, 0, held, 0, staged, 0, ds_ref, first_half
        )
        staged.flush(0)
        starts(5)
        rims.finish()
        total.finish()
        return carry

    lax.fori_loop(0, L, layer_body, 0)
    grad_ref[...] = grad_v[...]

    z, y = seq // 2, seq % 2
    devices = (
        {"grp": grp + 1 - 2 * (grp % 2)}, {"grp": (grp + 2) % 4}, {"seq": z * 2 + 1 - y},
    )

    def t_copy(i):
        return remote(ds_all, srecv.at[i], t_s.at[i], t_r.at[i], devices[i])

    for i in range(3):
        t_copy(i).start()
        scatter.pump(CHUNKS - 1 + i, i % 2 == 1)
        t_copy(i).wait()
        ds_all[...] += srecv[i]

    def tz_any(d, block):
        return remote(
            ds_all, szr.at[block], tz_s.at[d], tz_r.at[d], {"seq": ((z + d) % zs) * 2 + y}
        )

    over(1, zs, lambda d: tz_any(d, z).start())
    for t in range(CHUNKS + 2, CHUNKS + 6):
        scatter.pump(t, t % 2 == 0)

    def arrived(d):
        tz_any(d, (z + zs - d) % zs).wait_recv()
        tz_any(d, z).wait_send()

    over(1, zs, arrived)
    szr[z] = ds_all[...]
    small_out[...] = szr[0]

    def add(i):
        small_out[...] += szr[i]

    over(1, zs, add)
    over(0, CHUNKS // 2, scatter.finish)


class Keys:
    def __init__(self, chunks, layer, hs_s, k_s, val_s, scores_s, hs_v, k_v, val_v, s_ref, sems, rows):
        self.chunks, self.layer, self.rows = chunks, layer, rows
        self.hs_s, self.k_s, self.val_s = hs_s, k_s, val_s
        self.hs, self.k, self.val, self.sems = hs_v, k_v, val_v, sems
        self.scores_s, self.s_ref = scores_s, s_ref

    def scores(self, chunk, d):
        span = pl.ds(chunk * BACK_KEYS if isinstance(chunk, int) else pl.multiple_of(chunk * BACK_KEYS, BACK_KEYS), BACK_KEYS)
        return pltpu.make_async_copy(
            self.scores_s.at[self.layer, d, :, span], self.s_ref.at[d],
            self.sems.at[BACK_KEYS // self.rows + 2 + d],
        )

    def any(self, chunk, fn):
        per = BACK_KEYS // self.rows
        span = pl.ds(chunk * BACK_KEYS if isinstance(chunk, int) else pl.multiple_of(chunk * BACK_KEYS, BACK_KEYS), BACK_KEYS)
        fn(pltpu.make_async_copy(self.k_s.at[self.layer, span], self.k, self.sems.at[per]))
        fn(pltpu.make_async_copy(self.val_s.at[self.layer, span], self.val, self.sems.at[per + 1]))

        def one(b):
            fn(
                pltpu.make_async_copy(
                    self.hs_s.at[self.layer, chunk * per + b],
                    self.hs.at[pl.ds(pl.multiple_of(b * self.rows, self.rows), self.rows)],
                    self.sems.at[b],
                )
            )

        over(0, per, one)

    def start(self, chunk):
        self.any(chunk, lambda copy: copy.start())

    def wait(self, chunk):
        self.any(chunk, lambda copy: copy.wait())


def attention_backward(
    chunks, layer, keys, held, small, staged, q_v, lse_v,
    dctx_v, delta_v, s_ref, dp_ref, dq_v, dwin, left_v, right_v, dwkv, dh_s, key_sems,
    rows, own, between, total,
):
    per = BACK_KEYS // rows
    wk, wv = split(held.get(PK)), split(held.get(PV))
    dq_v[...] = jnp.zeros_like(dq_v)
    dwin[...] = jnp.zeros_like(dwin)
    left_v[...] = jnp.zeros_like(left_v)
    right_v[...] = jnp.zeros_like(right_v)
    if chunks > 1:
        for i in range(2):
            dwkv[i] = jnp.zeros(dwkv.shape[1:], F32)

    def quad(d, chunk):
        cols = slice(256 * d, 256 * d + 256)
        tall_q = stacked(q_v[:, cols] + small[21:22, cols])
        tall_c = stacked(dctx_v[:, cols])
        ks = split(keys.k[:, cols])
        dp_ref[...] = nt(split(tall_c), split(keys.val[:, cols]))
        keys.scores(chunk, d).wait()
        blocks = [chunk * per + jt for jt in range(per)]
        before = [jnp.where(block <= own - 2, 1.0, 0.0) for block in blocks]
        after = [jnp.where(block >= own + 2, 1.0, 0.0) for block in blocks]

        def tile(i):
            s0 = pl.multiple_of(i * ROWS, ROWS)
            at_rows = pl.ds(pl.multiple_of(4 * rows * d + s0, ROWS), ROWS)
            p = jnp.exp(s_ref[d, pl.ds(s0, ROWS), :] - lse_v[at_rows, :])
            s_ref[d, pl.ds(s0, ROWS), :] = p
            grad = p * (dp_ref[pl.ds(s0, ROWS), :] - delta_v[at_rows, :]) * 0.125
            dp_ref[pl.ds(s0, ROWS), :] = grad
            left = right = None
            for jt in range(per):
                part = grad[:, jt * rows : (jt + 1) * rows]
                left = part * before[jt] if left is None else left + part * before[jt]
                right = part * after[jt] if right is None else right + part * after[jt]
            left_v[at_rows, :] += jnp.sum(left, axis=-1, keepdims=True)
            right_v[at_rows, :] += jnp.sum(right, axis=-1, keepdims=True)

        over(0, 4 * rows // ROWS, tile)
        for i in range(3):
            block = own - 1 + i - chunk * per

            @pl.when((block >= 0) & (block < per))
            def _():
                lanes = pl.ds(pl.multiple_of(block * rows, rows), rows)
                dwin[d, :, i * rows : (i + 1) * rows] = dp_ref[:, lanes]

        dss = split(dp_ref[...])
        dq_v[:, cols] += unstacked(nn(dss, ks), rows)
        keys.val[:, cols] = nn(split(tall_c.T), split(s_ref[d])).T
        keys.k[:, cols] = nn(split(tall_q.T), dss).T
        if chunks > 1:

            @pl.when(chunk + 1 < chunks)
            def _():
                keys.scores(chunk + 1, d).start()

    def one(chunk):
        keys.wait(chunk)
        quad(0, chunk)
        quad(1, chunk)
        hst = split(keys.hs[...].T)
        dk, dval = split(keys.k[...]), split(keys.val[...])
        keys.hs[...] = nt(dk, wk) + nt(dval, wv)

        def store(b):
            return pltpu.make_async_copy(
                keys.hs.at[pl.ds(pl.multiple_of(b * rows, rows), rows)],
                dh_s.at[layer, chunk * per + b],
                key_sems.at[b],
            )

        over(0, per, lambda b: store(b).start())
        dwk, dwv = nn(hst, dk), nn(hst, dval)
        over(0, per, lambda b: store(b).wait())
        total.start(chunk * (per // 2), (chunk + 1) * (per // 2))
        if chunks > 1:
            thin = dwk.shape[1] // 2
            for i, value in enumerate((dwk, dwv)):
                for j in range(2):
                    dwkv[i, j] += value[:, j * thin : (j + 1) * thin].reshape(dwkv.shape[2:])
        else:
            staged.put(PK, dwk)
            staged.put(PV, dwv)
        if chunks > 1:
            pl.when(chunk + 1 < chunks)(lambda: keys.start(chunk + 1))
        pl.when(chunk == 0)(between)

    if chunks > 1:
        over(0, chunks, one)
        staged.put(PK, joined(dwkv[0]))
        staged.put(PV, joined(dwkv[1]))
    else:
        one(0)


def attention_ends(
    held, small, staged, rate_ref, table_ref, q_v, p_v, dq_v, dwin, left_v, right_v, v1_v, dh_own_v, ds_ref, rows,
):
    lane = lax.broadcasted_iota(jnp.int32, (rows, 128), 1)
    shape = (rows, 3 * rows)
    place = lax.broadcasted_iota(jnp.int32, shape, 1) - lax.broadcasted_iota(jnp.int32, shape, 0) - 65
    rate = rate_ref[...]
    qv = q_v[...] + small[22:23]
    dqu = dq_v[...]
    ds_ref[21:22] = jnp.sum(dqu, axis=0, keepdims=True)
    dtable, dqv = [], []
    for d in range(2):
        cols = slice(256 * d, 256 * d + 256)
        near = []
        for n in range(4):
            whole_window = dwin[d, n * rows : (n + 1) * rows, :]
            window = turned(whole_window)
            back = pltpu.roll(window, 3 * rows - 192, 1, stride=1, stride_axis=0)
            back = turned(back[:, :128])
            span = slice(4 * rows * d + n * rows, 4 * rows * d + (n + 1) * rows)
            left = left_v[span, :] + jnp.sum(
                jnp.where(place < 0, whole_window, 0.0), axis=-1, keepdims=True
            )
            right = right_v[span, :] + jnp.sum(
                jnp.where(place > 127, whole_window, 0.0), axis=-1, keepdims=True
            )
            back = back + jnp.where(lane == 0, left, 0.0)
            back = back + jnp.where(lane == 127, right, 0.0)
            near.append(
                jnp.concatenate(
                    [jnp.where(rate == 2, 0.0, back), jnp.where(rate == 2, back, 0.0)], axis=1
                )
            )
        near = split(jnp.concatenate(near, axis=0))
        dtable.append(tn_long(near, split(stacked(qv[:, cols]))))
        dqv.append(unstacked(nn(near, split(p_v[:, cols])), rows))
    dqv = jnp.concatenate(dqv, axis=1)
    ds_ref[22:23] = jnp.sum(dqv, axis=0, keepdims=True)
    staged.put(PP, tn_long(split(table_ref[...]), split(jnp.concatenate(dtable, axis=1))))
    dq = split(dqu + dqv)
    unit, _ = norm(v1_v[...])
    staged.put(PQ, tn(split(unit * small[2:3] + small[3:4]), dq))
    dh_own_v[...] = nt(dq, split(held.get(PQ)))


def run_backward(cot, small, table, rate, masks, whole, saved, seq_size):
    slab = whole.shape[-2]
    width = cot.shape[1]
    half_width = width // 2
    rows = cot.shape[0]
    zs = seq_size // 2
    frames = seq_size * rows
    chunks = frames // BACK_KEYS
    dma = pltpu.SemaphoreType.DMA
    regular = pltpu.SemaphoreType.REGULAR
    block = (rows, width)
    thin = (zs, 2, slab, half_width)
    square = (2,) + thin
    n = CHUNKS
    stream = (L, seq_size, rows, width)
    half = (L, zs, rows, width)
    return pl.pallas_call(
        functools.partial(backward_kernel, zs, chunks),
        in_specs=[WHOLE] * 5 + [FAR] + [FAR] * len(saved),
        out_specs=[WHOLE, FAR, WHOLE, FAR, FAR, FAR, FAR, FAR],
        out_shape=[
            shape_of(*block), shape_of(n, GROUP, 2, slab, half_width), shape_of(L, 24, width),
            shape_of(n, 2, 2, *square), shape_of(*stream), shape_of(*half), shape_of(*half),
            shape_of(n, zs - 1, 2, slab, half_width),
        ],
        scratch_shapes=[
            vmem(12, *square), vmem(STAGE, *square), vmem(HOLD, 2, *square), vmem(2, *square),
            vmem(LANDED, *thin), vmem(LANDED, 2, zs, slab, half_width), vmem(2, 2, zs, slab, half_width),
            vmem(zs - 1, 2, slab, half_width), vmem(n, 2, slab, half_width),
            vmem(*block), vmem(10, *block), vmem(rows, 4 * width), vmem(BACK_KEYS, width), vmem(BACK_KEYS, width),
            vmem(BACK_KEYS, width), vmem(8 * rows, 1), vmem(*table.shape), vmem(L, RIM, width), vmem(L, RIM, width),
            vmem(rows + 8, width), vmem(rows + 8, width), vmem(L, RIM, width), vmem(L, RIM, width),
            vmem(2, 4 * rows, BACK_KEYS), vmem(4 * rows, BACK_KEYS), vmem(*block), vmem(8 * rows, 1),
            vmem(*block), vmem(2, 4 * rows, 3 * rows), vmem(8 * rows, 1), vmem(8 * rows, 1), vmem(*block),
            vmem(*block), vmem(RING, *block), vmem(*block),
            vmem(L, 24, width), vmem(3, L, 24, width),
            vmem(zs, L, 24, width),
            dma((2,)), dma((n,)), dma((n,)), dma((n,)), dma((n, 2)), dma((n, 2)), dma((n, 2)), dma((n, 2)),
            dma((n, zs)), dma((n, zs)), dma((n,)), dma((n,)), dma((n, 2)), dma((n, 2)),
            regular, regular((2,)), regular((2,)),
            dma((3,)), dma((6,)), dma((STAGE,)), dma((L, 2)), dma((L, 2)), dma((BACK_KEYS // rows + 4,)), dma((2,)),
            dma((L, zs)), dma((L, zs)), dma((L, zs)), dma((L, zs)), dma((3,)), dma((3,)), dma((zs,)), dma((zs,)),
        ],
        compiler_params=pltpu.CompilerParams(
            collective_id=1, has_side_effects=True, vmem_limit_bytes=LIMIT
        ),
        name="backward",
    )(cot, small, table, rate, masks, whole, *saved)


def on_device(
    frames_in,
    cotangent,
    lengths,
    rate_flags,
    owner_list,
    master,
    moment_one,
    moment_two,
    average,
    small_params,
    small_moment_one,
    small_moment_two,
    small_average,
):
    local_rows, hidden_width = frames_in.shape[1:]
    seq_size = lax.axis_size("seq")
    me = lax.axis_index("grp")
    slab = hidden_width // seq_size
    stream_rows = local_rows * seq_size
    first_row = lax.axis_index("seq") * local_rows
    half_width = (KERNEL - 1) // 2
    lengths_row = lengths[0]
    flags_row = rate_flags[0]
    own_index = first_row + jnp.arange(local_rows, dtype=jnp.int32)
    own_items, _ = frame_info(own_index, lengths_row, flags_row)
    item_numbers = jnp.arange(lengths_row.shape[0], dtype=jnp.int32)
    rate = 1 + jnp.sum(
        jnp.where(own_items[:, None] == item_numbers[None, :], flags_row[None, :], 0),
        axis=1,
        keepdims=True,
    )
    key_items, _ = frame_info(jnp.arange(stream_rows, dtype=jnp.int32), lengths_row, flags_row)
    rim_index = first_row - half_width + jnp.arange(local_rows + 2 * half_width, dtype=jnp.int32)
    rim_items, _ = frame_info(rim_index, lengths_row, flags_row)
    masks = jnp.stack(
        [
            (rim_items[tap : tap + local_rows] == own_items).astype(jnp.float32)
            for tap in range(KERNEL)
        ],
        axis=1,
    )
    items_q, items_k = own_items[:, None], key_items[None, :]
    table = position_tables(hidden_width)

    places_of = jnp.concatenate([24 * layer + jnp.array(ORDER, jnp.int32) for layer in range(L)])
    slot_of = slot_index(owner_list)[places_of]
    local_slot = slot_of - me * CAP
    owned = ((local_slot >= 0) & (local_slot < CAP)).astype(jnp.int32)
    local_slot = jnp.clip(local_slot, 0, CAP - 1)
    w, values, *saved = run_forward(
        master.reshape(CAP, slab, 2, hidden_width // 2).transpose(0, 2, 1, 3), local_slot, owned.astype(jnp.float32), frames_in[0],
        small_params, table, items_q, items_k, rate, masks, seq_size,
    )
    grad, shares, small_sum = run_backward(
        cotangent[0], small_params, table, rate, masks, w, saved, seq_size
    )[:3]
    small_total = small_sum[:, : small_params.shape[1]]
    here = (
        slot_of[None, :] == (me * CAP + jnp.arange(CAP, dtype=jnp.int32))[:, None]
    ).astype(jnp.int32)
    used = jnp.sum(here, axis=1)
    block_of = jnp.sum(here * jnp.arange(here.shape[1], dtype=jnp.int32)[None, :], axis=1)
    new_master, master_copy, new_one, new_two, new_average = update_slots(
        shares.reshape((-1,) + shares.shape[2:]), block_of, used.astype(jnp.float32)[:, None],
        master, moment_one, moment_two, average,
    )
    new_small, new_small_one, new_small_two = adam_step(
        small_params, small_moment_one, small_moment_two, small_total, RATE_SMALL, 0.0
    )
    new_small_average = AVERAGE_KEEP * small_average + (1.0 - AVERAGE_KEEP) * new_small
    return (
        values[None],
        grad[None],
        new_master,
        master_copy,
        new_one,
        new_two,
        new_average,
        new_small,
        new_small_one,
        new_small_two,
        new_small_average,
    )


def solution(mesh):
    in_specs = (
        P("grp", "seq", None),
        P("grp", "seq", None),
        P("grp", None),
        P("grp", None),
        P(),
        P("grp", "seq"),
        P("grp", "seq"),
        P("grp", "seq"),
        P("grp", "seq"),
        P(),
        P(),
        P(),
        P(),
    )
    out_specs = (
        P("grp", "seq", None),
        P("grp", "seq", None),
        P("grp", "seq"),
        P("grp", "seq"),
        P("grp", "seq"),
        P("grp", "seq"),
        P("grp", "seq"),
        P(),
        P(),
        P(),
        P(),
    )
    return jax.shard_map(
        on_device, mesh=mesh, in_specs=in_specs, out_specs=out_specs, check_vma=False
    )
```

```python
import functools
import math

import jax
import jax.numpy as jnp
import numpy as np
from jax import lax
from jax.experimental import pallas as pl
from jax.experimental.pallas import tpu as pltpu
from jax.sharding import PartitionSpec as P

HEADS = 8
KERNEL = 9
NB = 128
L = 2
CAP = 16
STEP = 10
EPS_NORM = 1e-05
BETA_ONE = 0.9
BETA_TWO = 0.999
ADAM_EPS = 1e-08
RATE_MATRIX = 0.03
RATE_SMALL = 0.1
DECAY_WEIGHT = 0.01
AVERAGE_KEEP = 0.99


def position_tables(width):
    falling = NB // 2 - 1 - np.arange(NB)
    doubled = np.clip(2 * falling, -(NB // 2), NB // 2 - 1)
    offset = np.concatenate([falling, doubled]).astype(np.float64)[:, None]
    column = np.arange(width)
    frequency = np.exp(-math.log(10000.0) * (2 * (column // 2)) / width)[None, :]
    angles = offset * frequency
    return jnp.asarray(np.where(column[None, :] % 2 == 0, np.sin(angles), np.cos(angles)), jnp.float32)


def frame_info(frame_index, lengths_row, flags_row):
    item_ends = jnp.cumsum(lengths_row)
    item_starts = item_ends - lengths_row
    inside = (frame_index[:, None] >= item_starts[None, :]) & (
        frame_index[:, None] < item_ends[None, :]
    )
    numbers = jnp.arange(lengths_row.shape[0], dtype=jnp.int32)
    frame_items = jnp.sum(jnp.where(inside, numbers[None, :] + 1, 0), axis=1) - 1
    first_frame = jnp.sum(jnp.where(inside, item_starts[None, :], 0), axis=1)
    stride = jnp.sum(jnp.where(inside, 1 + flags_row[None, :], 0), axis=1)
    return (frame_items, (frame_index - first_frame) * stride)


def slot_index(owner_list):
    owners = owner_list[:, 0]
    numbers = jnp.arange(owners.shape[0], dtype=jnp.int32)
    earlier = (owners[None, :] == owners[:, None]) & (numbers[None, :] < numbers[:, None])
    owner_rank = jnp.sum(earlier.astype(jnp.int32), axis=1)
    return owners * CAP + owner_rank


def adam_step(attention_weights, first_moment, second_moment, gradient, step_rate, decay_rate):
    first_moment = BETA_ONE * first_moment + (1.0 - BETA_ONE) * gradient
    second_moment = BETA_TWO * second_moment + (1.0 - BETA_TWO) * gradient * gradient
    fixed_one = 1.0 - BETA_ONE**STEP
    fixed_two = 1.0 - BETA_TWO**STEP
    direction = first_moment / fixed_one / (jnp.sqrt(second_moment / fixed_two) + ADAM_EPS)
    return (
        attention_weights - step_rate * (direction + decay_rate * attention_weights),
        first_moment,
        second_moment,
    )


MESH = pl.DeviceIdType.MESH
CHUNKS = 12
GROUP = 4


def places():
    seq = lax.axis_index("seq")
    grp = lax.axis_index("grp")
    return seq, grp, seq // 2, seq % 2, grp // 2, grp % 2


def over(lo, hi, fn):
    def body(i, carry):
        fn(i)
        return carry

    lax.fori_loop(lo, hi, body, 0)


def remote(src, dst, s, r, dev):
    return pltpu.make_async_remote_copy(
        src_ref=src, dst_ref=dst, send_sem=s, recv_sem=r, device_id=dev, device_id_type=MESH
    )


def update_kernel(
    block_ref, used_ref, shares_ref, master_ref, one_ref, two_ref, average_ref,
    new_master, copy, new_one, new_two, new_average, rows_ref, sems,
):
    i = pl.program_id(0)
    slots = master_ref.shape[0]

    def fetch(s):
        return pltpu.make_async_copy(shares_ref.at[block_ref[s]], rows_ref.at[s], sems.at[s])

    @pl.when(i == 0)
    def _():
        over(0, slots, lambda s: fetch(s).start())
        over(0, slots, lambda s: fetch(s).wait())

    half = rows_ref.shape[-1]
    pieces = []
    for r in range(8):
        for h in range(2):
            pieces.append(rows_ref[:, h, i * 8 + r, :])
    gradient = jnp.concatenate(pieces, axis=1) * used_ref[...]
    master = master_ref[...]
    master, one, two = adam_step(
        master, one_ref[...], two_ref[...], gradient, RATE_MATRIX, DECAY_WEIGHT
    )
    new_master[...] = master
    copy[...] = master.astype(jnp.bfloat16)
    new_one[...] = one
    new_two[...] = two
    new_average[...] = AVERAGE_KEEP * average_ref[...] + (1.0 - AVERAGE_KEEP) * master


def update_slots(shares, block, used, master, moment_one, moment_two, average):
    slab, half = shares.shape[2:]
    slots, entries = master.shape
    columns = 8 * 2 * half
    spec = pl.BlockSpec((slots, columns), lambda i, block: (0, i))
    full = jax.ShapeDtypeStruct((slots, entries), jnp.float32)
    return pl.pallas_call(
        update_kernel,
        grid_spec=pltpu.PrefetchScalarGridSpec(
            num_scalar_prefetch=1,
            grid=(slab // 8,),
            in_specs=[
                pl.BlockSpec((slots, 1), lambda i, block: (0, 0)), pl.BlockSpec(memory_space=pl.ANY),
                spec, spec, spec, spec,
            ],
            out_specs=[spec] * 5,
            scratch_shapes=[
                pltpu.VMEM((slots, 2, slab, half), jnp.float32), pltpu.SemaphoreType.DMA((slots,)),
            ],
        ),
        out_shape=[full, jax.ShapeDtypeStruct((slots, entries), jnp.bfloat16), full, full, full],
        compiler_params=pltpu.CompilerParams(vmem_limit_bytes=LIMIT),
        name="update_slots",
    )(block, used, shares, master, moment_one, moment_two, average)


RATE, ITEM = KERNEL, KERNEL + 1
BF16 = jnp.bfloat16
F32 = jnp.float32
ROWS = 32
KEYS = 1024


def split(value):
    high = value.astype(BF16)
    return high, (value - high.astype(F32)).astype(BF16)


def dot(left, right, dims):
    return lax.dot_general(left, right, (dims, ((), ())), preferred_element_type=F32)


def dot3(left, right, dims):
    (lh, ll), (rh, rl) = left, right
    rows = lh.shape[0]
    if dims[0] == (1,) and rows <= 128:
        both = dot(jnp.concatenate([lh, ll], axis=0), rh, dims)
        return both[:rows] + (both[rows:] + dot(lh, rl, dims))
    return dot(lh, rh, dims) + (dot(ll, rh, dims) + dot(lh, rl, dims))


def nn(left, right):
    return dot3(left, right, ((1,), (0,)))


def nt(left, right):
    return dot3(left, right, ((1,), (1,)))


def tn(left, right):
    (lh, ll), (rh, rl) = left, right
    return dot(
        jnp.concatenate([lh, lh, ll], axis=0),
        jnp.concatenate([rh, rl, rh], axis=0),
        ((0,), (0,)),
    )


def tn_long(left, right):
    return dot3(left, right, ((0,), (0,)))


def norm(value):
    center = value - jnp.mean(value, axis=-1, keepdims=True)
    scale = lax.rsqrt(jnp.mean(center * center, axis=-1, keepdims=True) + EPS_NORM)
    return center * scale, scale


def norm_back(grad, unit, scale, gain):
    inner = grad * gain
    value_grad = scale * (
        inner
        - jnp.mean(inner, axis=-1, keepdims=True)
        - unit * jnp.mean(inner * unit, axis=-1, keepdims=True)
    )
    return (
        value_grad,
        jnp.sum(grad * unit, axis=0, keepdims=True),
        jnp.sum(grad, axis=0, keepdims=True),
    )


def sigmoid(value):
    return 1.0 / (1.0 + jnp.exp(-value))


def ffn_forward(v, small, row, weights, first, z_ref, middle=None):
    unit, _ = norm(v)
    h = split(unit * small[row : row + 1] + small[row + 1 : row + 2])
    total = None
    for j in range(4):
        z = nn(h, split(weights.get(first + j)))
        z_ref[:, 512 * j : 512 * j + 512] = z
        part = nn(split(z * sigmoid(z)), split(weights.get(first + 4 + j)))
        total = part if total is None else total + part
        if j == 1 and middle is not None:
            middle()
    return v + 0.5 * total


def ffn_backward(grad, v, z_ref, small, row, weights, first, grads, at, ds_ref, middle):
    unit, scale = norm(v)
    gain = small[row : row + 1]
    hth, htl = split((unit * gain + small[row + 1 : row + 2]).T)
    wide = jnp.concatenate([hth, hth, htl], axis=1)
    half = split(0.5 * grad)
    for j in range(4):
        z = z_ref[:, 512 * j : 512 * j + 512]
        grads.put(at + 4 + j, tn(split(z * sigmoid(z)), half))
    middle()
    total = None
    for j in range(4):
        z = z_ref[:, 512 * j : 512 * j + 512]
        s = sigmoid(z)
        da = nt(half, split(weights.get(first + 4 + j)))
        dz = split(da * (s * (1.0 + z * (1.0 - s))))
        tall = jnp.concatenate([dz[0], dz[1], dz[0]], axis=0)
        grads.put(at + j, dot(wide, tall, ((1,), (0,))))
        part = nt(dz, split(weights.get(first + j)))
        total = part if total is None else total + part
    back, dg, dc = norm_back(total, unit, scale, gain)
    ds_ref[row : row + 1] = dg
    ds_ref[row + 1 : row + 2] = dc
    return grad + back


def conv_mix(ext_ref, masks, small):
    mixed = None
    for t in range(KERNEL):
        part = ext_ref[t : t + masks.shape[0], :] * masks[:, t : t + 1] * small[12 + t : 13 + t]
        mixed = part if mixed is None else mixed + part
    return mixed


def conv_forward(v, ext_ref, masks, small, wc):
    unit, _ = norm(conv_mix(ext_ref, masks, small))
    n = unit * small[6:7] + small[7:8]
    return v + nn(split(n * sigmoid(n)), split(wc))


def conv_backward(grad, ext_ref, masks, small, wc, grads, at, dext_ref, ds_ref):
    unit, scale = norm(conv_mix(ext_ref, masks, small))
    gain = small[6:7]
    n = unit * gain + small[7:8]
    s = sigmoid(n)
    g = split(grad)
    grads.put(at, tn(split(n * s), g))
    dn = nt(g, split(wc)) * (s * (1.0 + n * (1.0 - s)))
    dm, dg, dc = norm_back(dn, unit, scale, gain)
    ds_ref[6:7] = dg
    ds_ref[7:8] = dc
    rows = masks.shape[0]
    dext_ref[...] = jnp.zeros_like(dext_ref)
    for t in range(KERNEL):
        dmt = dm * masks[:, t : t + 1]
        ds_ref[12 + t : 13 + t] = jnp.sum(dmt * ext_ref[t : t + rows, :], axis=0, keepdims=True)
        dext_ref[t : t + rows, :] += dmt * small[12 + t : 13 + t]


def fill_ext(ext_ref, low, middle, high):
    half = (KERNEL - 1) // 2
    rows = middle.shape[0]
    ext_ref[0:half, :] = low
    ext_ref[half : half + rows, :] = middle
    ext_ref[half + rows : 2 * half + rows, :] = high


def gate_forward(v, small, wa, wg):
    unit, _ = norm(v)
    h = split(unit * small[4:5] + small[5:6])
    za, zg = nn(h, split(wa)), nn(h, split(wg))
    return za, zg, za * sigmoid(zg)


def gate_backward(grad_glu, grad, v, za, zg, small, wa, wg, grads, at, ds_ref):
    unit, scale = norm(v)
    gain = small[4:5]
    h = split(unit * gain + small[5:6])
    s = sigmoid(zg)
    da = split(grad_glu * s)
    dg_ = split(grad_glu * za * s * (1.0 - s))
    grads.put(at, tn(h, da))
    grads.put(at + 1, tn(h, dg_))
    back, dg, dc = norm_back(nt(da, split(wa)) + nt(dg_, split(wg)), unit, scale, gain)
    ds_ref[4:5] = dg
    ds_ref[5:6] = dc
    return grad + back


def stacked(quad):
    rows = quad.shape[0]
    tall = jnp.concatenate([quad] * 4, axis=0)
    shape = (4 * rows, 256)
    head = lax.broadcasted_iota(jnp.int32, shape, 0) // rows
    lane = lax.broadcasted_iota(jnp.int32, shape, 1) // 64
    return jnp.where(head == lane, tall, 0.0)


def unstacked(tall, rows):
    shape = (rows, 256)
    lane = lax.broadcasted_iota(jnp.int32, shape, 1) // 64
    quad = tall[0:rows]
    for n in range(1, 4):
        quad = jnp.where(lane == n, tall[n * rows : (n + 1) * rows], quad)
    return quad


def turned(value):
    rows = value.shape[0]
    shape = (rows, rows)
    place = lax.broadcasted_iota(jnp.int32, shape, 0) + lax.broadcasted_iota(jnp.int32, shape, 1)
    swap = jnp.where(place == rows - 1, 1.0, 0.0).astype(BF16)
    high, low = split(value)
    return dot(swap, high, ((1,), (0,))) + dot(swap, low, ((1,), (0,)))


def place_bias(quad_q, table, rate, bias_ref, head0):
    rows = quad_q.shape[0]
    near = nt(split(stacked(quad_q)), split(table))
    row = lax.broadcasted_iota(jnp.int32, (rows, 3 * rows), 0)
    column = lax.broadcasted_iota(jnp.int32, (rows, 3 * rows), 1)
    place = column - row - 65
    for n in range(4):
        both = near[n * rows : (n + 1) * rows]
        one = jnp.where(rate == 2, both[:, 128:], both[:, :128])
        last, first = one[:, 0:1], one[:, 127:128]
        wide = jnp.concatenate([one, jnp.zeros((rows, 2 * rows), F32)], axis=1)
        rolled = pltpu.roll(wide, 65, 1, stride=1, stride_axis=0)
        window = jnp.where(place < 0, last, jnp.where(place > 127, first, rolled))
        bias_ref[head0 + n, 0] = jnp.broadcast_to(last, (rows, rows))
        for i in range(3):
            bias_ref[head0 + n, 1 + i] = window[:, i * rows : (i + 1) * rows]
        bias_ref[head0 + n, 4] = jnp.broadcast_to(first, (rows, rows))


def tile_scores(s_ref, bias_ref, items_q, items_k, tile, head0, own, chunk, rows):
    per = rows // ROWS
    head, part = tile // per, tile % per
    r0 = pl.multiple_of(part * ROWS, ROWS)
    s0 = pl.multiple_of(tile * ROWS, ROWS)
    iq = items_q[pl.ds(r0, ROWS), ITEM : ITEM + 1]
    tiles = []
    keys = s_ref.shape[1]
    for jt in range(keys // rows):
        kind = jnp.clip(chunk * (keys // rows) + jt - own + 2, 0, 4)
        bias = bias_ref[head0 + head, kind, pl.ds(r0, ROWS), :]
        tiles.append(s_ref[pl.ds(s0, ROWS), jt * rows : (jt + 1) * rows] + bias)
    scores = jnp.concatenate(tiles, axis=1) * 0.125
    return scores, iq == items_k, s0, r0


def vmem(*shape, dtype=jnp.float32):
    return pltpu.VMEM(shape, dtype)


def shape_of(*shape):
    return jax.ShapeDtypeStruct(shape, jnp.float32)


WHOLE = pl.BlockSpec(memory_space=pltpu.VMEM)
FAR = pl.BlockSpec(memory_space=pl.ANY)
LIMIT = 62 * 1024 * 1024


ORDER = (0, 1, 2, 3, 4, 5, 6, 7, 8, 12, 9, 10, 11, 13, 14, 15, 16, 17, 18, 19, 20, 21, 22, 23)
PQ, PP, PK, PV, PO, PA, PG, PC = range(8, 16)
PER = 6
RIM = 8
X, V1, V2, CTX, Q, ZA, ZG, GLU, V3, V4 = range(10)


def signal_rims(barrier, seq, count):
    for to in ((seq + 1) % count, (seq + count - 1) % count):
        pl.semaphore_signal(barrier, inc=1, device_id={"seq": to}, device_id_type=MESH)


def enter_all(seq, grp, zs):
    y, z = seq % 2, seq // 2
    barrier = pltpu.get_barrier_semaphore()
    for peer in (grp + 1 - 2 * (grp % 2), (grp + 2) % 4):
        pl.semaphore_signal(barrier, inc=1, device_id={"grp": peer}, device_id_type=MESH)
    pl.semaphore_signal(barrier, inc=1, device_id={"seq": z * 2 + 1 - y}, device_id_type=MESH)

    def greet(d):
        pl.semaphore_signal(
            barrier, inc=1, device_id={"seq": ((z + d) % zs) * 2 + y}, device_id_type=MESH
        )

    over(1, zs, greet)
    signal_rims(barrier, seq, 2 * zs)
    pl.semaphore_wait(barrier, zs + 4)


def side(even):
    return 0 if even else 1


def joined(halves):
    size = halves.shape[1] * halves.shape[2] * halves.shape[3]
    return jnp.concatenate([halves[i].reshape(size, halves.shape[-1]) for i in range(2)], axis=1)


class Gather:
    def __init__(self, zs, rows_ref, slot_ref, owned_ref, whole, table, sib, face, own, sems):
        self.zs = zs
        self.seq, self.grp, self.z, self.y, self.x, self.c = places()
        self.rows_ref, self.slot_ref, self.owned_ref = rows_ref, slot_ref, owned_ref
        self.whole, self.table, self.sib, self.face, self.own = whole, table, sib, face, own
        (
            self.local, self.sib_s, self.sib_r, self.face_s, self.face_r, self.z_s, self.z_r,
            self.a_s, self.a_r, self.b_s, self.b_r, self.c_s, self.c_r,
        ) = sems
        self.to_core = {"grp": self.grp + 1 - 2 * self.c}
        self.to_x = {"grp": (self.grp + 2) % 4}
        self.to_y = {"seq": self.z * 2 + 1 - self.y}
        self.place = 2 * self.c + self.x
        self.other = 2 * self.c + 1 - self.x

    def mine(self, place):
        return self.rows_ref[self.slot_ref[place]] * self.owned_ref[place]

    def sib_copy(self, k):
        return remote(self.table.at[k], self.sib.at[k], self.sib_s.at[k], self.sib_r.at[k], self.to_core)

    def face_copy(self, k):
        return remote(
            self.sib.at[k, 1 - self.x], self.face.at[k], self.face_s.at[k], self.face_r.at[k], self.to_x
        )

    def z_any(self, t, d, even, z):
        return remote(
            self.own.at[t // 2, side(even)],
            self.whole.at[GROUP * (t // 2) + self.place, side(even), z, self.y],
            self.z_s.at[t, d], self.z_r.at[t, d],
            {"seq": ((self.z + d) % self.zs) * 2 + self.y},
        )

    def z_copy(self, t, d, even):
        return self.z_any(t, d, even, self.z)

    def z_arrival(self, t, d, even):
        return self.z_any(t, d, even, (self.z + self.zs - d) % self.zs)

    def keep(self, k):
        return pltpu.make_async_copy(
            self.own.at[k], self.whole.at[GROUP * k + self.place, :, self.z, self.y], self.local.at[k]
        )

    def a_copy(self, t, even):
        part = self.whole.at[GROUP * (t // 2) + self.place, side(even), :, self.y]
        return remote(part, part, self.a_s.at[t], self.a_r.at[t], self.to_y if even else self.to_x)

    def a_arrival(self, t, even):
        first = GROUP * (t // 2)
        if even:
            part = self.whole.at[first + self.place, side(even), :, 1 - self.y]
        else:
            part = self.whole.at[first + self.other, side(even), :, self.y]
        return remote(part, part, self.a_s.at[t], self.a_r.at[t], self.to_y if even else self.to_x)

    def both(self, t, core):
        return pl.ds(GROUP * (t // 2) + 2 * core, 2)

    def b_any(self, t, even, place):
        if even:
            part = self.whole.at[GROUP * (t // 2) + place, 0]
        else:
            part = self.whole.at[self.both(t, self.c), 1, :, place]
        to = self.to_x if even else self.to_y
        return remote(part, part, self.b_s.at[t], self.b_r.at[t], to)

    def b_copy(self, t, even):
        return self.b_any(t, even, self.place if even else self.y)

    def b_arrival(self, t, even):
        return self.b_any(t, even, self.other if even else 1 - self.y)

    def c_any(self, t, even, core):
        part = self.whole.at[self.both(t, core), side(even)]
        return remote(part, part, self.c_s.at[t], self.c_r.at[t], self.to_core)

    def c_copy(self, t, even):
        return self.c_any(t, even, self.c)

    def c_arrival(self, t, even):
        return self.c_any(t, even, 1 - self.c)

    def begin(self, k):
        for i in range(2):
            self.table[k, i] = self.mine(GROUP * k + 2 * (1 - self.c) + i)
        self.sib_copy(k).start()

    def to_face(self, k):
        self.sib_copy(k).wait_recv()
        for i in range(2):
            self.sib[k, i] += self.mine(GROUP * k + 2 * self.c + i)
        self.face_copy(k).start()

    def to_z(self, t, even):
        if even:
            k = t // 2
            self.face_copy(k).wait_recv()
            self.own[k] = self.sib[k, self.x] + self.face[k]
            self.keep(k).start()
        over(1, self.zs, lambda d: self.z_copy(t, d, even).start())

    def to_a(self, t, even):
        over(1, self.zs, lambda d: self.z_arrival(t, d, even).wait_recv())
        if even:
            self.keep(t // 2).wait()
        self.a_copy(t, even).start()

    def to_b(self, t, even):
        self.a_arrival(t, even).wait_recv()
        self.b_copy(t, even).start()

    def to_c(self, t, even):
        self.b_arrival(t, even).wait_recv()
        self.c_copy(t, even).start()

    def open(self):
        over(0, CHUNKS, self.begin)
        over(0, 6, self.to_face)
        for t in range(4):
            self.to_z(t, t % 2 == 0)

    def step(self, t, even):
        steps = 2 * CHUNKS

        @pl.when((t >= 4) & (t - 4 < steps))
        def _():
            self.to_c(t - 4, even)

        @pl.when((t >= 2) & (t - 2 < steps))
        def _():
            self.to_b(t - 2, even)

        @pl.when(t < steps)
        def _():
            self.to_a(t, even)

        if even:

            @pl.when(t // 2 + 6 < CHUNKS)
            def _():
                self.to_face(t // 2 + 6)

        @pl.when(t + 4 < steps)
        def _():
            self.to_z(t + 4, even)

    def arrived(self, k):
        for even in (True, False):
            self.c_arrival(2 * k + (0 if even else 1), even).wait_recv()

    def finish(self, k):
        for even in (True, False):
            t = 2 * k + (0 if even else 1)
            self.c_copy(t, even).wait_send()
            self.b_copy(t, even).wait_send()
            self.a_copy(t, even).wait_send()
            over(1, self.zs, lambda d: self.z_copy(t, d, even).wait_send())
        self.face_copy(k).wait_send()
        self.sib_copy(k).wait_send()


class Share:
    def __init__(self, zs, layer, source, out, keep_sem, z_s, z_r, y_s, y_r):
        self.zs, self.layer, self.source, self.out = zs, layer, source, out
        self.seq = lax.axis_index("seq")
        self.z, self.y = self.seq // 2, self.seq % 2
        self.sems = (keep_sem, z_s, z_r, y_s, y_r)

    def z_any(self, d, z, i):
        _, z_s, z_r, _, _ = self.sems
        block = self.out.at[self.layer, z * 2 + (self.y if i == 0 else 1 - self.y)]
        return remote(
            self.source if i == 0 else block, block, z_s.at[self.layer, d, i], z_r.at[self.layer, d, i],
            {"seq": ((self.z + d) % self.zs) * 2 + self.y},
        )

    def z_copy(self, d, i):
        return self.z_any(d, self.z, i)

    def z_arrival(self, d, i):
        return self.z_any(d, (self.z + self.zs - d) % self.zs, i)

    def y_any(self, y):
        _, _, _, y_s, y_r = self.sems
        return remote(
            self.source, self.out.at[self.layer, self.z * 2 + y], y_s.at[self.layer], y_r.at[self.layer],
            {"seq": self.z * 2 + 1 - self.y},
        )

    def keep(self):
        return pltpu.make_async_copy(
            self.source, self.out.at[self.layer, self.seq], self.sems[0].at[self.layer]
        )

    def start(self):
        self.y_any(self.y).start()
        over(1, self.zs, lambda d: self.z_copy(d, 0).start())
        self.keep().start()

    def forward(self):
        self.y_any(1 - self.y).wait_recv()
        over(1, self.zs, lambda d: self.z_copy(d, 1).start())

    def wait(self):
        for i in range(2):
            over(1, self.zs, lambda d: self.z_arrival(d, i).wait_recv())
        self.keep().wait()

    def finish(self):
        self.y_any(self.y).wait_send()
        for i in range(2):
            over(1, self.zs, lambda d: self.z_copy(d, i).wait_send())


class Rims:
    def __init__(self, count, layer, low, high, before, after, sems, recv):
        seq = lax.axis_index("seq")
        self.up = remote(
            high, before.at[layer], sems.at[layer, 0], recv.at[layer, 0], {"seq": (seq + 1) % count}
        )
        self.down = remote(
            low, after.at[layer], sems.at[layer, 1], recv.at[layer, 1], {"seq": (seq + count - 1) % count}
        )

    def start(self):
        self.up.start()
        self.down.start()

    def wait(self):
        self.up.wait_recv()
        self.down.wait_recv()

    def finish(self):
        self.up.wait_send()
        self.down.wait_send()


def forward_kernel(
    zs, chunks,
    rows_ref, slot_ref, owned_ref, x_ref, small_all, table_ref, ik_ref, marks_ref,
    whole, out_ref, rows_s, z_s, hs_s, k_s, val_s, lse_s, p_s, before_s, after_s, scores_s,
    table_w, sib, face, own_w, weights, x_v, kept, z_v, h_v, hs_v, k_v, val_v, p_v, lse_v, before, after, ext, bias_ref, s_ref, e_ref, top_ref, sum_ref, acc_ref,
    local, sib_sm, sib_rm, face_sm, face_rm, z_sm, z_rm, a_sm, a_rm, b_sm, b_rm, c_sm, c_rm,
    load_sems, save_sems, keep_sem, sz_s, sz_r, sy_s, sy_r, rim_s, rim_r, key_sems,
):
    seq = lax.axis_index("seq")
    grp = lax.axis_index("grp")
    count = 2 * zs
    enter_all(seq, grp, zs)
    gather = Gather(
        zs, rows_ref, slot_ref, owned_ref, whole, table_w, sib, face, own_w,
        (local, sib_sm, sib_rm, face_sm, face_rm, z_sm, z_rm, a_sm, a_rm, b_sm, b_rm, c_sm, c_rm),
    )
    gather.open()
    for t in range(6):
        gather.step(t, t % 2 == 0)
    rows, width = x_ref.shape
    x_v[...] = x_ref[...]
    half = (KERNEL - 1) // 2
    slots = (0, 1, 2, 3, 0, 1)

    def layer_body(layer, carry):
        small = small_all.at[layer]

        def block(n):
            return joined(weights[slots[n // 4], n % 4])

        def load(i):
            return pltpu.make_async_copy(
                whole.at[pl.ds(GROUP * (PER * layer + i), GROUP)], weights.at[slots[i]], load_sems.at[slots[i]]
            )

        def saves(layer):
            pairs = [(kept, rows_s), (z_v, z_s), (lse_v, lse_s), (p_v, p_s)]
            return [
                pltpu.make_async_copy(v, s.at[layer], save_sems.at[i]) for i, (v, s) in enumerate(pairs)
            ]

        share = Share(zs, layer, h_v.at[layer], hs_s, keep_sem, sz_s, sz_r, sy_s, sy_r)
        rims = Rims(
            count, layer, kept.at[GLU, 0:RIM], kept.at[GLU, rows - RIM : rows], before, after, rim_s, rim_r
        )

        def steps(*numbers):
            for i in numbers:
                gather.step(2 * PER * layer + i, i % 2 == 0)

        def arrived(*numbers):
            for i in numbers:
                gather.arrived(PER * layer + i)
                load(i).start()

        class Held:
            def __init__(self):
                self.waited = set()

            def get(self, n):
                if n // 4 not in self.waited:
                    load(n // 4).wait()
                    self.waited.add(n // 4)
                return block(n)

        held = Held()
        arrived(0)
        steps(6, 7)
        arrived(1)

        @pl.when(layer > 0)
        def _():
            for copy in saves(layer - 1):
                copy.wait()

        v1 = ffn_forward(x_v[...], small, 0, held, 0, z_v.at[0])
        kept[X] = x_v[...]
        kept[V1] = v1
        unit, _ = norm(v1)
        h_v[layer] = unit * small[2:3] + small[3:4]
        share.start()
        steps(8, 9)
        arrived(2)
        q = nn(split(h_v[layer]), split(held.get(PQ)))
        kept[Q] = q
        table = nn(split(table_ref[...]), split(held.get(PP)))
        p_v[...] = table
        qv = q + small[22:23]
        for d in range(2):
            cols = slice(256 * d, 256 * d + 256)
            place_bias(qv[:, cols], table[:, cols], marks_ref[:, RATE : RATE + 1], bias_ref, 4 * d)
        share.forward()
        steps(10, 11, 12, 13)
        arrived(3)
        share.wait()
        attention_forward(
            chunks, count, layer, held, small, hs_s, k_s, val_s, scores_s, e_ref, hs_v, k_v, val_v, kept.at[Q], ik_ref, marks_ref,
            bias_ref, s_ref, top_ref, sum_ref, acc_ref, key_sems, rows, seq, lambda d: steps(14, 15) if d == 0 else None,
        )
        lse_v[...] = top_ref[...] + jnp.log(sum_ref[...])
        for d in range(2):
            span = slice(4 * rows * d, 4 * rows * (d + 1))
            kept[CTX, :, 256 * d : 256 * d + 256] = unstacked(acc_ref[span, :] / sum_ref[span, :], rows)
        v2 = kept[V1] + nn(split(kept[CTX]), split(held.get(PO)))
        kept[V2] = v2
        za, zg, glu = gate_forward(v2, small, held.get(PA), held.get(PG))
        kept[ZA] = za
        kept[ZG] = zg
        kept[GLU] = glu
        rims.start()
        steps(16, 17)
        arrived(4)
        rims.wait()
        fill_ext(ext, before[layer, RIM - half : RIM, :], kept[GLU], after[layer, 0:half, :])
        v3 = conv_forward(kept[V2], ext, marks_ref[...], small, held.get(PC))
        kept[V3] = v3
        arrived(5)
        v4 = ffn_forward(v3, small, 8, held, 16, z_v.at[1])
        kept[V4] = v4
        unit, _ = norm(v4)
        x_v[...] = unit * small[10:11] + small[11:12]
        for copy in saves(layer):
            copy.start()
        rims.finish()
        share.finish()
        return carry

    lax.fori_loop(0, L, layer_body, 0)
    out_ref[...] = x_v[...]
    last = [
        pltpu.make_async_copy(v, s.at[L - 1], save_sems.at[i])
        for i, (v, s) in enumerate([(kept, rows_s), (z_v, z_s), (lse_v, lse_s), (p_v, p_s)])
    ]
    edges = [
        pltpu.make_async_copy(before, before_s, save_sems.at[4]),
        pltpu.make_async_copy(after, after_s, save_sems.at[5]),
    ]
    for copy in edges:
        copy.start()
    for copy in last + edges:
        copy.wait()

    over(0, CHUNKS, gather.finish)


def attention_forward(
    chunks, count, layer, held, small, hs_s, k_s, val_s, scores_s, e_ref, hs_v, k_v, val_v, q_v, ik_ref, marks_ref,
    bias_ref, s_ref, top_ref, sum_ref, acc_ref, key_sems, rows, own, between,
):
    per = KEYS // rows
    wk, wv = split(held.get(PK)), split(held.get(PV))
    if chunks > 1:
        top_ref[...] = jnp.full_like(top_ref, -1e30)
        sum_ref[...] = jnp.zeros_like(sum_ref)
        acc_ref[...] = jnp.zeros_like(acc_ref)

    def one(chunk):
        def fetch(b):
            return pltpu.make_async_copy(
                hs_s.at[layer, chunk * per + b],
                hs_v.at[pl.ds(pl.multiple_of(b * rows, rows), rows)],
                key_sems.at[b],
            )

        over(0, per, lambda b: fetch(b).start())
        over(0, per, lambda b: fetch(b).wait())
        hs = split(hs_v[...])
        k_v[...] = nn(hs, wk)
        val_v[...] = nn(hs, wv)
        span = pl.ds(pl.multiple_of(chunk * KEYS, KEYS), KEYS)
        out = [
            pltpu.make_async_copy(k_v, k_s.at[layer, span], key_sems.at[per]),
            pltpu.make_async_copy(val_v, val_s.at[layer, span], key_sems.at[per + 1]),
        ]
        for copy in out:
            copy.start()
        items_k = ik_ref[:, span] if chunks > 1 else ik_ref[...]
        for d in range(2):
            cols = slice(256 * d, 256 * d + 256)
            qs = split(stacked(q_v[:, cols] + small[21:22, cols]))
            s_ref[...] = nt(qs, split(k_v[:, cols]))

            def tile(i):
                scores, same, s0, _ = tile_scores(
                    s_ref, bias_ref, marks_ref, items_k, i, 4 * d, own, chunk, rows
                )
                scores = jnp.where(same, scores, -1e30)
                at_rows = pl.ds(pl.multiple_of(4 * rows * d + s0, ROWS), ROWS)
                top = jnp.max(scores, axis=-1, keepdims=True)
                if chunks > 1:
                    old = top_ref[at_rows, :]
                    top = jnp.maximum(top, old)
                    factor = jnp.exp(old - top)
                s_ref[pl.ds(s0, ROWS), :] = scores
                e = jnp.where(same, jnp.exp(scores - top), 0.0)
                total = jnp.sum(e, axis=-1, keepdims=True)
                if chunks > 1:
                    total = total + sum_ref[at_rows, :] * factor
                    acc_ref[at_rows, :] = acc_ref[at_rows, :] * factor
                top_ref[at_rows, :] = top
                sum_ref[at_rows, :] = total
                high, low = split(e)
                e_ref[0, pl.ds(s0, ROWS), :] = high
                e_ref[1, pl.ds(s0, ROWS), :] = low

            over(0, 4 * rows // ROWS, tile)
            kept_scores = pltpu.make_async_copy(
                s_ref, scores_s.at[layer, d, :, span if chunks > 1 else slice(None)], key_sems.at[per + 2]
            )
            kept_scores.start()
            part = nn((e_ref[0], e_ref[1]), split(val_v[:, cols]))
            kept_scores.wait()
            span_q = slice(4 * rows * d, 4 * rows * (d + 1))
            if chunks > 1:
                acc_ref[span_q, :] += part
                pl.when(chunk == 0)(lambda d=d: between(d))
            else:
                acc_ref[span_q, :] = part
                between(d)
        for copy in out:
            copy.wait()

    if chunks > 1:
        over(0, chunks, one)
    else:
        one(0)


def run_forward(rows3, slot, owned, x, small, table, items_k, marks, seq_size):
    slab = rows3.shape[2]
    width = x.shape[1]
    thin = width // 2
    rows = x.shape[0]
    zs = seq_size // 2
    frames = seq_size * rows
    dma = pltpu.SemaphoreType.DMA
    smem = pl.BlockSpec(memory_space=pltpu.SMEM)
    block = (rows, width)
    tab = table.shape
    saved = [
        (10,) + block, (2, rows, 4 * width), (seq_size, rows, width), (frames, width), (frames, width),
        (8 * rows, 1), tab, (RIM, width), (RIM, width), (2, 4 * rows, frames),
    ]
    n = CHUNKS
    return pl.pallas_call(
        functools.partial(forward_kernel, zs, frames // KEYS),
        in_specs=[WHOLE, smem, smem] + [WHOLE] * 5,
        out_specs=[FAR, WHOLE] + [FAR] * len(saved),
        out_shape=[shape_of(GROUP * n, 2, zs, 2, slab, thin), shape_of(*block)]
        + [shape_of(L, *s) for s in saved],
        scratch_shapes=[
            vmem(n, 2, 2, slab, thin), vmem(n, 2, 2, slab, thin), vmem(n, 2, slab, thin), vmem(n, 2, slab, thin),
            vmem(4, 4, 2, zs, 2, slab, thin), vmem(*block), vmem(10, *block), vmem(2, rows, 4 * width), vmem(L, *block),
            vmem(KEYS, width), vmem(KEYS, width), vmem(KEYS, width), vmem(*tab), vmem(8 * rows, 1),
            vmem(L, RIM, width), vmem(L, RIM, width),
            vmem(rows + 8, width), vmem(8, 5, rows, rows), vmem(4 * rows, KEYS),
            vmem(2, 4 * rows, KEYS, dtype=jnp.bfloat16), vmem(8 * rows, 1), vmem(8 * rows, 1), vmem(8 * rows, 256),
            dma((n,)), dma((n,)), dma((n,)), dma((n,)), dma((n,)), dma((2 * n, zs)), dma((2 * n, zs)),
            dma((2 * n,)), dma((2 * n,)), dma((2 * n,)), dma((2 * n,)), dma((2 * n,)), dma((2 * n,)),
            dma((4,)), dma((6,)), dma((L,)), dma((L, zs, 2)), dma((L, zs, 2)), dma((L,)), dma((L,)),
            dma((L, 2)), dma((L, 2)), dma((KEYS // rows + 3,)),
        ],
        compiler_params=pltpu.CompilerParams(
            collective_id=0, has_side_effects=True, vmem_limit_bytes=LIMIT
        ),
        name="forward",
    )(rows3, slot, owned, x, small, table, items_k, marks)


HOLD = 5
LANDED = 3
STAGE = 3
RING = 4
BACK_KEYS = 512


class Scatter:
    def __init__(self, zs, g, out, near, own, ga, gy, gb, gz, gz_v, mine, sems, free):
        self.zs = zs
        self.seq, self.grp, self.z, self.y, self.x, self.c = places()
        self.g, self.out, self.near, self.own = g, out, near, own
        self.ga, self.gy, self.gb, self.gz, self.gz_v, self.mine = ga, gy, gb, gz, gz_v, mine
        (
            self.own_sem, self.keep_sem, self.n_s, self.n_r, self.a_s, self.a_r, self.b_s, self.b_r,
            self.z_s, self.z_r, self.x_s, self.x_r, self.c_s, self.c_r,
        ) = sems
        self.near_free, self.a_free, self.b_free = free
        self.to_core = {"grp": self.grp + 1 - 2 * self.c}
        self.to_x = {"grp": (self.grp + 2) % 4}
        self.to_y = {"seq": self.z * 2 + 1 - self.y}
        self.place = 2 * self.c + self.x
        self.other = 2 * self.c + 1 - self.x

    def n_copy(self, e):
        return remote(
            self.g.at[CHUNKS - 1 - e, 1 - self.c], self.near.at[e % HOLD], self.n_s.at[e], self.n_r.at[e],
            self.to_core,
        )

    def load(self, e):
        return pltpu.make_async_copy(self.g.at[CHUNKS - 1 - e, self.c], self.own, self.own_sem.at[0])

    def a_copies(self, e):
        slot = self.near.at[e % HOLD]
        return [
            remote(
                slot.at[1 - self.x, 0], self.ga.at[e % LANDED], self.a_s.at[e, 0], self.a_r.at[e, 0], self.to_x
            ),
            remote(
                slot.at[:, 1, :, 1 - self.y], self.gy.at[e % LANDED], self.a_s.at[e, 1], self.a_r.at[e, 1], self.to_y
            ),
        ]

    def b_copies(self, e):
        slot = self.near.at[e % HOLD]
        return [
            remote(
                slot.at[self.x, 0, :, 1 - self.y], self.gb.at[e % 2, 0], self.b_s.at[e, 0], self.b_r.at[e, 0],
                self.to_y,
            ),
            remote(
                slot.at[1 - self.x, 1, :, self.y], self.gb.at[e % 2, 1], self.b_s.at[e, 1], self.b_r.at[e, 1],
                self.to_x,
            ),
        ]

    def z_copy(self, e, d):
        to = (self.z + d) % self.zs
        return remote(
            self.near.at[e % HOLD, self.x, :, to, self.y], self.gz.at[e, d - 1], self.z_s.at[e, d],
            self.z_r.at[e, d], {"seq": to * 2 + self.y},
        )

    def pair(self, e):
        return pl.ds(CHUNKS - 1 - e, 2)

    def x_any(self, e, place):
        return remote(
            self.mine.at[self.pair(e)], self.out.at[self.pair(e), place], self.x_s.at[e], self.x_r.at[e], self.to_x
        )

    def c_any(self, e, parts):
        return [
            remote(p, q, self.c_s.at[e, i], self.c_r.at[e, i], self.to_core) for i, (p, q) in enumerate(parts)
        ]

    def c_copies(self, e):
        far = self.out.at[self.pair(e), self.other]
        return self.c_any(e, [(self.mine.at[self.pair(e)], self.out.at[self.pair(e), self.place]), (far, far)])

    def c_arrivals(self, e):
        sibling = 2 * (1 - self.c) + self.x
        parts = [self.out.at[self.pair(e), p] for p in (sibling, 2 * (1 - self.c) + 1 - self.x)]
        return self.c_any(e, [(p, p) for p in parts])

    def keep(self, e):
        return pltpu.make_async_copy(
            self.mine.at[self.pair(e)], self.out.at[self.pair(e), self.place], self.keep_sem.at[e]
        )

    def start(self, e):
        @pl.when(e >= HOLD)
        def _():
            pl.semaphore_wait(self.near_free, 1)

        self.n_copy(e).start()

    def signal(self, sem, to):
        pl.semaphore_signal(sem, inc=1, device_id=to, device_id_type=MESH)

    def to_a(self, e):
        self.n_copy(e).wait_recv()
        self.load(e).wait()
        slot = e % HOLD

        def add(i):
            self.near[slot, :, :, i] += self.own[:, :, i]

        over(0, self.zs, add)

        @pl.when(e >= LANDED)
        def _():
            pl.semaphore_wait(self.a_free.at[0], 1)
            pl.semaphore_wait(self.a_free.at[1], 1)

        for copy in self.a_copies(e):
            copy.start()

    def to_b(self, e):
        for copy in self.a_copies(e):
            copy.wait_recv()
        slot = e % HOLD

        def add(i):
            self.near[slot, self.x, 0, i] += self.ga[e % LANDED, i]
            for j in range(2):
                self.near[slot, j, 1, i, self.y] += self.gy[e % LANDED, j, i]

        over(0, self.zs, add)

        @pl.when(e + LANDED < CHUNKS)
        def _():
            self.signal(self.a_free.at[0], self.to_x)
            self.signal(self.a_free.at[1], self.to_y)

        @pl.when(e >= 2)
        def _():
            pl.semaphore_wait(self.b_free.at[0], 1)
            pl.semaphore_wait(self.b_free.at[1], 1)

        for copy in self.b_copies(e):
            copy.start()

    def to_z(self, e):
        for copy in self.b_copies(e):
            copy.wait_recv()
        slot = e % HOLD

        def add(i):
            for h in range(2):
                self.near[slot, self.x, h, i, self.y] += self.gb[e % 2, h, i]

        over(0, self.zs, add)

        @pl.when(e + 2 < CHUNKS)
        def _():
            self.signal(self.b_free.at[0], self.to_y)
            self.signal(self.b_free.at[1], self.to_x)

        over(1, self.zs, lambda d: self.z_copy(e, d).start())
        self.mine[CHUNKS - 1 - e] = self.near[slot, self.x, :, self.z, self.y]

    def to_out(self, e, last):
        k = CHUNKS - 1 - e

        over(1, self.zs, lambda d: self.z_copy(e, d).wait_recv())
        got = pltpu.make_async_copy(self.gz.at[e], self.gz_v, self.own_sem.at[1])
        got.start()
        got.wait()

        def add(d):
            self.mine[k] += self.gz_v[d]

        over(0, self.zs - 1, add)
        if last:
            self.x_any(e, self.place).start()
            self.keep(e).start()
        for copy in [self.n_copy(e)] + self.a_copies(e) + self.b_copies(e):
            copy.wait_send()
        over(1, self.zs, lambda d: self.z_copy(e, d).wait_send())

        @pl.when(e + HOLD < CHUNKS)
        def _():
            self.signal(self.near_free, self.to_core)

    def to_core_out(self, e):
        self.x_any(e, self.other).wait_recv()
        for copy in self.c_copies(e):
            copy.start()

    def pump(self, t, even):
        def stage(lag, fn, *rest):
            @pl.when((t >= lag) & (t - lag < CHUNKS))
            def _():
                fn(t - lag, *rest)

        stage(0, lambda e: self.load(e).start())
        stage(2, self.to_b)
        stage(3, self.to_z)
        stage(4, self.to_out, not even)
        if not even:
            stage(6, self.to_core_out)
        stage(0, self.to_a)

    def finish(self, p):
        e = 2 * p + 1
        for copy in self.c_arrivals(e):
            copy.wait_recv()
        self.keep(e).wait()
        self.x_any(e, self.place).wait_send()
        for copy in self.c_copies(e):
            copy.wait_send()


class Staged:
    def __init__(self, buffer, g, sems, layer):
        self.buffer, self.g, self.sems, self.layer = buffer, g, sems, layer
        self.count, self.open = 0, {}

    def copy(self, number, slot):
        j = number % 4
        return pltpu.make_async_copy(
            self.buffer.at[slot], self.g.at[PER * self.layer + number // 4, j // 2, j % 2], self.sems.at[slot]
        )

    def put(self, number, value):
        slot = self.count % STAGE
        self.count += 1
        for other, place in list(self.open.items()):
            if place == slot:
                self.close(other)
        shape, thin = self.buffer.shape[2:], self.buffer.shape[-1]
        for i in range(2):
            self.buffer[slot, i] = value[:, i * thin : (i + 1) * thin].reshape(shape)
        self.copy(number, slot).start()
        self.open[number] = slot

    def close(self, number):
        self.copy(number, self.open.pop(number)).wait()

    def flush(self, chunk):
        for number in list(self.open):
            if number // 4 == chunk:
                self.close(number)


class Sum:
    def __init__(self, zs, layer, d, from_y, from_z, held, extra, load_sem, y_s, y_r, z_s, z_r):
        self.zs, self.layer, self.d = zs, layer, d
        self.from_y, self.from_z, self.held, self.extra = from_y, from_z, held, extra
        self.sems = (load_sem, y_s, y_r, z_s, z_r)
        seq = lax.axis_index("seq")
        self.z, self.y = seq // 2, seq % 2

    def y_copy(self, to):
        _, y_s, y_r, _, _ = self.sems
        return remote(
            self.d.at[self.layer, to * 2 + 1 - self.y], self.from_y.at[self.layer, to],
            y_s.at[self.layer, to], y_r.at[self.layer, to], {"seq": self.z * 2 + 1 - self.y},
        )

    def z_copy(self, to):
        _, _, _, z_s, z_r = self.sems
        return remote(
            self.held.at[to % RING], self.from_z.at[self.layer, self.z], z_s.at[self.layer, to],
            z_r.at[self.layer, self.z], {"seq": to * 2 + self.y},
        )

    def z_arrival(self, source):
        _, _, _, z_s, z_r = self.sems
        return remote(
            self.held.at[source % RING], self.from_z.at[self.layer, source], z_s.at[self.layer, source],
            z_r.at[self.layer, source], {"seq": source * 2 + self.y},
        )

    def fetch(self, source, to, i):
        return pltpu.make_async_copy(source, to, self.sems[0].at[i])

    def both(self, z, to):
        own = self.fetch(self.d.at[self.layer, z * 2 + self.y], to, 0)
        own.start()
        self.y_copy(z).wait_recv()
        got = self.fetch(self.from_y.at[self.layer, z], self.extra, 1)
        got.start()
        own.wait()
        got.wait()
        to[...] += self.extra[...]

    def start(self, low, high):
        over(low, high, lambda z: self.y_copy(z).start())

    def forward(self, low, high):
        def one(to):
            @pl.when((to >= RING) & (to - RING != self.z))
            def _():
                self.z_copy(to - RING).wait_send()

            @pl.when(to != self.z)
            def _():
                self.both(to, self.held.at[to % RING])
                self.z_copy(to).start()

        over(low, high, one)

    def result(self, out):
        self.both(self.z, out)

        def add(source):
            @pl.when(source != self.z)
            def _():
                self.z_arrival(source).wait_recv()
                got = self.fetch(self.from_z.at[self.layer, source], self.extra, 1)
                got.start()
                got.wait()
                out[...] += self.extra[...]

        over(0, self.zs, add)

    def finish(self):
        over(0, self.zs, lambda z: self.y_copy(z).wait_send())

        def sent(to):
            @pl.when(to != self.z)
            def _():
                self.z_copy(to).wait_send()

        over(max(0, self.zs - RING), self.zs, sent)


def backward_kernel(
    zs, chunks,
    cot_ref, small_all, table_ref, marks_ref, whole,
    rows_s, zz_s, hs_s, k_s, val_s, lse_s, p_s, before_s, after_s, scores_s,
    grad_ref, out, small_out, g, dh_s, from_y, from_z, gz,
    weights, staging, near, own, ga, gy, gb, gz_v, mine, grad_v, kept, z_v, hs_v, k_v, val_v,
    lse_v, p_v, before_v, after_v, ext, dext, rim_before, rim_after,
    s_ref, dp_ref, dctx_v, delta_v, dq_v, dwin, left_v, right_v, dh_own_v, dh_v, held_v, extra_v,
    ds_all, srecv, szr,
    own_sem, keep_sem, n_s, n_r, a_s, a_r, b_s, b_r, z_s, z_r, x_sm, x_rm, c_s, c_r, near_free, a_free, b_free,
    load_sems, save_sems, stage_sems, rim_s, rim_r, key_sems, sum_load, sy_s, sy_r, sz_s, sz_r,
    t_s, t_r, tz_s, tz_r,
):
    seq = lax.axis_index("seq")
    grp = lax.axis_index("grp")
    count = 2 * zs
    enter_all(seq, grp, zs)
    scatter = Scatter(
        zs, g, out, near, own, ga, gy, gb, gz, gz_v, mine,
        (own_sem, keep_sem, n_s, n_r, a_s, a_r, b_s, b_r, z_s, z_r, x_sm, x_rm, c_s, c_r),
        (near_free, a_free, b_free),
    )
    rows, width = cot_ref.shape
    half = (KERNEL - 1) // 2
    grad_v[...] = cot_ref[...]
    edges = [
        pltpu.make_async_copy(before_s, before_v, save_sems.at[4]),
        pltpu.make_async_copy(after_s, after_v, save_sems.at[5]),
    ]
    for copy in edges:
        copy.start()
    for copy in edges:
        copy.wait()

    def layer_body(lay, carry):
        layer = L - 1 - lay
        e0 = PER * lay
        small = small_all.at[layer]
        ds_ref = ds_all.at[layer]
        ds_ref[...] = jnp.zeros_like(ds_ref)
        staged = Staged(staging, g, stage_sems, layer)

        class Held:
            def __init__(self):
                self.where, self.waited = {}, set()

            def copy(self, chunk):
                return pltpu.make_async_copy(
                    whole.at[pl.ds(GROUP * (PER * layer + chunk), GROUP)],
                    weights.at[pl.ds(GROUP * self.where[chunk], GROUP)],
                    load_sems.at[self.where[chunk]],
                )

            def begin(self, chunk, place):
                self.where[chunk] = place
                self.copy(chunk).start()

            def get(self, n):
                chunk = n // 4
                if chunk not in self.waited:
                    self.copy(chunk).wait()
                    self.waited.add(chunk)
                return joined(weights[GROUP * self.where[chunk] + n % 4])

        def starts(*numbers):
            for i in numbers:
                scatter.start(e0 + i)

        def early(*numbers):
            pl.when(lay == 0)(lambda: starts(*numbers))

        def late(*numbers):
            pl.when(lay > 0)(lambda: starts(*numbers))

        def pumps(*numbers):
            for i in numbers:
                scatter.pump(e0 + i, i % 2 == 0)

        held = Held()
        pairs = {
            "rows": (rows_s.at[layer], kept), "z": (zz_s.at[layer, 1], z_v), "lse": (lse_s.at[layer], lse_v),
            "p": (p_s.at[layer], p_v), "z1": (zz_s.at[layer, 0], z_v),
        }

        def saved(name):
            source, to = pairs[name]
            return pltpu.make_async_copy(source, to, save_sems.at[list(pairs).index(name) % 4])

        for name in ("rows", "z"):
            saved(name).start()
        held.begin(5, 1)
        held.begin(4, 0)
        held.begin(3, 2)
        for name in ("lse", "p"):
            saved(name).start()
        keys = Keys(chunks, layer, hs_s, k_s, val_s, scores_s, hs_v, k_v, val_v, s_ref, key_sems, rows)
        keys.start(0)
        for d in range(2):
            keys.scores(0, d).start()

        saved("rows").wait()
        saved("z").wait()
        unit, scale = norm(kept[V4])
        grad, dg, dc = norm_back(grad_v[...], unit, scale, small[10:11])
        ds_ref[10:11] = dg
        ds_ref[11:12] = dc

        def second_half():
            staged.flush(5)
            early(0)
            pumps(-1)
            late(0)

        grad = ffn_backward(
            grad, kept[V3], z_v, small, 8, held, 16, staged, 16, ds_ref,
            second_half,
        )
        staged.flush(4)
        early(1)
        grad_v[...] = grad
        saved("z1").start()
        fill_ext(ext, before_v[layer, RIM - half : RIM, :], kept[GLU], after_v[layer, 0:half, :])
        conv_backward(grad, ext, marks_ref[...], small, held.get(PC), staged, PC, dext, ds_ref)
        rims = Rims(
            count, layer, dext.at[0:RIM], dext.at[rows + 2 * half - RIM : rows + 2 * half],
            rim_before, rim_after, rim_s, rim_r,
        )
        rims.start()
        held.begin(2, 0)
        pumps(0)
        late(1)

        saved("lse").wait()
        saved("p").wait()
        rims.wait()
        dq_v[...] = dext[half : half + rows, :]
        dq_v[0:half, :] += rim_before[layer, RIM - half : RIM, :]
        dq_v[rows - half : rows, :] += rim_after[layer, 0:half, :]
        grad = gate_backward(
            dq_v[...], grad_v[...], kept[V2], kept[ZA], kept[ZG], small, held.get(PA), held.get(PG),
            staged, PA, ds_ref,
        )
        grad_v[...] = grad
        halves = split(grad)
        staged.put(PO, tn(split(kept[CTX]), halves))
        dctx = nt(halves, split(held.get(PO)))
        dctx_v[...] = dctx
        staged.flush(3)
        held.begin(0, 2)
        early(2)

        prod = dctx_v[...] * kept[CTX]
        for d in range(2):
            cols = slice(256 * d, 256 * d + 256)
            delta_v[4 * rows * d : 4 * rows * (d + 1), :] = jnp.sum(
                stacked(prod[:, cols]), axis=-1, keepdims=True
            )
        pumps(1)
        late(2)
        total = Sum(
            zs, layer, dh_s, from_y, from_z, held_v, extra_v, sum_load, sy_s, sy_r, sz_s, sz_r
        )

        def between():
            pass

        attention_backward(
            chunks, layer, keys, held, small, staged, kept.at[Q], lse_v,
            dctx_v, delta_v, s_ref, dp_ref, dq_v, dwin, left_v, right_v, weights.at[4:6], dh_s, key_sems,
            rows, seq, between, total,
        )
        total.forward(0, zs // 2)
        attention_ends(
            held, small, staged, marks_ref, table_ref, kept.at[Q], p_v, dq_v, dwin, left_v, right_v, kept.at[V1], dh_own_v,
            ds_ref, rows,
        )
        held.begin(1, 1)
        staged.flush(2)
        early(3)
        pumps(2)
        late(3)
        total.forward(zs // 2, zs)
        pumps(3)
        total.result(dh_v)
        unit, scale = norm(kept[V1])
        back, dg, dc = norm_back(dh_own_v[...] + dh_v[...], unit, scale, small[2:3])
        ds_ref[2:3] = dg
        ds_ref[3:4] = dc
        grad = grad_v[...] + back
        saved("z1").wait()

        def first_half():
            staged.flush(1)
            starts(4)
            pumps(4)

        grad_v[...] = ffn_backward(
            grad, kept[X], z_v, small, 0, held, 0, staged, 0, ds_ref, first_half
        )
        staged.flush(0)
        starts(5)
        rims.finish()
        total.finish()
        return carry

    lax.fori_loop(0, L, layer_body, 0)
    grad_ref[...] = grad_v[...]

    z, y = seq // 2, seq % 2
    devices = (
        {"grp": grp + 1 - 2 * (grp % 2)}, {"grp": (grp + 2) % 4}, {"seq": z * 2 + 1 - y},
    )

    def t_copy(i):
        return remote(ds_all, srecv.at[i], t_s.at[i], t_r.at[i], devices[i])

    for i in range(3):
        t_copy(i).start()
        scatter.pump(CHUNKS - 1 + i, i % 2 == 1)
        t_copy(i).wait()
        ds_all[...] += srecv[i]

    def tz_any(d, block):
        return remote(
            ds_all, szr.at[block], tz_s.at[d], tz_r.at[d], {"seq": ((z + d) % zs) * 2 + y}
        )

    over(1, zs, lambda d: tz_any(d, z).start())
    for t in range(CHUNKS + 2, CHUNKS + 6):
        scatter.pump(t, t % 2 == 0)

    def arrived(d):
        tz_any(d, (z + zs - d) % zs).wait_recv()
        tz_any(d, z).wait_send()

    over(1, zs, arrived)
    szr[z] = ds_all[...]
    small_out[...] = szr[0]

    def add(i):
        small_out[...] += szr[i]

    over(1, zs, add)
    over(0, CHUNKS // 2, scatter.finish)


class Keys:
    def __init__(self, chunks, layer, hs_s, k_s, val_s, scores_s, hs_v, k_v, val_v, s_ref, sems, rows):
        self.chunks, self.layer, self.rows = chunks, layer, rows
        self.hs_s, self.k_s, self.val_s = hs_s, k_s, val_s
        self.hs, self.k, self.val, self.sems = hs_v, k_v, val_v, sems
        self.scores_s, self.s_ref = scores_s, s_ref

    def scores(self, chunk, d):
        span = pl.ds(chunk * BACK_KEYS if isinstance(chunk, int) else pl.multiple_of(chunk * BACK_KEYS, BACK_KEYS), BACK_KEYS)
        return pltpu.make_async_copy(
            self.scores_s.at[self.layer, d, :, span], self.s_ref.at[d],
            self.sems.at[BACK_KEYS // self.rows + 2 + d],
        )

    def any(self, chunk, fn):
        per = BACK_KEYS // self.rows
        span = pl.ds(chunk * BACK_KEYS if isinstance(chunk, int) else pl.multiple_of(chunk * BACK_KEYS, BACK_KEYS), BACK_KEYS)
        fn(pltpu.make_async_copy(self.k_s.at[self.layer, span], self.k, self.sems.at[per]))
        fn(pltpu.make_async_copy(self.val_s.at[self.layer, span], self.val, self.sems.at[per + 1]))

        def one(b):
            fn(
                pltpu.make_async_copy(
                    self.hs_s.at[self.layer, chunk * per + b],
                    self.hs.at[pl.ds(pl.multiple_of(b * self.rows, self.rows), self.rows)],
                    self.sems.at[b],
                )
            )

        over(0, per, one)

    def start(self, chunk):
        self.any(chunk, lambda copy: copy.start())

    def wait(self, chunk):
        self.any(chunk, lambda copy: copy.wait())


def attention_backward(
    chunks, layer, keys, held, small, staged, q_v, lse_v,
    dctx_v, delta_v, s_ref, dp_ref, dq_v, dwin, left_v, right_v, dwkv, dh_s, key_sems,
    rows, own, between, total,
):
    per = BACK_KEYS // rows
    wk, wv = split(held.get(PK)), split(held.get(PV))
    dq_v[...] = jnp.zeros_like(dq_v)
    dwin[...] = jnp.zeros_like(dwin)
    left_v[...] = jnp.zeros_like(left_v)
    right_v[...] = jnp.zeros_like(right_v)
    if chunks > 1:
        for i in range(2):
            dwkv[i] = jnp.zeros(dwkv.shape[1:], F32)

    def quad(d, chunk):
        cols = slice(256 * d, 256 * d + 256)
        tall_q = stacked(q_v[:, cols] + small[21:22, cols])
        tall_c = stacked(dctx_v[:, cols])
        ks = split(keys.k[:, cols])
        dp_ref[...] = nt(split(tall_c), split(keys.val[:, cols]))
        keys.scores(chunk, d).wait()
        blocks = [chunk * per + jt for jt in range(per)]
        before = [jnp.where(block <= own - 2, 1.0, 0.0) for block in blocks]
        after = [jnp.where(block >= own + 2, 1.0, 0.0) for block in blocks]

        def tile(i):
            s0 = pl.multiple_of(i * ROWS, ROWS)
            at_rows = pl.ds(pl.multiple_of(4 * rows * d + s0, ROWS), ROWS)
            p = jnp.exp(s_ref[d, pl.ds(s0, ROWS), :] - lse_v[at_rows, :])
            s_ref[d, pl.ds(s0, ROWS), :] = p
            grad = p * (dp_ref[pl.ds(s0, ROWS), :] - delta_v[at_rows, :]) * 0.125
            dp_ref[pl.ds(s0, ROWS), :] = grad
            left = right = None
            for jt in range(per):
                part = grad[:, jt * rows : (jt + 1) * rows]
                left = part * before[jt] if left is None else left + part * before[jt]
                right = part * after[jt] if right is None else right + part * after[jt]
            left_v[at_rows, :] += jnp.sum(left, axis=-1, keepdims=True)
            right_v[at_rows, :] += jnp.sum(right, axis=-1, keepdims=True)

        over(0, 4 * rows // ROWS, tile)
        for i in range(3):
            block = own - 1 + i - chunk * per

            @pl.when((block >= 0) & (block < per))
            def _():
                lanes = pl.ds(pl.multiple_of(block * rows, rows), rows)
                dwin[d, :, i * rows : (i + 1) * rows] = dp_ref[:, lanes]

        dss = split(dp_ref[...])
        dq_v[:, cols] += unstacked(nn(dss, ks), rows)
        keys.val[:, cols] = nn(split(tall_c.T), split(s_ref[d])).T
        keys.k[:, cols] = nn(split(tall_q.T), dss).T
        if chunks > 1:

            @pl.when(chunk + 1 < chunks)
            def _():
                keys.scores(chunk + 1, d).start()

    def one(chunk):
        keys.wait(chunk)
        quad(0, chunk)
        quad(1, chunk)
        hst = split(keys.hs[...].T)
        dk, dval = split(keys.k[...]), split(keys.val[...])
        keys.hs[...] = nt(dk, wk) + nt(dval, wv)

        def store(b):
            return pltpu.make_async_copy(
                keys.hs.at[pl.ds(pl.multiple_of(b * rows, rows), rows)],
                dh_s.at[layer, chunk * per + b],
                key_sems.at[b],
            )

        over(0, per, lambda b: store(b).start())
        dwk, dwv = nn(hst, dk), nn(hst, dval)
        over(0, per, lambda b: store(b).wait())
        total.start(chunk * (per // 2), (chunk + 1) * (per // 2))
        if chunks > 1:
            thin = dwk.shape[1] // 2
            for i, value in enumerate((dwk, dwv)):
                for j in range(2):
                    dwkv[i, j] += value[:, j * thin : (j + 1) * thin].reshape(dwkv.shape[2:])
        else:
            staged.put(PK, dwk)
            staged.put(PV, dwv)
        if chunks > 1:
            pl.when(chunk + 1 < chunks)(lambda: keys.start(chunk + 1))
        pl.when(chunk == 0)(between)

    if chunks > 1:
        over(0, chunks, one)
        staged.put(PK, joined(dwkv[0]))
        staged.put(PV, joined(dwkv[1]))
    else:
        one(0)


def attention_ends(
    held, small, staged, marks_ref, table_ref, q_v, p_v, dq_v, dwin, left_v, right_v, v1_v, dh_own_v, ds_ref, rows,
):
    lane = lax.broadcasted_iota(jnp.int32, (rows, 128), 1)
    shape = (rows, 3 * rows)
    place = lax.broadcasted_iota(jnp.int32, shape, 1) - lax.broadcasted_iota(jnp.int32, shape, 0) - 65
    rate = marks_ref[:, RATE : RATE + 1]
    qv = q_v[...] + small[22:23]
    dqu = dq_v[...]
    ds_ref[21:22] = jnp.sum(dqu, axis=0, keepdims=True)
    dtable, dqv = [], []
    for d in range(2):
        cols = slice(256 * d, 256 * d + 256)
        near = []
        for n in range(4):
            whole_window = dwin[d, n * rows : (n + 1) * rows, :]
            window = turned(whole_window)
            back = pltpu.roll(window, 3 * rows - 192, 1, stride=1, stride_axis=0)
            back = turned(back[:, :128])
            span = slice(4 * rows * d + n * rows, 4 * rows * d + (n + 1) * rows)
            left = left_v[span, :] + jnp.sum(
                jnp.where(place < 0, whole_window, 0.0), axis=-1, keepdims=True
            )
            right = right_v[span, :] + jnp.sum(
                jnp.where(place > 127, whole_window, 0.0), axis=-1, keepdims=True
            )
            back = back + jnp.where(lane == 0, left, 0.0)
            back = back + jnp.where(lane == 127, right, 0.0)
            near.append(
                jnp.concatenate(
                    [jnp.where(rate == 2, 0.0, back), jnp.where(rate == 2, back, 0.0)], axis=1
                )
            )
        near = split(jnp.concatenate(near, axis=0))
        dtable.append(tn_long(near, split(stacked(qv[:, cols]))))
        dqv.append(unstacked(nn(near, split(p_v[:, cols])), rows))
    dqv = jnp.concatenate(dqv, axis=1)
    ds_ref[22:23] = jnp.sum(dqv, axis=0, keepdims=True)
    staged.put(PP, tn_long(split(table_ref[...]), split(jnp.concatenate(dtable, axis=1))))
    dq = split(dqu + dqv)
    unit, _ = norm(v1_v[...])
    staged.put(PQ, tn(split(unit * small[2:3] + small[3:4]), dq))
    dh_own_v[...] = nt(dq, split(held.get(PQ)))


def run_backward(cot, small, table, marks, whole, saved, seq_size):
    slab = whole.shape[-2]
    width = cot.shape[1]
    half_width = width // 2
    rows = cot.shape[0]
    zs = seq_size // 2
    frames = seq_size * rows
    chunks = frames // BACK_KEYS
    dma = pltpu.SemaphoreType.DMA
    regular = pltpu.SemaphoreType.REGULAR
    block = (rows, width)
    thin = (zs, 2, slab, half_width)
    square = (2,) + thin
    n = CHUNKS
    stream = (L, seq_size, rows, width)
    half = (L, zs, rows, width)
    return pl.pallas_call(
        functools.partial(backward_kernel, zs, chunks),
        in_specs=[WHOLE] * 4 + [FAR] + [FAR] * len(saved),
        out_specs=[WHOLE, FAR, WHOLE, FAR, FAR, FAR, FAR, FAR],
        out_shape=[
            shape_of(*block), shape_of(n, GROUP, 2, slab, half_width), shape_of(L, 24, width),
            shape_of(n, 2, 2, *square), shape_of(*stream), shape_of(*half), shape_of(*half),
            shape_of(n, zs - 1, 2, slab, half_width),
        ],
        scratch_shapes=[
            vmem(12, *square), vmem(STAGE, *square), vmem(HOLD, 2, *square), vmem(2, *square),
            vmem(LANDED, *thin), vmem(LANDED, 2, zs, slab, half_width), vmem(2, 2, zs, slab, half_width),
            vmem(zs - 1, 2, slab, half_width), vmem(n, 2, slab, half_width),
            vmem(*block), vmem(10, *block), vmem(rows, 4 * width), vmem(BACK_KEYS, width), vmem(BACK_KEYS, width),
            vmem(BACK_KEYS, width), vmem(8 * rows, 1), vmem(*table.shape), vmem(L, RIM, width), vmem(L, RIM, width),
            vmem(rows + 8, width), vmem(rows + 8, width), vmem(L, RIM, width), vmem(L, RIM, width),
            vmem(2, 4 * rows, BACK_KEYS), vmem(4 * rows, BACK_KEYS), vmem(*block), vmem(8 * rows, 1),
            vmem(*block), vmem(2, 4 * rows, 3 * rows), vmem(8 * rows, 1), vmem(8 * rows, 1), vmem(*block),
            vmem(*block), vmem(RING, *block), vmem(*block),
            vmem(L, 24, width), vmem(3, L, 24, width),
            vmem(zs, L, 24, width),
            dma((2,)), dma((n,)), dma((n,)), dma((n,)), dma((n, 2)), dma((n, 2)), dma((n, 2)), dma((n, 2)),
            dma((n, zs)), dma((n, zs)), dma((n,)), dma((n,)), dma((n, 2)), dma((n, 2)),
            regular, regular((2,)), regular((2,)),
            dma((3,)), dma((6,)), dma((STAGE,)), dma((L, 2)), dma((L, 2)), dma((BACK_KEYS // rows + 4,)), dma((2,)),
            dma((L, zs)), dma((L, zs)), dma((L, zs)), dma((L, zs)), dma((3,)), dma((3,)), dma((zs,)), dma((zs,)),
        ],
        compiler_params=pltpu.CompilerParams(
            collective_id=1, has_side_effects=True, vmem_limit_bytes=LIMIT
        ),
        name="backward",
    )(cot, small, table, marks, whole, *saved)


def on_device(
    frames_in,
    cotangent,
    lengths,
    rate_flags,
    owner_list,
    master,
    moment_one,
    moment_two,
    average,
    small_params,
    small_moment_one,
    small_moment_two,
    small_average,
):
    local_rows, hidden_width = frames_in.shape[1:]
    seq_size = lax.axis_size("seq")
    me = lax.axis_index("grp")
    slab = hidden_width // seq_size
    stream_rows = local_rows * seq_size
    first_row = lax.axis_index("seq") * local_rows
    half_width = (KERNEL - 1) // 2
    lengths_row = lengths[0]
    flags_row = rate_flags[0]
    own_index = first_row + jnp.arange(local_rows, dtype=jnp.int32)
    own_items, _ = frame_info(own_index, lengths_row, flags_row)
    item_numbers = jnp.arange(lengths_row.shape[0], dtype=jnp.int32)
    rate = 1 + jnp.sum(
        jnp.where(own_items[:, None] == item_numbers[None, :], flags_row[None, :], 0),
        axis=1,
    )
    key_items, _ = frame_info(jnp.arange(stream_rows, dtype=jnp.int32), lengths_row, flags_row)
    rim_index = first_row - half_width + jnp.arange(local_rows + 2 * half_width, dtype=jnp.int32)
    rim_items, _ = frame_info(rim_index, lengths_row, flags_row)
    marks = jnp.stack(
        [
            (rim_items[tap : tap + local_rows] == own_items).astype(jnp.float32)
            for tap in range(KERNEL)
        ]
        + [rate.astype(jnp.float32), own_items.astype(jnp.float32)],
        axis=1,
    )
    items_k = key_items.astype(jnp.float32)[None, :]
    table = position_tables(hidden_width)

    places_of = jnp.concatenate([24 * layer + jnp.array(ORDER, jnp.int32) for layer in range(L)])
    slot_of = slot_index(owner_list)[places_of]
    local_slot = slot_of - me * CAP
    owned = ((local_slot >= 0) & (local_slot < CAP)).astype(jnp.int32)
    local_slot = jnp.clip(local_slot, 0, CAP - 1)
    w, values, *saved = run_forward(
        master.reshape(CAP, slab, 2, hidden_width // 2).transpose(0, 2, 1, 3), local_slot, owned.astype(jnp.float32), frames_in[0],
        small_params, table, items_k, marks, seq_size,
    )
    grad, shares, small_sum = run_backward(
        cotangent[0], small_params, table, marks, w, saved, seq_size
    )[:3]
    small_total = small_sum[:, : small_params.shape[1]]
    here = (
        slot_of[None, :] == (me * CAP + jnp.arange(CAP, dtype=jnp.int32))[:, None]
    ).astype(jnp.int32)
    used = jnp.sum(here, axis=1)
    block_of = jnp.sum(here * jnp.arange(here.shape[1], dtype=jnp.int32)[None, :], axis=1)
    new_master, master_copy, new_one, new_two, new_average = update_slots(
        shares.reshape((-1,) + shares.shape[2:]), block_of, used.astype(jnp.float32)[:, None],
        master, moment_one, moment_two, average,
    )
    new_small, new_small_one, new_small_two = adam_step(
        small_params, small_moment_one, small_moment_two, small_total, RATE_SMALL, 0.0
    )
    new_small_average = AVERAGE_KEEP * small_average + (1.0 - AVERAGE_KEEP) * new_small
    return (
        values[None],
        grad[None],
        new_master,
        master_copy,
        new_one,
        new_two,
        new_average,
        new_small,
        new_small_one,
        new_small_two,
        new_small_average,
    )


def solution(mesh):
    in_specs = (
        P("grp", "seq", None),
        P("grp", "seq", None),
        P("grp", None),
        P("grp", None),
        P(),
        P("grp", "seq"),
        P("grp", "seq"),
        P("grp", "seq"),
        P("grp", "seq"),
        P(),
        P(),
        P(),
        P(),
    )
    out_specs = (
        P("grp", "seq", None),
        P("grp", "seq", None),
        P("grp", "seq"),
        P("grp", "seq"),
        P("grp", "seq"),
        P("grp", "seq"),
        P("grp", "seq"),
        P(),
        P(),
        P(),
        P(),
    )
    return jax.shard_map(
        on_device, mesh=mesh, in_specs=in_specs, out_specs=out_specs, check_vma=False
    )
```
